32 devices in a mesh: grp: 2 (over y), tmpl: 4 (over z), slab: 2 (over x), sub: 2 (over core).
Axes of the slice: x: 2, y: 2, z: 4, core: 2. Of those that a mesh axis runs over, the one named last changes fastest.
Arguments:
- records: bfloat16 [256, 3, 1024], P(('grp', 'tmpl'), None, 'slab'), parts along dimension 0, may hold values from -6 to 6
- owner_slots: int32 [256], P(('grp', 'tmpl')), parts along dimension 0, may hold values from 0 to 127, each once
- gap_start: int32 [256, 4], P('grp'), parts along dimension 0, may hold values from 0 to 1023
- gap_len: int32 [256, 4], P('grp'), parts along dimension 0, may hold values from 1 to 127
- templates: bfloat16 [64, 20, 3, 300], P(('grp', 'tmpl', 'slab'), 'sub'), parts along dimension 0, may hold values from -6 to 6
- station_ids: int32 [64, 20], P(('grp', 'tmpl', 'slab'), 'sub'), parts along dimension 0, may hold values from 0 to 127, all different within a row
- offsets: int32 [64, 20], P(('grp', 'tmpl', 'slab'), 'sub'), parts along dimension 0, may hold values from 0 to 200
Outputs:
- stack: float32 [64, 1024], P(('grp', 'tmpl'), ('slab', 'sub')), parts along dimension 0
The draws below stay inside these ranges and needn't reach their ends.
There are 2 independent parts, one for each index of `grp`. The reference program is written for one: setup_inputs(seed, part) draws one part's arguments, and reference() takes and returns one part's arrays. A program takes and returns all parts, laid end to end along the dimension named above; each array names one. Nothing has to cross between parts.
Inputs may be any that keep to these rules, and one draw needn't show every extreme that they name: `station_ids`: the 20 stations of one template are distinct. `owner_slots`: each station is held by exactly one slot.
All inputs are finite; a program needn't handle non-finite values.
Results may differ from the reference program's by a relative error of at most 0.0003.
Values may be sent and summed in bfloat16 or wider, within the bound.
No kernel may reach another device: no remote copies, remote signals or barrier semaphores. Data moves between devices by JAX's collectives and lax.ppermute only.
A program may use at most 192 MiB of HBM per device.

```python
import jax
import jax.numpy as jnp
from jax import lax

STATIONS = 128
TSTA = 20
L = 300
OFFMAX = 200
GAPS = 4
SLAB_T = 512
K_BLK = 4
TIME = 1024
TEMPLATES = 32


def with_ends(values, stream_key, least, top_value):
    longest = values.shape.index(max(values.shape))
    spots = []
    for shift in (0, 1):
        where = [jax.random.randint(jax.random.fold_in(stream_key, axis), (), 0, length) for axis, length in enumerate(values.shape)]
        where[longest] = (where[longest] + shift) % values.shape[longest]
        spots.append(tuple(where))
    return values.at[spots[0]].set(least).at[spots[1]].set(top_value)


def shard_levels(key, shape, pieces, least, high):
    loudness, own = 1.0, jax.random.fold_in(key, 6)
    for position, parts in pieces:
        heights = jnp.exp(jax.random.uniform(jax.random.fold_in(own, position), (parts,), jnp.float32, least / len(pieces), high / len(pieces)))
        loudness = loudness * jnp.repeat(heights, shape[position] // parts).reshape([-1 if axis == position else 1 for axis in range(len(shape))])
    return loudness


def distinct(stream_key, rows, count, top, lift):
    ranking = jax.random.permutation(jax.random.fold_in(stream_key, 1), count)
    boost = ranking
    for power in range(3):
        boost = boost * boost // count
    boost = boost * lift // count
    chance = jax.random.randint(jax.random.fold_in(stream_key, 2), (rows, count), 0, 4096) + boost
    holders = jax.random.permutation(jax.random.fold_in(stream_key, 3), rows)[jnp.arange(count) % rows]
    chance = jnp.where(jnp.arange(rows)[:, None] == holders[None, :], 1 << 14, chance)
    priority = chance * count + jnp.arange(count)
    return lax.top_k(priority.astype(jnp.int32), top)[1].astype(jnp.int32)


def noise(stream_key, shape, deviation, reach, shards=(), kind=jnp.bfloat16):
    factor_of = shard_levels(stream_key, shape, shards, -0.22, 0.18) if shards else 1.0
    values = jax.random.normal(stream_key, shape, jnp.float32) * deviation * factor_of
    return jnp.minimum(jnp.maximum(values, -reach), reach).astype(kind)


def setup_inputs(seed: int = 0, part: int = 0) -> dict:
    splits = jax.random.split(jax.random.key(seed), 8)
    part_keys = jax.random.split(jax.random.fold_in(splits[7], part), 8)
    return {
        "records": noise(part_keys[0], (STATIONS, 3, TIME), 1.0, 6.0, ((0, 4), (2, 2))),
        "owner_slots": jax.random.permutation(part_keys[1], STATIONS).astype(jnp.int32),
        "gap_start": with_ends(jax.random.randint(part_keys[2], (STATIONS, GAPS), 0, TIME), jax.random.fold_in(part_keys[2], 1), 0, TIME - 1).astype(jnp.int32),
        "gap_len": with_ends(jax.random.randint(part_keys[3], (STATIONS, GAPS), 1, SLAB_T // 4), jax.random.fold_in(part_keys[3], 1), 1, (SLAB_T // 4) - 1).astype(jnp.int32),
        "templates": noise(part_keys[4], (TEMPLATES, TSTA, 3, L), 1.0, 6.0, ((0, 8), (1, 2))),
        "station_ids": distinct(part_keys[5], TEMPLATES, STATIONS, TSTA, 0),
        "offsets": with_ends(jax.random.randint(part_keys[6], (TEMPLATES, TSTA), 0, OFFMAX + 1), jax.random.fold_in(part_keys[6], 1), 0, OFFMAX).astype(jnp.int32),
    }


def correlate(data_ext, rms_data, slot_of, block, sids, offs, width):
    count, js, comps, taps = block.shape
    slots = slot_of[sids].astype(jnp.int32)

    def window(slot, off):
        start = (slot.astype(jnp.int32), jnp.zeros((), jnp.int32), off.astype(jnp.int32))
        seg = lax.dynamic_slice(data_ext, start, (1, comps, width + taps - 1))[0]
        scale = lax.dynamic_slice(rms_data, start, (1, comps, width))[0]
        return (seg, scale)
    segs, scales = jax.vmap(jax.vmap(window))(slots, offs)
    chans = count * js * comps
    num = lax.conv_general_dilated(segs.reshape(1, chans, width + taps - 1), block.reshape(chans, 1, taps), (1,), 'VALID', dimension_numbers=('NCH', 'OIH', 'NCH'), feature_group_count=chans, preferred_element_type=jnp.float32)
    wide = block.astype(jnp.float32)
    wrms = jnp.sqrt(lax.optimization_barrier(jnp.mean(wide * wide, axis=-1)) + 1e-06)
    ncc = num.reshape(count, js, comps, width) / (taps * wrms[..., None] * scales)
    return lax.optimization_barrier(jnp.sum(ncc, axis=(1, 2)))

def window_rms(data_ext, taps):
    wide = data_ext.astype(jnp.float32)
    sums = lax.reduce_window(wide * wide, jnp.array(0, wide.dtype), lax.add, (1, 1, taps), (1, 1, 1), 'VALID')
    return jnp.sqrt(sums / taps + 1e-06)

def reference(records, owner_slots, gap_start, gap_len, templates, station_ids, offsets):
    times = jnp.arange(TIME, dtype=jnp.int32)
    starts = gap_start[owner_slots]
    ends = starts + gap_len[owner_slots]
    hit = (times[None, None, :] >= starts[:, :, None]) & (times[None, None, :] < ends[:, :, None])
    live = jnp.logical_not(jnp.any(hit, axis=1))
    masked = jnp.where(live[:, None, :], records, jnp.zeros((), records.dtype))
    rim = OFFMAX + L - 1
    data_ext = jnp.concatenate([masked, jnp.zeros((STATIONS, 3, rim), records.dtype)], axis=2)
    rms_data = window_rms(data_ext, L)
    slot_of = jnp.zeros((STATIONS,), jnp.int32).at[owner_slots].set(jnp.arange(STATIONS, dtype=jnp.int32))
    nblk = TEMPLATES // K_BLK
    blocks = (templates.reshape(nblk, K_BLK, TSTA, 3, L), station_ids.reshape(nblk, K_BLK, TSTA), offsets.reshape(nblk, K_BLK, TSTA))

    def one_block(item):
        return correlate(data_ext, rms_data, slot_of, item[0], item[1], item[2], TIME)
    return lax.map(one_block, blocks).reshape(TEMPLATES, TIME)
```

```python
import jax
import jax.numpy as jnp
from jax import lax
from jax.experimental import pallas as pl
from jax.experimental.pallas import tpu as pltpu
from jax.sharding import PartitionSpec as P

LANES = 128
SPAN = 64
EXTRA = 16


def round_up(value, step):
    return -(-value // step) * step


def prepare_kernel(sids, offs, gap_start, gap_len, templates, filters, scale, sid_col, off_col, mask, band):
    count, js = sids.shape
    refs = count * js
    comps, taps = templates.shape[1:]
    nstation = gap_start.shape[0]
    depth = filters.shape[2]
    for k in range(count):
        for j in range(js):
            row = k * js + j
            sid_col[row, :] = jnp.full((LANES,), sids[k, j], jnp.int32)
            off_col[row, :] = jnp.full((LANES,), offs[k, j], jnp.int32)

    def one_ref(r, carry):
        wave = templates[r].astype(jnp.float32)
        wave = jnp.concatenate([wave, jnp.zeros((comps, depth - taps), jnp.float32)], axis=1)
        power = jnp.sum(wave * wave, axis=1, keepdims=True) / taps
        factor = 1.0 / (taps * jnp.sqrt(power + 1e-06))
        for c in range(comps):
            scale[pl.ds(c * refs + r, 1), :] = jnp.broadcast_to(factor[c : c + 1], (1, LANES))
            rows = jnp.broadcast_to(wave[c : c + 1], (SPAN, depth))
            rows = pltpu.roll(rows, 0, 1, stride=1, stride_axis=0)
            filters[c * refs + r] = rows.astype(jnp.bfloat16)
        return carry

    lax.fori_loop(0, refs, one_ref, 0, unroll=4)
    own = lax.broadcasted_iota(jnp.int32, (refs, nstation), 1) == sid_col[:, :nstation]
    own = jnp.where(own, 1.0, 0.0)
    starts = gap_start[...]
    ends = starts + gap_len[...]
    live = jnp.ones(mask.shape, jnp.float32)
    times = lax.broadcasted_iota(jnp.int32, mask.shape, 1).astype(jnp.float32)
    first = jnp.dot(own, starts.astype(jnp.float32), precision=lax.Precision.HIGHEST)
    last = jnp.dot(own, ends.astype(jnp.float32), precision=lax.Precision.HIGHEST)
    for g in range(starts.shape[1]):
        inside = (times >= first[:, g : g + 1] - 0.5) & (times < last[:, g : g + 1] - 0.5)
        live = jnp.where(inside, 0.0, live)
    mask[...] = live
    lead = lax.broadcasted_iota(jnp.int32, band.shape, 0) - lax.broadcasted_iota(jnp.int32, band.shape, 1)
    band[...] = jnp.where((lead >= 0) & (lead < taps), 1.0, 0.0).astype(jnp.bfloat16)


def correlate_kernel(comps, rows_slab, nslab, taps, *args):
    nsub = len(args) - 6 - 6
    blocks = args[:nsub]
    filters, scale, sid_col, off_col, mask, band = args[nsub : nsub + 6]
    out, segs, low, high, norm, total = args[nsub + 6 :]
    refs, time = mask.shape
    width = blocks[0].shape[2]
    chunks = time // LANES
    per = width // LANES
    chans = comps * refs
    count = out.shape[1]
    js = refs // count
    tall = low.shape[1]
    pieces = [(part, z) for part in blocks for z in range(part.shape[0])]
    depth = len(pieces) * rows_slab
    owner = []
    lines = round_up(depth, width) // width
    for q in range(lines):
        lane = lax.broadcasted_iota(jnp.int32, (1, width), 1) + q * width
        line = jnp.full((1, width), -1.0, jnp.float32)
        for b, (part, z) in enumerate(pieces):
            tail = part[z, nslab * rows_slab : nslab * rows_slab + EXTRA, :].astype(jnp.float32)
            here = (lane >= b * rows_slab) & (lane < (b + 1) * rows_slab)
            line = jnp.where(here, tail[q : q + 1], line)
        owner.append(line)
    owner = jnp.concatenate(owner, axis=1)[:, :depth]
    row = lax.broadcasted_iota(jnp.int32, (1, depth), 1)
    row = lax.rem(lax.rem(row, rows_slab), comps)
    wanted = sid_col[:, :1].astype(jnp.float32)
    match = owner == wanted
    picks = [jnp.where(match & (row == c), 1.0, 0.0).astype(jnp.bfloat16) for c in range(comps)]
    pick = jnp.concatenate(picks, axis=0)
    for s in range(nslab):
        stack = jnp.concatenate([part[z, s * rows_slab : (s + 1) * rows_slab, :] for part, z in pieces], axis=0)
        got = jnp.dot(pick, stack, preferred_element_type=jnp.float32)
        for c in range(comps):
            segs[c * refs : (c + 1) * refs, s * width : (s + 1) * width] = (
                got[c * refs : (c + 1) * refs] * mask[:, s * width : (s + 1) * width]
            )
    lane = lax.broadcasted_iota(jnp.int32, (8, LANES), 1)
    zero = jnp.zeros((8, LANES), jnp.float32)
    for i in range(chans // 8):
        ref_row = (i * 8) % refs
        off = off_col[ref_row : ref_row + 8, :]
        place = lax.bitwise_and(lane + off, LANES - 1)
        fine = lax.bitwise_and(off, LANES - 1)
        near = lane + fine < LANES
        far = off >= LANES
        turned = [
            jnp.take_along_axis(segs[i * 8 : i * 8 + 8, r * LANES : (r + 1) * LANES], place, axis=1)
            for r in range(chunks)
        ]
        turned += [zero, zero]
        moved = [jnp.where(near, turned[r], turned[r + 1]) for r in range(chunks + 1)]
        for r in range(chunks):
            segs[i * 8 : i * 8 + 8, r * LANES : (r + 1) * LANES] = jnp.where(far, moved[r + 1], moved[r])
    for i in range(chans // 8):
        top = i * 8 * tall
        mine = [segs[i * 8 : i * 8 + 8, r * LANES : (r + 1) * LANES] for r in range(chunks)] + [zero]
        for r in range(chunks):
            low[pl.ds(i * 8, 8), r, :] = mine[r]
            half = jnp.where(lane < LANES - SPAN, pltpu.roll(mine[r], SPAN, 1), pltpu.roll(mine[r + 1], SPAN, 1))
            high[pl.ds(i * 8, 8), r, :] = half
        for r in range(chunks, tall):
            low[pl.ds(i * 8, 8), r, :] = zero
            high[pl.ds(i * 8, 8), r, :] = zero
    kept = []
    for r in range(chunks):
        part = segs[:, r * LANES : (r + 1) * LANES]
        power = part * part
        lead = power.astype(jnp.bfloat16)
        rest = (power - lead.astype(jnp.float32)).astype(jnp.bfloat16)
        kept.append((lead, rest))
    reach = band.shape[0] // LANES
    for r in range(chunks):
        upto = min(reach, chunks - r)
        lead = jnp.concatenate([kept[r + p][0] for p in range(upto)], axis=1)
        rest = jnp.concatenate([kept[r + p][1] for p in range(upto)], axis=1)
        bands = band[: upto * LANES, :]
        sums = jnp.dot(lead, bands, preferred_element_type=jnp.float32)
        sums = sums + jnp.dot(rest, bands, preferred_element_type=jnp.float32)
        factor = scale[...] * lax.rsqrt(sums / taps + 1e-06)
        for i in range(chans // 8):
            norm[pl.ds(i * 8, 8), r, :] = factor[i * 8 : i * 8 + 8]
    span = filters.shape[2] // LANES
    for k in range(count):
        acc = jnp.zeros((chunks, LANES), jnp.float32)
        for c in range(comps):
            for j in range(js):
                ch = c * refs + k * js + j
                left = jnp.concatenate([low[ch, p : p + chunks, :] for p in range(span)], axis=1)
                right = jnp.concatenate([high[ch, p : p + chunks, :] for p in range(span)], axis=1)
                both = jnp.concatenate([left, right], axis=0).astype(jnp.bfloat16)
                res = lax.dot_general(
                    both, filters[ch], (((1,), (1,)), ((), ())), preferred_element_type=jnp.float32
                )
                wide = jnp.concatenate([res[:chunks], res[chunks:]], axis=1)
                acc = acc + wide * norm[ch]
        total[k] = acc
    place = lax.axis_index("slab") * lax.axis_size("sub") + lax.axis_index("sub")
    quarters = out.shape[0]
    each = chunks // quarters
    for q in range(quarters):
        target = lax.bitwise_xor(place, q)
        for e in range(each):
            line = total[:, target * each + e, :]
            out[q, :, e * LANES : (e + 1) * LANES] = line


def on_device(records, owner_slots, gap_start, gap_len, templates, station_ids, offsets):
    nloc, comps, width = records.shape
    count, js, _, taps = templates.shape
    nslab, nsub, ntmpl = (lax.axis_size(name) for name in ("slab", "sub", "tmpl"))
    time = width * nslab
    refs = count * js
    chans = comps * refs
    here, core = lax.axis_index("slab"), lax.axis_index("sub")
    half = nloc // nsub
    rows = half * comps
    rows_slab = round_up(rows, 16)
    mine = lax.dynamic_slice_in_dim(records, half * core, half, 0).reshape(rows, width)
    mine = jnp.pad(mine, ((0, rows_slab - rows), (0, 0)))
    own = lax.dynamic_slice_in_dim(owner_slots, half * core, half, 0)
    own = jnp.pad(jnp.repeat(own, comps), (0, rows_slab - rows), constant_values=-1)
    index = jnp.arange(EXTRA * width, dtype=jnp.int32) % rows_slab
    own = jnp.sum(jnp.where(index[:, None] == jnp.arange(rows_slab)[None, :], own[None, :], 0), axis=1)
    own = own.reshape(EXTRA, width).astype(records.dtype)
    block = jnp.zeros((nslab * rows_slab + EXTRA, width), records.dtype)
    block = lax.dynamic_update_slice(block, own, (nslab * rows_slab, 0))
    block = lax.dynamic_update_slice(block, mine, (here * rows_slab, 0))
    for d in range(1, nslab):
        got = lax.ppermute(mine, "slab", [(i, i ^ d) for i in range(nslab)])
        block = lax.dynamic_update_slice(block, got, ((here ^ d) * rows_slab, 0))
    if ntmpl <= 8:
        column = jnp.stack(
            [block] + [lax.ppermute(block, "tmpl", [(i, i ^ d) for i in range(ntmpl)]) for d in range(1, ntmpl)]
        )
    else:
        column = lax.all_gather(block, "tmpl", axis=0)
    parts = [column] + [
        lax.ppermute(column, "sub", [(i, i ^ d) for i in range(nsub)]) for d in range(1, nsub)
    ]
    vmem, smem = pl.BlockSpec(memory_space=pltpu.VMEM), pl.BlockSpec(memory_space=pltpu.SMEM)
    depth = round_up(taps + SPAN - 1, LANES)
    tables = pl.pallas_call(
        prepare_kernel,
        out_shape=[
            jax.ShapeDtypeStruct((chans, SPAN, depth), jnp.bfloat16),
            jax.ShapeDtypeStruct((chans, LANES), jnp.float32),
            jax.ShapeDtypeStruct((refs, LANES), jnp.int32),
            jax.ShapeDtypeStruct((refs, LANES), jnp.int32),
            jax.ShapeDtypeStruct((refs, time), jnp.float32),
            jax.ShapeDtypeStruct((round_up(taps + LANES - 1, LANES), LANES), jnp.bfloat16),
        ],
        in_specs=[smem, smem, vmem, vmem, vmem],
        out_specs=[vmem] * 6,
        compiler_params=pltpu.CompilerParams(vmem_limit_bytes=40 << 20),
        name="prepare",
    )(station_ids, offsets, gap_start, gap_len, templates.reshape(refs, comps, taps))
    chunks = time // LANES
    quarters = nslab * nsub

    def body(*args):
        correlate_kernel(comps, rows_slab, nslab, taps, *args)

    tall = chunks + 8
    sums = pl.pallas_call(
        body,
        out_shape=jax.ShapeDtypeStruct((quarters, count, time // quarters), jnp.float32),
        in_specs=[vmem] * (nsub + 6),
        out_specs=vmem,
        scratch_shapes=[
            pltpu.VMEM((chans, time), jnp.float32),
            pltpu.VMEM((chans, tall, LANES), jnp.float32),
            pltpu.VMEM((chans, tall, LANES), jnp.float32),
            pltpu.VMEM((chans, chunks, LANES), jnp.float32),
            pltpu.VMEM((count, chunks, LANES), jnp.float32),
        ],
        compiler_params=pltpu.CompilerParams(vmem_limit_bytes=40 << 20),
        name="correlate",
    )(*parts, *tables)
    result = jnp.zeros((nslab, count, time // quarters), jnp.float32)
    got = [sums[0]] + [
        lax.ppermute(sums[q], ("slab", "sub"), [(i, i ^ q) for i in range(quarters)]) for q in range(1, quarters)
    ]
    for d in range(nslab):
        line = sum(got[d * nsub + 1 : (d + 1) * nsub], got[d * nsub])
        result = lax.dynamic_update_slice(result, line[None], (here ^ d, 0, 0))
    return result.reshape(nslab * count, time // quarters)


def solution(mesh):
    in_specs = (
        P(("grp", "tmpl"), None, "slab"),
        P(("grp", "tmpl")),
        P("grp", None),
        P("grp", None),
        P(("grp", "tmpl", "slab"), "sub", None, None),
        P(("grp", "tmpl", "slab"), "sub"),
        P(("grp", "tmpl", "slab"), "sub"),
    )
    out_specs = P(("grp", "tmpl"), ("slab", "sub"))
    return jax.shard_map(
        on_device, mesh=mesh, in_specs=in_specs, out_specs=out_specs, check_vma=False
    )
```

```python
import jax
import jax.numpy as jnp
from jax import lax
from jax.experimental import pallas as pl
from jax.experimental.pallas import tpu as pltpu
from jax.sharding import PartitionSpec as P

LANES = 128
SPAN = 64
EXTRA = 8


def round_up(value, step):
    return -(-value // step) * step


def prepare_kernel(sids, offs, gap_start, gap_len, templates, filters, scale, sid_col, off_col, mask, band):
    count, js = sids.shape
    refs = count * js
    comps, taps = templates.shape[1:]
    nstation = gap_start.shape[0]
    depth = filters.shape[2]
    for k in range(count):
        for j in range(js):
            row = k * js + j
            sid_col[row, :] = jnp.full((LANES,), sids[k, j], jnp.int32)
            off_col[row, :] = jnp.full((LANES,), offs[k, j], jnp.int32)

    def one_ref(r, carry):
        wave = templates[r].astype(jnp.float32)
        wave = jnp.concatenate([wave, jnp.zeros((comps, depth - taps), jnp.float32)], axis=1)
        power = jnp.sum(wave * wave, axis=1, keepdims=True) / taps
        factor = 1.0 / (taps * jnp.sqrt(power + 1e-06))
        for c in range(comps):
            scale[pl.ds(c * refs + r, 1), :] = jnp.broadcast_to(factor[c : c + 1], (1, LANES))
            rows = jnp.broadcast_to(wave[c : c + 1], (SPAN, depth))
            rows = pltpu.roll(rows, 0, 1, stride=1, stride_axis=0)
            filters[c * refs + r] = rows.astype(jnp.bfloat16)
        return carry

    lax.fori_loop(0, refs, one_ref, 0, unroll=4)
    own = lax.broadcasted_iota(jnp.int32, (refs, nstation), 1) == sid_col[:, :nstation]
    own = jnp.where(own, 1.0, 0.0)
    starts = gap_start[...]
    ends = starts + gap_len[...]
    live = jnp.ones(mask.shape, jnp.float32)
    times = lax.broadcasted_iota(jnp.int32, mask.shape, 1).astype(jnp.float32)
    first = jnp.dot(own, starts.astype(jnp.float32), precision=lax.Precision.HIGHEST)
    last = jnp.dot(own, ends.astype(jnp.float32), precision=lax.Precision.HIGHEST)
    for g in range(starts.shape[1]):
        inside = (times >= first[:, g : g + 1] - 0.5) & (times < last[:, g : g + 1] - 0.5)
        live = jnp.where(inside, 0.0, live)
    mask[...] = live
    lead = lax.broadcasted_iota(jnp.int32, band.shape, 0) - lax.broadcasted_iota(jnp.int32, band.shape, 1)
    band[...] = jnp.where((lead >= 0) & (lead < taps), 1.0, 0.0).astype(jnp.bfloat16)


def correlate_kernel(comps, rows_slab, nslab, nsub, taps, *args):
    heads, args = args[:nsub], args[nsub:]
    tails, args = args[: nsub * (nslab - 1)], args[nsub * (nslab - 1) :]
    filters, scale, sid_col, off_col, mask, band = args[:6]
    keep, send, segs, low, high, norm, total = args[6:]
    refs, time = mask.shape
    ntmpl, _, width = heads[0].shape
    chunks = time // LANES
    chans = comps * refs
    count = keep.shape[1]
    js = refs // count
    tall = low.shape[1]
    here, core = lax.axis_index("slab"), lax.axis_index("sub")
    depth = nsub * ntmpl * rows_slab
    owner = []
    lines = round_up(depth, width) // width
    for q in range(lines):
        lane = lax.broadcasted_iota(jnp.int32, (1, width), 1) + q * width
        line = jnp.full((1, width), -1.0, jnp.float32)
        for b in range(nsub * ntmpl):
            tail = heads[b // ntmpl][b % ntmpl, rows_slab : rows_slab + EXTRA, :].astype(jnp.float32)
            inside = (lane >= b * rows_slab) & (lane < (b + 1) * rows_slab)
            line = jnp.where(inside, tail[q : q + 1], line)
        owner.append(line)
    owner = jnp.concatenate(owner, axis=1)[:, :depth]
    row = lax.broadcasted_iota(jnp.int32, (1, depth), 1)
    row = lax.rem(row, rows_slab) // (rows_slab // comps)
    wanted = sid_col[:, :1].astype(jnp.float32)
    match = owner == wanted
    picks = [jnp.where(match & (row == c), 1.0, 0.0).astype(jnp.bfloat16) for c in range(comps)]
    pick = jnp.concatenate(picks, axis=0)
    for d in range(nslab):
        parts = heads if d == 0 else tails[(d - 1) * nsub : d * nsub]
        stack = jnp.concatenate([part[z, :rows_slab, :] for part in parts for z in range(ntmpl)], axis=0)
        got = jnp.dot(pick, stack, preferred_element_type=jnp.float32)
        spot = pl.ds(pl.multiple_of(lax.bitwise_xor(here, d) * width, LANES), width)
        live = mask[:, spot]
        for c in range(comps):
            segs[c * refs : (c + 1) * refs, spot] = got[c * refs : (c + 1) * refs] * live
    lane = lax.broadcasted_iota(jnp.int32, (8, LANES), 1)
    zero = jnp.zeros((8, LANES), jnp.float32)
    for i in range(chans // 8):
        ref_row = (i * 8) % refs
        off = off_col[ref_row : ref_row + 8, :]
        place = lax.bitwise_and(lane + off, LANES - 1)
        fine = lax.bitwise_and(off, LANES - 1)
        near = lane + fine < LANES
        far = off >= LANES
        turned = [
            jnp.take_along_axis(segs[i * 8 : i * 8 + 8, r * LANES : (r + 1) * LANES], place, axis=1)
            for r in range(chunks)
        ]
        turned += [zero, zero]
        moved = [jnp.where(near, turned[r], turned[r + 1]) for r in range(chunks + 1)]
        for r in range(chunks):
            segs[i * 8 : i * 8 + 8, r * LANES : (r + 1) * LANES] = jnp.where(far, moved[r + 1], moved[r])
    for i in range(chans // 8):
        top = i * 8 * tall
        mine = [segs[i * 8 : i * 8 + 8, r * LANES : (r + 1) * LANES] for r in range(chunks)] + [zero]
        for r in range(chunks):
            low[pl.ds(i * 8, 8), r, :] = mine[r]
            half = jnp.where(lane < LANES - SPAN, pltpu.roll(mine[r], SPAN, 1), pltpu.roll(mine[r + 1], SPAN, 1))
            high[pl.ds(i * 8, 8), r, :] = half
        for r in range(chunks, tall):
            low[pl.ds(i * 8, 8), r, :] = zero
            high[pl.ds(i * 8, 8), r, :] = zero
    kept = []
    for r in range(chunks):
        part = segs[:, r * LANES : (r + 1) * LANES]
        power = part * part
        lead = power.astype(jnp.bfloat16)
        rest = (power - lead.astype(jnp.float32)).astype(jnp.bfloat16)
        kept.append((lead, rest))
    reach = band.shape[0] // LANES
    for r in range(chunks):
        upto = min(reach, chunks - r)
        lead = jnp.concatenate([kept[r + p][0] for p in range(upto)], axis=1)
        rest = jnp.concatenate([kept[r + p][1] for p in range(upto)], axis=1)
        bands = band[: upto * LANES, :]
        sums = jnp.dot(lead, bands, preferred_element_type=jnp.float32)
        sums = sums + jnp.dot(rest, bands, preferred_element_type=jnp.float32)
        factor = scale[...] * lax.rsqrt(sums / taps + 1e-06)
        for i in range(chans // 8):
            norm[pl.ds(i * 8, 8), r, :] = factor[i * 8 : i * 8 + 8]
    span = filters.shape[2] // LANES
    for k in range(count):
        acc = jnp.zeros((chunks, LANES), jnp.float32)
        for c in range(comps):
            for j in range(js):
                ch = c * refs + k * js + j
                left = jnp.concatenate([low[ch, p : p + chunks, :] for p in range(span)], axis=1)
                right = jnp.concatenate([high[ch, p : p + chunks, :] for p in range(span)], axis=1)
                both = jnp.concatenate([left, right], axis=0).astype(jnp.bfloat16)
                res = lax.dot_general(
                    both, filters[ch], (((1,), (1,)), ((), ())), preferred_element_type=jnp.float32
                )
                wide = jnp.concatenate([res[:chunks], res[chunks:]], axis=1)
                acc = acc + wide * norm[ch]
        total[k] = acc
    each = chunks // (nslab * nsub)
    for d in range(nslab):
        for e in range(each):
            first = lax.bitwise_xor(here, d) * nsub * each + e
            keep[d, :, e * LANES : (e + 1) * LANES] = total[:, first + core * each, :]
            for m in range(1, nsub):
                other = first + lax.bitwise_xor(core, m) * each
                send[m - 1, d, :, e * LANES : (e + 1) * LANES] = total[:, other, :]


def swapped(value, axis, distance):
    return lax.ppermute(value, axis, [(i, i ^ distance) for i in range(lax.axis_size(axis))])


def on_device(records, owner_slots, gap_start, gap_len, templates, station_ids, offsets):
    nloc, comps, width = records.shape
    count, js, _, taps = templates.shape
    nslab, nsub, ntmpl = (lax.axis_size(name) for name in ("slab", "sub", "tmpl"))
    time = width * nslab
    refs = count * js
    chans = comps * refs
    here, core = lax.axis_index("slab"), lax.axis_index("sub")
    half = nloc // nsub
    high = round_up(half, 16)
    rows_slab = comps * high
    mine = lax.dynamic_slice_in_dim(records.transpose(1, 0, 2), half * core, half, 1)
    mine = jnp.pad(mine, ((0, 0), (0, high - half), (0, 0))).reshape(rows_slab, width)
    own = lax.dynamic_slice_in_dim(owner_slots, half * core, half, 0)
    index = jnp.arange(EXTRA * width, dtype=jnp.int32).reshape(1, EXTRA, width) % high
    slots = jnp.arange(half, dtype=jnp.int32)[:, None, None]
    own = jnp.sum(jnp.where(index == slots, own[:, None, None] + 1, 0), axis=0) - 1
    block = jnp.concatenate([mine, own.astype(records.dtype)], axis=0)
    if ntmpl <= 8:
        column = [block] + [swapped(block, "tmpl", d) for d in range(1, ntmpl)]
    else:
        column = list(lax.all_gather(block, "tmpl", axis=0))
    head = jnp.stack(column)
    waves = jnp.stack([part[:rows_slab] for part in column])
    tails = [swapped(waves, "slab", d) for d in range(1, nslab)]
    heads = [head] + [swapped(head, "sub", m) for m in range(1, nsub)]
    vmem, smem = pl.BlockSpec(memory_space=pltpu.VMEM), pl.BlockSpec(memory_space=pltpu.SMEM)
    depth = round_up(taps + SPAN - 1, LANES)
    tables = pl.pallas_call(
        prepare_kernel,
        out_shape=[
            jax.ShapeDtypeStruct((chans, SPAN, depth), jnp.bfloat16),
            jax.ShapeDtypeStruct((chans, LANES), jnp.float32),
            jax.ShapeDtypeStruct((refs, LANES), jnp.int32),
            jax.ShapeDtypeStruct((refs, LANES), jnp.int32),
            jax.ShapeDtypeStruct((refs, time), jnp.float32),
            jax.ShapeDtypeStruct((round_up(taps + LANES - 1, LANES), LANES), jnp.bfloat16),
        ],
        in_specs=[smem, smem, vmem, vmem, vmem],
        out_specs=[vmem] * 6,
        compiler_params=pltpu.CompilerParams(vmem_limit_bytes=40 << 20),
        name="prepare",
    )(station_ids, offsets, gap_start, gap_len, templates.reshape(refs, comps, taps))
    tails, tables = lax.optimization_barrier((tails, tables))
    lasts = []
    for tail in tails:
        lasts += [tail] + [swapped(tail, "sub", m) for m in range(1, nsub)]
    chunks = time // LANES
    each = width // nsub

    def body(*args):
        correlate_kernel(comps, rows_slab, nslab, nsub, taps, *args)

    tall = chunks + 8
    keep, send = pl.pallas_call(
        body,
        out_shape=[
            jax.ShapeDtypeStruct((nslab, count, each), jnp.float32),
            jax.ShapeDtypeStruct((nsub - 1, nslab, count, each), jnp.float32),
        ],
        in_specs=[vmem] * (nsub * nslab + 6),
        out_specs=[vmem] * 2,
        scratch_shapes=[
            pltpu.VMEM((chans, time), jnp.float32),
            pltpu.VMEM((chans, tall, LANES), jnp.float32),
            pltpu.VMEM((chans, tall, LANES), jnp.float32),
            pltpu.VMEM((chans, chunks, LANES), jnp.float32),
            pltpu.VMEM((count, chunks, LANES), jnp.float32),
        ],
        compiler_params=pltpu.CompilerParams(vmem_limit_bytes=40 << 20),
        name="correlate",
    )(*heads, *lasts, *tables)
    for m in range(1, nsub):
        keep = keep + swapped(send[m - 1], "sub", m)
    lines = [keep[0]] + [swapped(keep[d], "slab", d) for d in range(1, nslab)]
    result = []
    for s in range(nslab):
        line = lines[0]
        for d in range(1, nslab):
            line = jnp.where((here ^ d) == s, lines[d], line)
        result.append(line)
    return jnp.concatenate(result, axis=0)


def solution(mesh):
    in_specs = (
        P(("grp", "tmpl"), None, "slab"),
        P(("grp", "tmpl")),
        P("grp", None),
        P("grp", None),
        P(("grp", "tmpl", "slab"), "sub", None, None),
        P(("grp", "tmpl", "slab"), "sub"),
        P(("grp", "tmpl", "slab"), "sub"),
    )
    out_specs = P(("grp", "tmpl"), ("slab", "sub"))
    return jax.shard_map(
        on_device, mesh=mesh, in_specs=in_specs, out_specs=out_specs, check_vma=False
    )
```

```python
import functools

import jax
import jax.numpy as jnp
from jax import lax
from jax.experimental import pallas as pl
from jax.experimental.pallas import tpu as pltpu
from jax.sharding import PartitionSpec as P

LANES = 128
SPAN = 64
GROUP = 4
EXTRA = 8


def round_up(value, step):
    return -(-value // step) * step


def pack_kernel(owner_slots, records, block, sems):
    comps, nloc, width = records.shape
    half = (block.shape[0] - EXTRA) // comps
    first = pl.multiple_of(lax.axis_index("sub") * half, half)
    copies = []
    for c in range(comps):
        source, place = records.at[c, pl.ds(first, half), :], block.at[c * half : (c + 1) * half, :]
        copies.append(pltpu.make_async_copy(source, place, sems.at[c]))
        copies[-1].start()
    lane = lax.rem(lax.broadcasted_iota(jnp.int32, (EXTRA, width), 1), half)
    line = jnp.full((EXTRA, width), -1, jnp.int32)
    for i in range(half):
        line = jnp.where(lane == i, owner_slots[first + i], line)
    block[comps * half :, :] = line.astype(jnp.float32).astype(block.dtype)
    for copy in copies:
        copy.wait()


def tables_kernel(taps, sids, offs, gap_start, gap_len, sid_col, off_col, mask, band):
    count, js = sids.shape
    refs = count * js
    nstation = gap_start.shape[1]
    for k in range(count):
        for j in range(js):
            row = k * js + j
            sid_col[row, :] = jnp.full((LANES,), sids[k, j], jnp.int32)
            off_col[row, :] = jnp.full((LANES,), offs[k, j], jnp.int32)
    own = lax.broadcasted_iota(jnp.int32, (refs, nstation), 1) == sid_col[:, :nstation]
    starts = gap_start[...].astype(jnp.float32)
    ends = starts + gap_len[...].astype(jnp.float32)
    live = jnp.ones(mask.shape, jnp.float32)
    times = lax.broadcasted_iota(jnp.int32, mask.shape, 1).astype(jnp.float32)
    for g in range(starts.shape[0]):
        first = jnp.sum(jnp.where(own, starts[g : g + 1], 0.0), axis=1, keepdims=True)
        last = jnp.sum(jnp.where(own, ends[g : g + 1], 0.0), axis=1, keepdims=True)
        live = jnp.where((times >= first) & (times < last), 0.0, live)
    mask[...] = live
    rows = lax.rem(lax.broadcasted_iota(jnp.int32, band.shape, 0), LANES)
    cols = lax.broadcasted_iota(jnp.int32, band.shape, 1)
    lead = rows + (cols // LANES) * LANES - lax.rem(cols, LANES)
    band[...] = jnp.where((lead >= 0) & (lead < taps), 1.0, 0.0).astype(jnp.bfloat16)


def filters_kernel(templates, filters, scale):
    js, comps, count, taps = templates.shape
    refs = count * js
    depth = filters.shape[2]

    def one_station(j, carry):
        for c in range(comps):
            wave = templates[j, c].astype(jnp.float32)
            wave = jnp.concatenate([wave, jnp.zeros((count, depth - taps), jnp.float32)], axis=1)
            power = jnp.sum(wave * wave, axis=1, keepdims=True) / taps
            factor = 1.0 / (taps * jnp.sqrt(power + 1e-06))
            for k in range(count):
                ch = c * refs + k * js + j
                scale[pl.ds(ch, 1), :] = jnp.broadcast_to(factor[k : k + 1], (1, LANES))
                rows = jnp.broadcast_to(wave[k : k + 1], (SPAN, depth))
                filters[ch] = pltpu.roll(rows, 0, 1, stride=1, stride_axis=0).astype(jnp.bfloat16)
        return carry

    lax.fori_loop(0, js, one_station, 0)


def correlate_kernel(comps, rows_slab, nslab, nsub, taps, *args):
    heads, args = args[:nsub], args[nsub:]
    tails, args = args[: nsub * (nslab - 1)], args[nsub * (nslab - 1) :]
    filters, scale, sid_col, off_col, mask, band = args[:6]
    keep, send, segs, low, high, norm, total = args[6:]
    refs, time = mask.shape
    ntmpl, _, width = heads[0].shape
    chunks = time // LANES
    chans = comps * refs
    count = keep.shape[1]
    js = refs // count
    tall = low.shape[1]
    here, core = lax.axis_index("slab"), lax.axis_index("sub")
    depth = nsub * ntmpl * rows_slab
    owner = []
    lines = round_up(depth, width) // width
    for q in range(lines):
        lane = lax.broadcasted_iota(jnp.int32, (1, width), 1) + q * width
        line = jnp.full((1, width), -1.0, jnp.float32)
        for b in range(nsub * ntmpl):
            tail = heads[b // ntmpl][b % ntmpl, rows_slab : rows_slab + EXTRA, :].astype(jnp.float32)
            inside = (lane >= b * rows_slab) & (lane < (b + 1) * rows_slab)
            line = jnp.where(inside, tail[q : q + 1], line)
        owner.append(line)
    owner = jnp.concatenate(owner, axis=1)[:, :depth]
    row = lax.broadcasted_iota(jnp.int32, (1, depth), 1)
    row = lax.rem(row, rows_slab) // (rows_slab // comps)
    wanted = sid_col[:, :1].astype(jnp.float32)
    match = owner == wanted
    picks = [jnp.where(match & (row == c), 1.0, 0.0).astype(jnp.bfloat16) for c in range(comps)]
    pick = jnp.concatenate(picks, axis=0)
    for d in range(nslab):
        parts = heads if d == 0 else tails[(d - 1) * nsub : d * nsub]
        stack = jnp.concatenate([part[z, :rows_slab, :] for part in parts for z in range(ntmpl)], axis=0)
        got = jnp.dot(pick, stack, preferred_element_type=jnp.float32)
        spot = pl.ds(pl.multiple_of(lax.bitwise_xor(here, d) * width, LANES), width)
        live = mask[:, spot]
        for c in range(comps):
            segs[c * refs : (c + 1) * refs, spot] = got[c * refs : (c + 1) * refs] * live
    lane = lax.broadcasted_iota(jnp.int32, (8, LANES), 1)
    zero = jnp.zeros((8, LANES), jnp.float32)
    for i in range(chans // 8):
        ref_row = (i * 8) % refs
        off = off_col[ref_row : ref_row + 8, :]
        place = lax.bitwise_and(lane + off, LANES - 1)
        fine = lax.bitwise_and(off, LANES - 1)
        near = lane + fine < LANES
        far = off >= LANES
        turned = [
            jnp.take_along_axis(segs[i * 8 : i * 8 + 8, r * LANES : (r + 1) * LANES], place, axis=1)
            for r in range(chunks)
        ]
        turned += [zero, zero]
        moved = [jnp.where(near, turned[r], turned[r + 1]) for r in range(chunks + 1)]
        for r in range(chunks):
            segs[i * 8 : i * 8 + 8, r * LANES : (r + 1) * LANES] = jnp.where(far, moved[r + 1], moved[r])
    for i in range(chans // 8):
        top = i * 8 * tall
        mine = [segs[i * 8 : i * 8 + 8, r * LANES : (r + 1) * LANES] for r in range(chunks)] + [zero]
        for r in range(chunks):
            low[pl.ds(i * 8, 8), r, :] = mine[r]
            half = jnp.where(lane < LANES - SPAN, pltpu.roll(mine[r], SPAN, 1), pltpu.roll(mine[r + 1], SPAN, 1))
            high[pl.ds(i * 8, 8), r, :] = half
        for r in range(chunks, tall):
            low[pl.ds(i * 8, 8), r, :] = zero
            high[pl.ds(i * 8, 8), r, :] = zero
    reach = band.shape[1] // LANES
    sums = {}
    for r in reversed(range(chunks)):
        part = segs[:, r * LANES : (r + 1) * LANES]
        power = part * part
        lead = power.astype(jnp.bfloat16)
        rest = (power - lead.astype(jnp.float32)).astype(jnp.bfloat16)
        sums[r] = jnp.dot(jnp.concatenate([lead, rest], axis=1), band[...], preferred_element_type=jnp.float32)
        window = sums[r][:, :LANES]
        for p in range(1, min(reach, chunks - r)):
            window = window + sums[r + p][:, p * LANES : (p + 1) * LANES]
        factor = scale[...] * lax.rsqrt(window / taps + 1e-06)
        for i in range(chans // 8):
            norm[pl.ds(i * 8, 8), r, :] = factor[i * 8 : i * 8 + 8]
    span = filters.shape[2] // LANES
    accs = [jnp.zeros((chunks, LANES), jnp.float32) for _ in range(count)]
    side = lax.broadcasted_iota(jnp.int32, (chunks, LANES), 1) < SPAN
    for base in range(0, chans, GROUP):
        rows = []
        for ch in range(base, base + GROUP):
            for source in (low, high):
                rows.append(jnp.concatenate([source[ch, p : p + chunks, :] for p in range(span)], axis=1))
        both = jnp.concatenate(rows, axis=0).astype(jnp.bfloat16)
        weights = filters[base : base + GROUP].reshape(GROUP * SPAN, span * LANES)
        res = lax.dot_general(both, weights, (((1,), (1,)), ((), ())), preferred_element_type=jnp.float32)
        for g in range(GROUP):
            left = (g // 2) * LANES
            tile = res[2 * g * chunks : 2 * (g + 1) * chunks, left : left + LANES]
            early, late = tile[:chunks], tile[chunks:]
            if g % 2 == 0:
                wide = jnp.where(side, early, pltpu.roll(late, SPAN, 1))
            else:
                wide = jnp.where(side, pltpu.roll(early, SPAN, 1), late)
            k = ((base + g) % refs) // js
            accs[k] = accs[k] + wide * norm[base + g]
    for k in range(count):
        total[k] = accs[k]
    each = chunks // (nslab * nsub)
    for d in range(nslab):
        for e in range(each):
            first = lax.bitwise_xor(here, d) * nsub * each + e
            turn = nsub - 1 if d else 0
            near = first + lax.bitwise_xor(core, turn) * each
            keep[d, :, e * LANES : (e + 1) * LANES] = total[:, near, :]
            for m in range(1, nsub):
                other = first + lax.bitwise_xor(core, m ^ turn) * each
                send[m - 1, d, :, e * LANES : (e + 1) * LANES] = total[:, other, :]


def swapped(value, axis, distance):
    return lax.ppermute(value, axis, [(i, i ^ distance) for i in range(lax.axis_size(axis))])


def on_device(records, owner_slots, gap_start, gap_len, templates, station_ids, offsets):
    nloc, comps, width = records.shape
    count, js, _, taps = templates.shape
    nslab, nsub, ntmpl = (lax.axis_size(name) for name in ("slab", "sub", "tmpl"))
    time = width * nslab
    refs = count * js
    chans = comps * refs
    here, core = lax.axis_index("slab"), lax.axis_index("sub")
    vmem, smem = pl.BlockSpec(memory_space=pltpu.VMEM), pl.BlockSpec(memory_space=pltpu.SMEM)
    half = nloc // nsub
    high = round_up(half, 16)
    rows_slab = comps * high
    if high == half:
        block = pl.pallas_call(
            pack_kernel,
            out_shape=jax.ShapeDtypeStruct((rows_slab + EXTRA, width), records.dtype),
            in_specs=[smem, pl.BlockSpec(memory_space=pl.ANY)],
            out_specs=vmem,
            scratch_shapes=[pltpu.SemaphoreType.DMA((comps,))],
            name="pack",
        )(owner_slots, records.transpose(1, 0, 2))
    else:
        mine = lax.dynamic_slice_in_dim(records.transpose(1, 0, 2), half * core, half, 1)
        mine = jnp.pad(mine, ((0, 0), (0, high - half), (0, 0))).reshape(rows_slab, width)
        own = lax.dynamic_slice_in_dim(owner_slots, half * core, half, 0)
        index = jnp.arange(EXTRA * width, dtype=jnp.int32).reshape(1, EXTRA, width) % high
        slots = jnp.arange(half, dtype=jnp.int32)[:, None, None]
        own = jnp.sum(jnp.where(index == slots, own[:, None, None] + 1, 0), axis=0) - 1
        block = jnp.concatenate([mine, own.astype(records.dtype)], axis=0)
    if ntmpl <= 8:
        column = [block] + [swapped(block, "tmpl", d) for d in range(1, ntmpl)]
    else:
        column = list(lax.all_gather(block, "tmpl", axis=0))
    reach = round_up(taps + LANES - 1, LANES)
    tables = pl.pallas_call(
        functools.partial(tables_kernel, taps),
        out_shape=[
            jax.ShapeDtypeStruct((refs, LANES), jnp.int32),
            jax.ShapeDtypeStruct((refs, LANES), jnp.int32),
            jax.ShapeDtypeStruct((refs, time), jnp.float32),
            jax.ShapeDtypeStruct((2 * LANES, reach), jnp.bfloat16),
        ],
        in_specs=[smem, smem, vmem, vmem],
        out_specs=[vmem] * 4,
        name="tables",
    )(station_ids, offsets, gap_start.T, gap_len.T)
    column, tables = lax.optimization_barrier((column, tables))
    head = jnp.stack(column)
    waves = jnp.stack([part[:rows_slab] for part in column])
    tails = [swapped(waves, "slab", d) for d in range(1, nslab)]
    heads = [head] + [swapped(head, "sub", m) for m in range(1, nsub)]
    depth = round_up(taps + SPAN - 1, LANES)
    bank = pl.pallas_call(
        filters_kernel,
        out_shape=[
            jax.ShapeDtypeStruct((chans, SPAN, depth), jnp.bfloat16),
            jax.ShapeDtypeStruct((chans, LANES), jnp.float32),
        ],
        in_specs=[vmem],
        out_specs=[vmem] * 2,
        compiler_params=pltpu.CompilerParams(vmem_limit_bytes=40 << 20),
        name="filters",
    )(templates.transpose(1, 2, 0, 3))
    tails, bank = lax.optimization_barrier((tails, bank))
    lasts = []
    for tail in tails:
        lasts += [tail] + [swapped(tail, "sub", m) for m in range(1, nsub)]
    chunks = time // LANES
    each = width // nsub

    def body(*args):
        correlate_kernel(comps, rows_slab, nslab, nsub, taps, *args)

    tall = chunks + 8
    keep, send = pl.pallas_call(
        body,
        out_shape=[
            jax.ShapeDtypeStruct((nslab, count, each), jnp.float32),
            jax.ShapeDtypeStruct((nsub - 1, nslab, count, each), jnp.float32),
        ],
        in_specs=[vmem] * (nsub * nslab + 6),
        out_specs=[vmem] * 2,
        scratch_shapes=[
            pltpu.VMEM((chans, time), jnp.float32),
            pltpu.VMEM((chans, tall, LANES), jnp.float32),
            pltpu.VMEM((chans, tall, LANES), jnp.float32),
            pltpu.VMEM((chans, chunks, LANES), jnp.float32),
            pltpu.VMEM((count, chunks, LANES), jnp.float32),
        ],
        compiler_params=pltpu.CompilerParams(vmem_limit_bytes=40 << 20),
        name="correlate",
    )(*heads, *lasts, *bank, *tables)
    for m in range(1, nsub):
        keep = keep + swapped(send[m - 1], "sub", m)
    lines = [keep[0]]
    for d in range(1, nslab):
        lines.append(swapped(keep[d], ("slab", "sub"), d * nsub + nsub - 1))
    result = []
    for s in range(nslab):
        line = lines[0]
        for d in range(1, nslab):
            line = jnp.where((here ^ d) == s, lines[d], line)
        result.append(line)
    return jnp.concatenate(result, axis=0)


def solution(mesh):
    in_specs = (
        P(("grp", "tmpl"), None, "slab"),
        P(("grp", "tmpl")),
        P("grp", None),
        P("grp", None),
        P(("grp", "tmpl", "slab"), "sub", None, None),
        P(("grp", "tmpl", "slab"), "sub"),
        P(("grp", "tmpl", "slab"), "sub"),
    )
    out_specs = P(("grp", "tmpl"), ("slab", "sub"))
    return jax.shard_map(
        on_device, mesh=mesh, in_specs=in_specs, out_specs=out_specs, check_vma=False
    )
```

```python
import functools

import jax
import jax.numpy as jnp
from jax import lax
from jax.experimental import pallas as pl
from jax.experimental.pallas import tpu as pltpu
from jax.sharding import PartitionSpec as P

LANES = 128
SPAN = 64
GROUP = 4
EXTRA = 8


def round_up(value, step):
    return -(-value // step) * step


def pack_kernel(owner_slots, records, block, sems):
    comps, nloc, width = records.shape
    half = (block.shape[0] - EXTRA) // comps
    first = pl.multiple_of(lax.axis_index("sub") * half, half)
    copies = []
    for c in range(comps):
        source, place = records.at[c, pl.ds(first, half), :], block.at[c * half : (c + 1) * half, :]
        copies.append(pltpu.make_async_copy(source, place, sems.at[c]))
        copies[-1].start()
    lane = lax.rem(lax.broadcasted_iota(jnp.int32, (EXTRA, width), 1), half)
    line = jnp.full((EXTRA, width), -1, jnp.int32)
    for i in range(half):
        line = jnp.where(lane == i, owner_slots[first + i], line)
    block[comps * half :, :] = line.astype(jnp.float32).astype(block.dtype)
    for copy in copies:
        copy.wait()


def tables_kernel(taps, sids, offs, gap_start, gap_len, sid_col, off_col, mask, band):
    count, js = sids.shape
    refs = count * js
    nstation = gap_start.shape[1]
    for k in range(count):
        for j in range(js):
            row = k * js + j
            sid_col[row, :] = jnp.full((LANES,), sids[k, j], jnp.int32)
            off_col[row, :] = jnp.full((LANES,), offs[k, j], jnp.int32)
    own = lax.broadcasted_iota(jnp.int32, (refs, nstation), 1) == sid_col[:, :nstation]
    starts = gap_start[...].astype(jnp.float32)
    ends = starts + gap_len[...].astype(jnp.float32)
    live = jnp.ones(mask.shape, jnp.float32)
    times = lax.broadcasted_iota(jnp.int32, mask.shape, 1).astype(jnp.float32)
    for g in range(starts.shape[0]):
        first = jnp.sum(jnp.where(own, starts[g : g + 1], 0.0), axis=1, keepdims=True)
        last = jnp.sum(jnp.where(own, ends[g : g + 1], 0.0), axis=1, keepdims=True)
        live = jnp.where((times >= first) & (times < last), 0.0, live)
    mask[...] = live
    rows = lax.rem(lax.broadcasted_iota(jnp.int32, band.shape, 0), LANES)
    cols = lax.broadcasted_iota(jnp.int32, band.shape, 1)
    lead = rows + (cols // LANES) * LANES - lax.rem(cols, LANES)
    band[...] = jnp.where((lead >= 0) & (lead < taps), 1.0, 0.0).astype(jnp.bfloat16)


def filters_kernel(templates, filters, scale):
    js, comps, count, taps = templates.shape
    refs = count * js
    depth = filters.shape[2]

    def one_station(j, carry):
        for c in range(comps):
            wave = templates[j, c].astype(jnp.float32)
            wave = jnp.concatenate([wave, jnp.zeros((count, depth - taps), jnp.float32)], axis=1)
            power = jnp.sum(wave * wave, axis=1, keepdims=True) / taps
            factor = 1.0 / (taps * jnp.sqrt(power + 1e-06))
            for k in range(count):
                ch = c * refs + k * js + j
                scale[pl.ds(ch, 1), :] = jnp.broadcast_to(factor[k : k + 1], (1, LANES))
                rows = jnp.broadcast_to(wave[k : k + 1], (SPAN, depth))
                filters[ch] = pltpu.roll(rows, 0, 1, stride=1, stride_axis=0).astype(jnp.bfloat16)
        return carry

    lax.fori_loop(0, js, one_station, 0)


def correlate_kernel(comps, rows_slab, nslab, nsub, taps, *args):
    heads, args = args[:nsub], args[nsub:]
    tails, args = args[: nsub * (nslab - 1)], args[nsub * (nslab - 1) :]
    filters, scale, sid_col, off_col, mask, band = args[:6]
    keep, send, segs, low, high, norm, total = args[6:]
    refs, time = mask.shape
    ntmpl, _, width = heads[0].shape
    chunks = time // LANES
    chans = comps * refs
    count = keep.shape[1]
    js = refs // count
    tall = low.shape[1]
    here, core = lax.axis_index("slab"), lax.axis_index("sub")
    depth = nsub * ntmpl * rows_slab
    owner = []
    lines = round_up(depth, width) // width
    for q in range(lines):
        lane = lax.broadcasted_iota(jnp.int32, (1, width), 1) + q * width
        line = jnp.full((1, width), -1.0, jnp.float32)
        for b in range(nsub * ntmpl):
            tail = heads[b // ntmpl][b % ntmpl, rows_slab : rows_slab + EXTRA, :].astype(jnp.float32)
            inside = (lane >= b * rows_slab) & (lane < (b + 1) * rows_slab)
            line = jnp.where(inside, tail[q : q + 1], line)
        owner.append(line)
    owner = jnp.concatenate(owner, axis=1)[:, :depth]
    row = lax.broadcasted_iota(jnp.int32, (1, depth), 1)
    row = lax.rem(row, rows_slab) // (rows_slab // comps)
    wanted = sid_col[:, :1].astype(jnp.float32)
    match = owner == wanted
    picks = [jnp.where(match & (row == c), 1.0, 0.0).astype(jnp.bfloat16) for c in range(comps)]
    pick = jnp.concatenate(picks, axis=0)
    for d in range(nslab):
        parts = heads if d == 0 else tails[(d - 1) * nsub : d * nsub]
        stack = jnp.concatenate([part[z, :rows_slab, :] for part in parts for z in range(ntmpl)], axis=0)
        got = jnp.dot(pick, stack, preferred_element_type=jnp.float32)
        spot = pl.ds(pl.multiple_of(lax.bitwise_xor(here, d) * width, LANES), width)
        live = mask[:, spot]
        for c in range(comps):
            segs[c * refs : (c + 1) * refs, spot] = got[c * refs : (c + 1) * refs] * live
    lane = lax.broadcasted_iota(jnp.int32, (8, LANES), 1)
    zero = jnp.zeros((8, LANES), jnp.float32)
    for i in range(chans // 8):
        ref_row = (i * 8) % refs
        off = off_col[ref_row : ref_row + 8, :]
        place = lax.bitwise_and(lane + off, LANES - 1)
        fine = lax.bitwise_and(off, LANES - 1)
        near = lane + fine < LANES
        far = off >= LANES
        turned = [
            jnp.take_along_axis(segs[i * 8 : i * 8 + 8, r * LANES : (r + 1) * LANES], place, axis=1)
            for r in range(chunks)
        ]
        turned += [zero, zero]
        moved = [jnp.where(near, turned[r], turned[r + 1]) for r in range(chunks + 1)]
        for r in range(chunks):
            segs[i * 8 : i * 8 + 8, r * LANES : (r + 1) * LANES] = jnp.where(far, moved[r + 1], moved[r])
    for i in range(chans // 8):
        top = i * 8 * tall
        mine = [segs[i * 8 : i * 8 + 8, r * LANES : (r + 1) * LANES] for r in range(chunks)] + [zero]
        for r in range(chunks):
            low[pl.ds(i * 8, 8), r, :] = mine[r]
            half = jnp.where(lane < LANES - SPAN, pltpu.roll(mine[r], SPAN, 1), pltpu.roll(mine[r + 1], SPAN, 1))
            high[pl.ds(i * 8, 8), r, :] = half
        for r in range(chunks, tall):
            low[pl.ds(i * 8, 8), r, :] = zero
            high[pl.ds(i * 8, 8), r, :] = zero
    reach = band.shape[1] // LANES
    sums = {}
    for r in reversed(range(chunks)):
        part = segs[:, r * LANES : (r + 1) * LANES]
        power = part * part
        lead = power.astype(jnp.bfloat16)
        rest = (power - lead.astype(jnp.float32)).astype(jnp.bfloat16)
        sums[r] = jnp.dot(jnp.concatenate([lead, rest], axis=1), band[...], preferred_element_type=jnp.float32)
        window = sums[r][:, :LANES]
        for p in range(1, min(reach, chunks - r)):
            window = window + sums[r + p][:, p * LANES : (p + 1) * LANES]
        factor = scale[...] * lax.rsqrt(window / taps + 1e-06)
        for i in range(chans // 8):
            norm[pl.ds(i * 8, 8), r, :] = factor[i * 8 : i * 8 + 8]
    span = filters.shape[2] // LANES
    accs = [jnp.zeros((chunks, LANES), jnp.float32) for _ in range(count)]
    side = lax.broadcasted_iota(jnp.int32, (chunks, LANES), 1) < SPAN
    for base in range(0, chans, GROUP):
        rows = []
        for ch in range(base, base + GROUP):
            for source in (low, high):
                rows.append(jnp.concatenate([source[ch, p : p + chunks, :] for p in range(span)], axis=1))
        both = jnp.concatenate(rows, axis=0).astype(jnp.bfloat16)
        weights = filters[base : base + GROUP].reshape(GROUP * SPAN, span * LANES)
        res = lax.dot_general(both, weights, (((1,), (1,)), ((), ())), preferred_element_type=jnp.float32)
        for g in range(GROUP):
            left = (g // 2) * LANES
            tile = res[2 * g * chunks : 2 * (g + 1) * chunks, left : left + LANES]
            early, late = tile[:chunks], tile[chunks:]
            if g % 2 == 0:
                wide = jnp.where(side, early, pltpu.roll(late, SPAN, 1))
            else:
                wide = jnp.where(side, pltpu.roll(early, SPAN, 1), late)
            k = ((base + g) % refs) // js
            accs[k] = accs[k] + wide * norm[base + g]
    for k in range(count):
        total[k] = accs[k]
    each = chunks // (nslab * nsub)
    for d in range(nslab):
        for e in range(each):
            first = lax.bitwise_xor(here, d) * nsub * each + e
            turn = nsub - 1 if d else 0
            near = first + lax.bitwise_xor(core, turn) * each
            keep[d, :, e * LANES : (e + 1) * LANES] = total[:, near, :]
            for m in range(1, nsub):
                other = first + lax.bitwise_xor(core, m ^ turn) * each
                send[m - 1, d, :, e * LANES : (e + 1) * LANES] = total[:, other, :]


def swapped(value, axis, distance):
    return lax.ppermute(value, axis, [(i, i ^ distance) for i in range(lax.axis_size(axis))])


def on_device(records, owner_slots, gap_start, gap_len, templates, station_ids, offsets):
    nloc, comps, width = records.shape
    count, js, _, taps = templates.shape
    nslab, nsub, ntmpl = (lax.axis_size(name) for name in ("slab", "sub", "tmpl"))
    time = width * nslab
    refs = count * js
    chans = comps * refs
    here, core = lax.axis_index("slab"), lax.axis_index("sub")
    vmem, smem = pl.BlockSpec(memory_space=pltpu.VMEM), pl.BlockSpec(memory_space=pltpu.SMEM)
    half = nloc // nsub
    high = round_up(half, 16)
    rows_slab = comps * high
    if high == half:
        block = pl.pallas_call(
            pack_kernel,
            out_shape=jax.ShapeDtypeStruct((rows_slab + EXTRA, width), records.dtype),
            in_specs=[smem, pl.BlockSpec(memory_space=pl.ANY)],
            out_specs=vmem,
            scratch_shapes=[pltpu.SemaphoreType.DMA((comps,))],
            compiler_params=pltpu.CompilerParams(vmem_limit_bytes=4 << 20),
            name="pack",
        )(owner_slots, records.transpose(1, 0, 2))
    else:
        mine = lax.dynamic_slice_in_dim(records.transpose(1, 0, 2), half * core, half, 1)
        mine = jnp.pad(mine, ((0, 0), (0, high - half), (0, 0))).reshape(rows_slab, width)
        own = lax.dynamic_slice_in_dim(owner_slots, half * core, half, 0)
        index = jnp.arange(EXTRA * width, dtype=jnp.int32).reshape(1, EXTRA, width) % high
        slots = jnp.arange(half, dtype=jnp.int32)[:, None, None]
        own = jnp.sum(jnp.where(index == slots, own[:, None, None] + 1, 0), axis=0) - 1
        block = jnp.concatenate([mine, own.astype(records.dtype)], axis=0)
    if ntmpl <= 8:
        column = [block] + [swapped(block, "tmpl", d) for d in range(1, ntmpl)]
    else:
        column = list(lax.all_gather(block, "tmpl", axis=0))
    reach = round_up(taps + LANES - 1, LANES)
    tables = pl.pallas_call(
        functools.partial(tables_kernel, taps),
        out_shape=[
            jax.ShapeDtypeStruct((refs, LANES), jnp.int32),
            jax.ShapeDtypeStruct((refs, LANES), jnp.int32),
            jax.ShapeDtypeStruct((refs, time), jnp.float32),
            jax.ShapeDtypeStruct((2 * LANES, reach), jnp.bfloat16),
        ],
        in_specs=[smem, smem, vmem, vmem],
        out_specs=[vmem] * 4,
        compiler_params=pltpu.CompilerParams(vmem_limit_bytes=8 << 20),
        name="tables",
    )(station_ids, offsets, gap_start.T, gap_len.T)
    column, tables = lax.optimization_barrier((column, tables))
    head = jnp.stack(column)
    waves = jnp.stack([part[:rows_slab] for part in column])
    tails = [swapped(waves, "slab", d) for d in range(1, nslab)]
    heads = [head] + [swapped(head, "sub", m) for m in range(1, nsub)]
    depth = round_up(taps + SPAN - 1, LANES)
    bank = pl.pallas_call(
        filters_kernel,
        out_shape=[
            jax.ShapeDtypeStruct((chans, SPAN, depth), jnp.bfloat16),
            jax.ShapeDtypeStruct((chans, LANES), jnp.float32),
        ],
        in_specs=[vmem],
        out_specs=[vmem] * 2,
        compiler_params=pltpu.CompilerParams(vmem_limit_bytes=24 << 20),
        name="filters",
    )(templates.transpose(1, 2, 0, 3))
    tails, bank = lax.optimization_barrier((tails, bank))
    lasts = []
    for tail in tails:
        lasts += [tail] + [swapped(tail, "sub", m) for m in range(1, nsub)]
    chunks = time // LANES
    each = width // nsub

    def body(*args):
        correlate_kernel(comps, rows_slab, nslab, nsub, taps, *args)

    tall = chunks + 8
    keep, send = pl.pallas_call(
        body,
        out_shape=[
            jax.ShapeDtypeStruct((nslab, count, each), jnp.float32),
            jax.ShapeDtypeStruct((nsub - 1, nslab, count, each), jnp.float32),
        ],
        in_specs=[vmem] * (nsub * nslab + 6),
        out_specs=[vmem] * 2,
        scratch_shapes=[
            pltpu.VMEM((chans, time), jnp.float32),
            pltpu.VMEM((chans, tall, LANES), jnp.float32),
            pltpu.VMEM((chans, tall, LANES), jnp.float32),
            pltpu.VMEM((chans, chunks, LANES), jnp.float32),
            pltpu.VMEM((count, chunks, LANES), jnp.float32),
        ],
        compiler_params=pltpu.CompilerParams(vmem_limit_bytes=40 << 20),
        name="correlate",
    )(*heads, *lasts, *bank, *tables)
    for m in range(1, nsub):
        keep = keep + swapped(send[m - 1], "sub", m)
    lines = [keep[0]]
    for d in range(1, nslab):
        lines.append(swapped(keep[d], ("slab", "sub"), d * nsub + nsub - 1))
    result = []
    for s in range(nslab):
        line = lines[0]
        for d in range(1, nslab):
            line = jnp.where((here ^ d) == s, lines[d], line)
        result.append(line)
    return jnp.concatenate(result, axis=0)


def solution(mesh):
    in_specs = (
        P(("grp", "tmpl"), None, "slab"),
        P(("grp", "tmpl")),
        P("grp", None),
        P("grp", None),
        P(("grp", "tmpl", "slab"), "sub", None, None),
        P(("grp", "tmpl", "slab"), "sub"),
        P(("grp", "tmpl", "slab"), "sub"),
    )
    out_specs = P(("grp", "tmpl"), ("slab", "sub"))
    return jax.shard_map(
        on_device, mesh=mesh, in_specs=in_specs, out_specs=out_specs, check_vma=False
    )
```

```python
import functools

import jax
import jax.numpy as jnp
from jax import lax
from jax.experimental import pallas as pl
from jax.experimental.pallas import tpu as pltpu
from jax.sharding import PartitionSpec as P

LANES = 128
SPAN = 64
EXTRA = 8


def round_up(value, step):
    return -(-value // step) * step


def pack_kernel(owner_slots, records, block, owners, sems):
    comps, _, width = records.shape
    half = (block.shape[0] - EXTRA) // comps
    first = pl.multiple_of(lax.axis_index("sub") * half, half)
    copies = [pltpu.make_async_copy(owner_slots, owners, sems.at[comps])]
    for c in range(comps):
        source, place = records.at[c, pl.ds(first, half), :], block.at[c * half : (c + 1) * half, :]
        copies.append(pltpu.make_async_copy(source, place, sems.at[c]))
    for copy in copies:
        copy.start()
    copies[0].wait()
    lane = lax.rem(lax.broadcasted_iota(jnp.int32, (EXTRA, width), 1), half)
    line = jnp.full((EXTRA, width), -1, jnp.int32)
    for i in range(half):
        line = jnp.where(lane == i, owners[first + i], line)
    block[comps * half :, :] = line.astype(jnp.float32).astype(block.dtype)
    for copy in copies[1:]:
        copy.wait()


def tables_kernel(taps, nfar, *args):
    fars, args = args[:nfar], args[nfar:]
    sids_in, offs_in, start_in, len_in, sid_col, off_col, mask, band = args[:8]
    sids, offs, gap_start, gap_len, sems = args[8:]
    pairs = ((sids_in, sids), (offs_in, offs), (start_in, gap_start), (len_in, gap_len))
    copies = [pltpu.make_async_copy(source, place, sems.at[i]) for i, (source, place) in enumerate(pairs)]
    for copy in copies:
        copy.start()
    rows = lax.rem(lax.broadcasted_iota(jnp.int32, band.shape, 0), LANES)
    cols = lax.broadcasted_iota(jnp.int32, band.shape, 1)
    lead = rows + (cols // LANES) * LANES - lax.rem(cols, LANES)
    band[...] = jnp.where((lead >= 0) & (lead < taps), 1.0, 0.0).astype(jnp.bfloat16)
    for copy in copies:
        copy.wait()
    count, js = sids.shape
    refs = count * js
    nstation = gap_start.shape[1]
    for k in range(count):
        for j in range(js):
            row = j * count + k
            off_col[row, :] = jnp.full((LANES,), offs[k, j], jnp.int32)
            for d, source in enumerate((sids,) + tuple(fars)):
                sid_col[d, row, :] = jnp.full((LANES,), source[k, j], jnp.int32)
    own = lax.broadcasted_iota(jnp.int32, (refs, nstation), 1) == sid_col[0, :, :nstation]
    starts = gap_start[...].astype(jnp.float32)
    ends = starts + gap_len[...].astype(jnp.float32)
    live = jnp.ones(mask.shape, jnp.float32)
    times = lax.broadcasted_iota(jnp.int32, mask.shape, 1).astype(jnp.float32)
    for g in range(starts.shape[0]):
        first = jnp.sum(jnp.where(own, starts[g : g + 1], 0.0), axis=1, keepdims=True)
        last = jnp.sum(jnp.where(own, ends[g : g + 1], 0.0), axis=1, keepdims=True)
        live = jnp.where((times >= first) & (times < last), 0.0, live)
    mask[...] = live


def filters_kernel(begin, templates, filters, scale):
    js, comps, count, taps = templates.shape
    groups, depth, _ = filters.shape

    def one_group(i, carry):
        g = begin + i
        wave = templates[lax.rem(g, js), g // js].astype(jnp.float32)
        wave = jnp.concatenate([wave, jnp.zeros((count, depth - taps), jnp.float32)], axis=1)
        power = jnp.sum(wave * wave, axis=1, keepdims=True) / taps
        factor = 1.0 / (taps * jnp.sqrt(power + 1e-06))
        rows = []
        for k in range(count):
            scale[pl.ds(i * count + k, 1), :] = jnp.broadcast_to(factor[k : k + 1], (1, LANES))
            row = jnp.broadcast_to(wave[k : k + 1], (SPAN, depth))
            rows.append(pltpu.roll(row, 0, 1, stride=1, stride_axis=0))
        filters[i] = jnp.concatenate(rows, axis=0).T.astype(jnp.bfloat16)
        return carry

    lax.fori_loop(0, groups, one_group, 0)


def select_kernel(comps, rows_slab, nsub, *args):
    heads, (sid_col, mask, near), fars = args[:nsub], args[nsub : nsub + 3], args[nsub + 3 :]
    refs = mask.shape[0]
    ntmpl, _, width = heads[0].shape
    here = lax.axis_index("slab")
    depth = nsub * ntmpl * rows_slab
    owner = []
    for q in range(round_up(depth, width) // width):
        lane = lax.broadcasted_iota(jnp.int32, (1, width), 1) + q * width
        line = jnp.full((1, width), -1.0, jnp.float32)
        for b in range(nsub * ntmpl):
            tail = heads[b // ntmpl][b % ntmpl, rows_slab : rows_slab + EXTRA, :].astype(jnp.float32)
            inside = (lane >= b * rows_slab) & (lane < (b + 1) * rows_slab)
            line = jnp.where(inside, tail[q : q + 1], line)
        owner.append(line)
    owner = jnp.concatenate(owner, axis=1)[:, :depth]
    row = lax.broadcasted_iota(jnp.int32, (1, depth), 1)
    row = lax.rem(row, rows_slab) // (rows_slab // comps)
    stack = jnp.concatenate([part[z, :rows_slab, :] for part in heads for z in range(ntmpl)], axis=0)
    owners = [jnp.where(row == c, owner, -1.0) for c in range(comps)]
    for d, out in enumerate((near,) + tuple(fars)):
        wanted = sid_col[d, :, :1].astype(jnp.float32)
        pick = [jnp.where(owners[c] == wanted, 1.0, 0.0).astype(jnp.bfloat16) for c in range(comps)]
        got = jnp.dot(jnp.concatenate(pick, axis=0), stack, preferred_element_type=jnp.float32)
        if d:
            out[...] = got.astype(out.dtype)
        else:
            live = mask[:, pl.ds(pl.multiple_of(here * width, LANES), width)]
            for c in range(comps):
                out[c * refs : (c + 1) * refs, :] = got[c * refs : (c + 1) * refs] * live


def correlate_kernel(nslab, nsub, taps, nbank, *args):
    near, fars, args = args[0], args[1:nslab], args[nslab:]
    banks, scales, args = args[:nbank], args[nbank : 2 * nbank], args[2 * nbank :]
    off_col, mask, band, keep, send, segs, low, high, norm, total = args
    refs, time = mask.shape
    chans, width = near.shape
    comps = chans // refs
    chunks = time // LANES
    count = keep.shape[1]
    tall = low.shape[1]
    here, core = lax.axis_index("slab"), lax.axis_index("sub")
    for d in range(nslab):
        spot = pl.ds(pl.multiple_of(lax.bitwise_xor(here, d) * width, LANES), width)
        if d == 0:
            segs[:, spot] = near[...]
        else:
            live = mask[:, spot]
            for c in range(comps):
                got = fars[d - 1][c * refs : (c + 1) * refs, :].astype(jnp.float32)
                segs[c * refs : (c + 1) * refs, spot] = got * live
    lane = lax.broadcasted_iota(jnp.int32, (8, LANES), 1)
    zero = jnp.zeros((8, LANES), jnp.float32)
    for i in range(chans // 8):
        ref_row = (i * 8) % refs
        off = off_col[ref_row : ref_row + 8, :]
        place = lax.bitwise_and(lane + off, LANES - 1)
        fine = lax.bitwise_and(off, LANES - 1)
        close = lane + fine < LANES
        far = off >= LANES
        turned = [
            jnp.take_along_axis(segs[i * 8 : i * 8 + 8, r * LANES : (r + 1) * LANES], place, axis=1)
            for r in range(chunks)
        ]
        turned += [zero, zero]
        moved = [jnp.where(close, turned[r], turned[r + 1]) for r in range(chunks + 1)]
        mine = [jnp.where(far, moved[r + 1], moved[r]) for r in range(chunks)] + [zero]
        for r in range(chunks):
            segs[i * 8 : i * 8 + 8, r * LANES : (r + 1) * LANES] = mine[r]
            low[pl.ds(i * 8, 8), r, :] = mine[r]
            half = jnp.where(lane < LANES - SPAN, pltpu.roll(mine[r], SPAN, 1), pltpu.roll(mine[r + 1], SPAN, 1))
            high[pl.ds(i * 8, 8), r, :] = half
        for r in range(chunks, tall):
            low[pl.ds(i * 8, 8), r, :] = zero
            high[pl.ds(i * 8, 8), r, :] = zero
    reach = band.shape[1] // LANES
    scale = jnp.concatenate([part[...] for part in scales], axis=0)
    sums = {}
    for r in reversed(range(chunks)):
        part = segs[:, r * LANES : (r + 1) * LANES]
        power = part * part
        lead = power.astype(jnp.bfloat16)
        rest = (power - lead.astype(jnp.float32)).astype(jnp.bfloat16)
        sums[r] = jnp.dot(jnp.concatenate([lead, rest], axis=1), band[...], preferred_element_type=jnp.float32)
        window = sums[r][:, :LANES]
        for p in range(1, min(reach, chunks - r)):
            window = window + sums[r + p][:, p * LANES : (p + 1) * LANES]
        factor = scale * lax.rsqrt(window / taps + 1e-06)
        for i in range(chans // 8):
            norm[pl.ds(i * 8, 8), r, :] = factor[i * 8 : i * 8 + 8]
    span = banks[0].shape[1] // LANES
    accs = [jnp.zeros((chunks, LANES), jnp.float32) for _ in range(count)]
    side = lax.broadcasted_iota(jnp.int32, (chunks, LANES), 1) < SPAN
    weights = [(bank, i) for bank in banks for i in range(bank.shape[0])]
    for g, (bank, i) in enumerate(weights):
        base = g * count
        rows = []
        for ch in range(base, base + count):
            for source in (low, high):
                rows.append(jnp.concatenate([source[ch, p : p + chunks, :] for p in range(span)], axis=1))
        both = jnp.concatenate(rows, axis=0).astype(jnp.bfloat16)
        res = jnp.dot(both, bank[i], preferred_element_type=jnp.float32)
        for k in range(count):
            left = (k // 2) * LANES
            tile = res[2 * k * chunks : 2 * (k + 1) * chunks, left : left + LANES]
            early, late = tile[:chunks], tile[chunks:]
            if k % 2 == 0:
                wide = jnp.where(side, early, pltpu.roll(late, SPAN, 1))
            else:
                wide = jnp.where(side, pltpu.roll(early, SPAN, 1), late)
            accs[k] = accs[k] + wide * norm[base + k]
    for k in range(count):
        total[k] = accs[k]
    each = chunks // (nslab * nsub)
    for d in range(nslab):
        for e in range(each):
            first = lax.bitwise_xor(here, d) * nsub * each + e
            turn = nsub - 1 if d else 0
            mine = first + lax.bitwise_xor(core, turn) * each
            keep[d, :, e * LANES : (e + 1) * LANES] = total[:, mine, :]
            for m in range(1, nsub):
                other = first + lax.bitwise_xor(core, m ^ turn) * each
                send[m - 1, d, :, e * LANES : (e + 1) * LANES] = total[:, other, :]


def swapped(value, axis, distance):
    return lax.ppermute(value, axis, [(i, i ^ distance) for i in range(lax.axis_size(axis))])


def params(mib):
    return pltpu.CompilerParams(vmem_limit_bytes=mib << 20)


def on_device(records, owner_slots, gap_start, gap_len, templates, station_ids, offsets):
    nloc, comps, width = records.shape
    count, js, _, taps = templates.shape
    nslab, nsub, ntmpl = (lax.axis_size(name) for name in ("slab", "sub", "tmpl"))
    time = width * nslab
    refs = count * js
    chans = comps * refs
    here, core = lax.axis_index("slab"), lax.axis_index("sub")
    vmem, smem = pl.BlockSpec(memory_space=pltpu.VMEM), pl.BlockSpec(memory_space=pltpu.SMEM)
    hbm = pl.BlockSpec(memory_space=pltpu.HBM)
    half = nloc // nsub
    high = round_up(half, 16)
    rows_slab = comps * high
    if high == half:
        block = pl.pallas_call(
            pack_kernel,
            out_shape=jax.ShapeDtypeStruct((rows_slab + EXTRA, width), records.dtype),
            in_specs=[hbm, hbm],
            out_specs=vmem,
            scratch_shapes=[pltpu.SMEM((nloc,), jnp.int32), pltpu.SemaphoreType.DMA((comps + 1,))],
            compiler_params=params(4),
            name="pack",
        )(owner_slots, records.transpose(1, 0, 2))
    else:
        mine = lax.dynamic_slice_in_dim(records.transpose(1, 0, 2), half * core, half, 1)
        mine = jnp.pad(mine, ((0, 0), (0, high - half), (0, 0))).reshape(rows_slab, width)
        own = lax.dynamic_slice_in_dim(owner_slots, half * core, half, 0)
        index = jnp.arange(EXTRA * width, dtype=jnp.int32).reshape(1, EXTRA, width) % high
        slots = jnp.arange(half, dtype=jnp.int32)[:, None, None]
        own = jnp.sum(jnp.where(index == slots, own[:, None, None] + 1, 0), axis=0) - 1
        block = jnp.concatenate([mine, own.astype(records.dtype)], axis=0)
    if ntmpl <= 8:
        column = [block] + [swapped(block, "tmpl", d) for d in range(1, ntmpl)]
    else:
        column = list(lax.all_gather(block, "tmpl", axis=0))
    asked = [swapped(station_ids, "slab", d) for d in range(1, nslab)]
    reach = round_up(taps + LANES - 1, LANES)
    sid_col, off_col, mask, band = pl.pallas_call(
        functools.partial(tables_kernel, taps, nslab - 1),
        out_shape=[
            jax.ShapeDtypeStruct((nslab, refs, LANES), jnp.int32),
            jax.ShapeDtypeStruct((refs, LANES), jnp.int32),
            jax.ShapeDtypeStruct((refs, time), jnp.float32),
            jax.ShapeDtypeStruct((2 * LANES, reach), jnp.bfloat16),
        ],
        in_specs=[smem] * (nslab - 1) + [hbm] * 4,
        out_specs=[vmem] * 4,
        scratch_shapes=[
            pltpu.SMEM(station_ids.shape, jnp.int32),
            pltpu.SMEM(offsets.shape, jnp.int32),
            pltpu.VMEM(gap_start.T.shape, jnp.int32),
            pltpu.VMEM(gap_len.T.shape, jnp.int32),
            pltpu.SemaphoreType.DMA((4,)),
        ],
        compiler_params=params(8),
        name="tables",
    )(*asked, station_ids, offsets, gap_start.T, gap_len.T)
    depth = round_up(taps + SPAN - 1, LANES)
    waves = templates.transpose(1, 2, 0, 3)

    def bank(begin, groups, source):
        return pl.pallas_call(
            functools.partial(filters_kernel, begin),
            out_shape=[
                jax.ShapeDtypeStruct((groups, depth, count * SPAN), jnp.bfloat16),
                jax.ShapeDtypeStruct((groups * count, LANES), jnp.float32),
            ],
            in_specs=[vmem],
            out_specs=[vmem] * 2,
            compiler_params=params(16),
            name="filters",
        )(source)

    groups = comps * js
    early = groups // 2 // 2 * 2
    bank_a, scale_a = bank(0, early, waves)
    column, bank_a, mask = lax.optimization_barrier((column, bank_a, mask))
    head = jnp.stack(column)
    heads = [head] + [swapped(head, "sub", m) for m in range(1, nsub)]
    near, *fars = pl.pallas_call(
        functools.partial(select_kernel, comps, rows_slab, nsub),
        out_shape=[jax.ShapeDtypeStruct((chans, width), jnp.float32)]
        + [jax.ShapeDtypeStruct((chans, width), records.dtype)] * (nslab - 1),
        in_specs=[vmem] * (nsub + 2),
        out_specs=[vmem] * nslab,
        compiler_params=params(16),
        name="select",
    )(*heads, sid_col, mask)
    fars = [swapped(far, "slab", d + 1) for d, far in enumerate(fars)]
    bank_b, scale_b = bank(early, groups - early, waves)
    fars, bank_b = lax.optimization_barrier((fars, bank_b))
    chunks = time // LANES
    each = width // nsub
    tall = chunks + 8
    keep, send = pl.pallas_call(
        functools.partial(correlate_kernel, nslab, nsub, taps, 2),
        out_shape=[
            jax.ShapeDtypeStruct((nslab, count, each), jnp.float32),
            jax.ShapeDtypeStruct((nsub - 1, nslab, count, each), jnp.float32),
        ],
        in_specs=[vmem] * (nslab + 7),
        out_specs=[vmem] * 2,
        scratch_shapes=[
            pltpu.VMEM((chans, time), jnp.float32),
            pltpu.VMEM((chans, tall, LANES), jnp.float32),
            pltpu.VMEM((chans, tall, LANES), jnp.float32),
            pltpu.VMEM((chans, chunks, LANES), jnp.float32),
            pltpu.VMEM((count, chunks, LANES), jnp.float32),
        ],
        compiler_params=params(32),
        name="correlate",
    )(near, *fars, bank_a, bank_b, scale_a, scale_b, off_col, mask, band)
    for m in range(1, nsub):
        keep = keep + swapped(send[m - 1], "sub", m)
    lines = [keep[0]]
    for d in range(1, nslab):
        lines.append(swapped(keep[d], ("slab", "sub"), d * nsub + nsub - 1))
    result = []
    for s in range(nslab):
        line = lines[0]
        for d in range(1, nslab):
            line = jnp.where((here ^ d) == s, lines[d], line)
        result.append(line)
    return jnp.concatenate(result, axis=0)


def solution(mesh):
    in_specs = (
        P(("grp", "tmpl"), None, "slab"),
        P(("grp", "tmpl")),
        P("grp", None),
        P("grp", None),
        P(("grp", "tmpl", "slab"), "sub", None, None),
        P(("grp", "tmpl", "slab"), "sub"),
        P(("grp", "tmpl", "slab"), "sub"),
    )
    out_specs = P(("grp", "tmpl"), ("slab", "sub"))
    return jax.shard_map(
        on_device, mesh=mesh, in_specs=in_specs, out_specs=out_specs, check_vma=False
    )
```

```python
import functools

import jax
import jax.numpy as jnp
from jax import lax
from jax.experimental import pallas as pl
from jax.experimental.pallas import tpu as pltpu
from jax.sharding import PartitionSpec as P

LANES = 128
SPAN = 64
EXTRA = 8


def round_up(value, step):
    return -(-value // step) * step


def pack_kernel(owner_slots, records, block, owners, sems):
    comps, _, width = records.shape
    half = (block.shape[0] - EXTRA) // comps
    first = pl.multiple_of(lax.axis_index("sub") * half, half)
    copies = [pltpu.make_async_copy(owner_slots, owners, sems.at[comps])]
    for c in range(comps):
        source, place = records.at[c, pl.ds(first, half), :], block.at[c * half : (c + 1) * half, :]
        copies.append(pltpu.make_async_copy(source, place, sems.at[c]))
    for copy in copies:
        copy.start()
    copies[0].wait()
    lane = lax.rem(lax.broadcasted_iota(jnp.int32, (EXTRA, width), 1), half)
    line = jnp.full((EXTRA, width), -1, jnp.int32)
    for i in range(half):
        line = jnp.where(lane == i, owners[first + i], line)
    block[comps * half :, :] = line.astype(jnp.float32).astype(block.dtype)
    for copy in copies[1:]:
        copy.wait()


def tables_kernel(sids_in, offs_in, start_in, len_in, waves_in, sid_col, off_col, mask, band, scale, waves, *scratch):
    sids, offs, gap_start, gap_len, sems = scratch
    pairs = ((waves_in, waves), (sids_in, sids), (offs_in, offs), (start_in, gap_start), (len_in, gap_len))
    copies = [pltpu.make_async_copy(source, place, sems.at[i]) for i, (source, place) in enumerate(pairs)]
    for copy in copies:
        copy.start()
    js, comps, count, taps = waves.shape
    refs = count * js
    rows = lax.rem(lax.broadcasted_iota(jnp.int32, band.shape, 0), LANES)
    cols = lax.broadcasted_iota(jnp.int32, band.shape, 1)
    lead = rows + (cols // LANES) * LANES - lax.rem(cols, LANES)
    band[...] = jnp.where((lead >= 0) & (lead < taps), 1.0, 0.0).astype(jnp.bfloat16)
    for copy in copies:
        copy.wait()
    for k in range(count):
        for j in range(js):
            row = j * count + k
            off_col[row, :] = jnp.full((LANES,), offs[k, j], jnp.int32)
            sid_col[row, :] = jnp.full((LANES,), sids[k, j], jnp.int32)
    nstation = gap_start.shape[1]
    own = lax.broadcasted_iota(jnp.int32, (refs, nstation), 1) == sid_col[:, :nstation]
    starts = gap_start[...].astype(jnp.float32)
    ends = starts + gap_len[...].astype(jnp.float32)
    live = jnp.ones(mask.shape, jnp.float32)
    times = lax.broadcasted_iota(jnp.int32, mask.shape, 1).astype(jnp.float32)
    for g in range(starts.shape[0]):
        first = jnp.sum(jnp.where(own, starts[g : g + 1], 0.0), axis=1, keepdims=True)
        last = jnp.sum(jnp.where(own, ends[g : g + 1], 0.0), axis=1, keepdims=True)
        live = jnp.where((times >= first) & (times < last), 0.0, live)
    mask[...] = live
    for c in range(comps):
        for j in range(js):
            wave = waves[j, c].astype(jnp.float32)
            power = jnp.sum(wave * wave, axis=1, keepdims=True) / taps
            factor = 1.0 / (taps * jnp.sqrt(power + 1e-06))
            first = (c * js + j) * count
            scale[first : first + count, :] = jnp.broadcast_to(factor, (count, LANES))


def filters_kernel(begin, waves, filters):
    js, _, count, taps = waves.shape
    groups, depth, _ = filters.shape

    def one_group(i, carry):
        g = begin + i
        wave = waves[lax.rem(g, js), g // js].astype(jnp.float32)
        wave = jnp.concatenate([wave, jnp.zeros((count, depth - taps), jnp.float32)], axis=1)
        rows = []
        for k in range(count):
            row = jnp.broadcast_to(wave[k : k + 1], (SPAN, depth))
            rows.append(pltpu.roll(row, 0, 1, stride=1, stride_axis=0))
        filters[i] = jnp.concatenate(rows, axis=0).T.astype(jnp.bfloat16)
        return carry

    lax.fori_loop(0, groups, one_group, 0, unroll=5)


def select_kernel(comps, rows_slab, nsub, *args):
    heads, args = args[:nsub], args[nsub:]
    nslab = len(args) // 2
    sid_cols, mask, outs = args[:nslab], args[nslab], args[nslab + 1 :]
    refs = mask.shape[0]
    ntmpl, _, width = heads[0].shape
    here = lax.axis_index("slab")
    depth = nsub * ntmpl * rows_slab
    owner = []
    for q in range(round_up(depth, width) // width):
        lane = lax.broadcasted_iota(jnp.int32, (1, width), 1) + q * width
        line = jnp.full((1, width), -1.0, jnp.float32)
        for b in range(nsub * ntmpl):
            tail = heads[b // ntmpl][b % ntmpl, rows_slab : rows_slab + EXTRA, :].astype(jnp.float32)
            inside = (lane >= b * rows_slab) & (lane < (b + 1) * rows_slab)
            line = jnp.where(inside, tail[q : q + 1], line)
        owner.append(line)
    owner = jnp.concatenate(owner, axis=1)[:, :depth]
    row = lax.broadcasted_iota(jnp.int32, (1, depth), 1)
    row = lax.rem(row, rows_slab) // (rows_slab // comps)
    stack = jnp.concatenate([part[z, :rows_slab, :] for part in heads for z in range(ntmpl)], axis=0)
    owners = [jnp.where(row == c, owner, -1.0) for c in range(comps)]
    for d, out in enumerate(outs):
        wanted = sid_cols[d][:, :1].astype(jnp.float32)
        pick = [jnp.where(owners[c] == wanted, 1.0, 0.0).astype(jnp.bfloat16) for c in range(comps)]
        got = jnp.dot(jnp.concatenate(pick, axis=0), stack, preferred_element_type=jnp.float32)
        if d:
            out[...] = got.astype(out.dtype)
        else:
            live = mask[:, pl.ds(pl.multiple_of(here * width, LANES), width)]
            for c in range(comps):
                out[c * refs : (c + 1) * refs, :] = got[c * refs : (c + 1) * refs] * live


def correlate_kernel(nslab, nsub, taps, nbank, *args):
    near, fars, args = args[0], args[1:nslab], args[nslab:]
    banks, args = args[:nbank], args[nbank:]
    off_col, mask, band, scale, keep, send, segs, low, high, norm, total = args
    refs, time = mask.shape
    chans, width = near.shape
    comps = chans // refs
    chunks = time // LANES
    count = keep.shape[1]
    tall = low.shape[1]
    here, core = lax.axis_index("slab"), lax.axis_index("sub")
    for d in range(nslab):
        spot = pl.ds(pl.multiple_of(lax.bitwise_xor(here, d) * width, LANES), width)
        if d == 0:
            segs[:, spot] = near[...]
        else:
            live = mask[:, spot]
            for c in range(comps):
                got = fars[d - 1][c * refs : (c + 1) * refs, :].astype(jnp.float32)
                segs[c * refs : (c + 1) * refs, spot] = got * live
    lane = lax.broadcasted_iota(jnp.int32, (8, LANES), 1)
    zero = jnp.zeros((8, LANES), jnp.float32)
    for i in range(chans // 8):
        ref_row = (i * 8) % refs
        off = off_col[ref_row : ref_row + 8, :]
        place = lax.bitwise_and(lane + off, LANES - 1)
        fine = lax.bitwise_and(off, LANES - 1)
        close = lane + fine < LANES
        far = off >= LANES
        turned = [
            jnp.take_along_axis(segs[i * 8 : i * 8 + 8, r * LANES : (r + 1) * LANES], place, axis=1)
            for r in range(chunks)
        ]
        turned += [zero, zero]
        moved = [jnp.where(close, turned[r], turned[r + 1]) for r in range(chunks + 1)]
        mine = [jnp.where(far, moved[r + 1], moved[r]) for r in range(chunks)] + [zero]
        for r in range(chunks):
            segs[i * 8 : i * 8 + 8, r * LANES : (r + 1) * LANES] = mine[r]
            low[pl.ds(i * 8, 8), r, :] = mine[r]
            half = jnp.where(lane < LANES - SPAN, pltpu.roll(mine[r], SPAN, 1), pltpu.roll(mine[r + 1], SPAN, 1))
            high[pl.ds(i * 8, 8), r, :] = half
        for r in range(chunks, tall):
            low[pl.ds(i * 8, 8), r, :] = zero
            high[pl.ds(i * 8, 8), r, :] = zero
    reach = band.shape[1] // LANES
    sums = {}
    for r in reversed(range(chunks)):
        part = segs[:, r * LANES : (r + 1) * LANES]
        power = part * part
        lead = power.astype(jnp.bfloat16)
        rest = (power - lead.astype(jnp.float32)).astype(jnp.bfloat16)
        sums[r] = jnp.dot(jnp.concatenate([lead, rest], axis=1), band[...], preferred_element_type=jnp.float32)
        window = sums[r][:, :LANES]
        for p in range(1, min(reach, chunks - r)):
            window = window + sums[r + p][:, p * LANES : (p + 1) * LANES]
        factor = scale[...] * lax.rsqrt(window / taps + 1e-06)
        for i in range(chans // 8):
            norm[pl.ds(i * 8, 8), r, :] = factor[i * 8 : i * 8 + 8]
    span = banks[0].shape[1] // LANES
    accs = [jnp.zeros((chunks, LANES), jnp.float32) for _ in range(count)]
    side = lax.broadcasted_iota(jnp.int32, (chunks, LANES), 1) < SPAN
    weights = [(bank, i) for bank in banks for i in range(bank.shape[0])]
    for g, (bank, i) in enumerate(weights):
        base = g * count
        rows = []
        for ch in range(base, base + count):
            for source in (low, high):
                rows.append(jnp.concatenate([source[ch, p : p + chunks, :] for p in range(span)], axis=1))
        both = jnp.concatenate(rows, axis=0).astype(jnp.bfloat16)
        res = jnp.dot(both, bank[i], preferred_element_type=jnp.float32)
        for k in range(count):
            left = (k // 2) * LANES
            tile = res[2 * k * chunks : 2 * (k + 1) * chunks, left : left + LANES]
            early, late = tile[:chunks], tile[chunks:]
            if k % 2 == 0:
                wide = jnp.where(side, early, pltpu.roll(late, SPAN, 1))
            else:
                wide = jnp.where(side, pltpu.roll(early, SPAN, 1), late)
            accs[k] = accs[k] + wide * norm[base + k]
    for k in range(count):
        total[k] = accs[k]
    each = chunks // (nslab * nsub)
    for d in range(nslab):
        for e in range(each):
            first = lax.bitwise_xor(here, d) * nsub * each + e
            turn = nsub - 1 if d else 0
            mine = first + lax.bitwise_xor(core, turn) * each
            keep[d, :, e * LANES : (e + 1) * LANES] = total[:, mine, :]
            for m in range(1, nsub):
                other = first + lax.bitwise_xor(core, m ^ turn) * each
                send[m - 1, d, :, e * LANES : (e + 1) * LANES] = total[:, other, :]


def swapped(value, axis, distance):
    return lax.ppermute(value, axis, [(i, i ^ distance) for i in range(lax.axis_size(axis))])


def stays(value):
    return pltpu.with_memory_space_constraint(value, pltpu.HBM)


def params(mib):
    return pltpu.CompilerParams(vmem_limit_bytes=mib << 20)


def on_device(records, owner_slots, gap_start, gap_len, templates, station_ids, offsets):
    nloc, comps, width = records.shape
    count, js, _, taps = templates.shape
    nslab, nsub, ntmpl = (lax.axis_size(name) for name in ("slab", "sub", "tmpl"))
    time = width * nslab
    refs = count * js
    chans = comps * refs
    here, core = lax.axis_index("slab"), lax.axis_index("sub")
    vmem, smem = pl.BlockSpec(memory_space=pltpu.VMEM), pl.BlockSpec(memory_space=pltpu.SMEM)
    hbm = pl.BlockSpec(memory_space=pltpu.HBM)
    half = nloc // nsub
    high = round_up(half, 16)
    rows_slab = comps * high
    if high == half:
        block = pl.pallas_call(
            pack_kernel,
            out_shape=jax.ShapeDtypeStruct((rows_slab + EXTRA, width), records.dtype),
            in_specs=[hbm, hbm],
            out_specs=vmem,
            scratch_shapes=[pltpu.SMEM((nloc,), jnp.int32), pltpu.SemaphoreType.DMA((comps + 1,))],
            compiler_params=params(4),
            name="pack",
        )(stays(owner_slots), stays(records.transpose(1, 0, 2)))
    else:
        mine = lax.dynamic_slice_in_dim(records.transpose(1, 0, 2), half * core, half, 1)
        mine = jnp.pad(mine, ((0, 0), (0, high - half), (0, 0))).reshape(rows_slab, width)
        own = lax.dynamic_slice_in_dim(owner_slots, half * core, half, 0)
        index = jnp.arange(EXTRA * width, dtype=jnp.int32).reshape(1, EXTRA, width) % high
        slots = jnp.arange(half, dtype=jnp.int32)[:, None, None]
        own = jnp.sum(jnp.where(index == slots, own[:, None, None] + 1, 0), axis=0) - 1
        block = jnp.concatenate([mine, own.astype(records.dtype)], axis=0)
    if ntmpl <= 8:
        column = [block] + [swapped(block, "tmpl", d) for d in range(1, ntmpl)]
    else:
        column = list(lax.all_gather(block, "tmpl", axis=0))
    waves = templates.transpose(1, 2, 0, 3)
    reach = round_up(taps + LANES - 1, LANES)
    sid_col, off_col, mask, band, scale, waves = pl.pallas_call(
        tables_kernel,
        out_shape=[
            jax.ShapeDtypeStruct((refs, LANES), jnp.int32),
            jax.ShapeDtypeStruct((refs, LANES), jnp.int32),
            jax.ShapeDtypeStruct((refs, time), jnp.float32),
            jax.ShapeDtypeStruct((2 * LANES, reach), jnp.bfloat16),
            jax.ShapeDtypeStruct((chans, LANES), jnp.float32),
            jax.ShapeDtypeStruct(waves.shape, waves.dtype),
        ],
        in_specs=[hbm] * 5,
        out_specs=[vmem] * 6,
        scratch_shapes=[
            pltpu.SMEM(station_ids.shape, jnp.int32),
            pltpu.SMEM(offsets.shape, jnp.int32),
            pltpu.VMEM(gap_start.T.shape, jnp.int32),
            pltpu.VMEM(gap_len.T.shape, jnp.int32),
            pltpu.SemaphoreType.DMA((5,)),
        ],
        compiler_params=params(8),
        name="tables",
    )(*[stays(value) for value in (station_ids, offsets, gap_start.T, gap_len.T, waves)])
    sid_cols = [sid_col] + [swapped(sid_col, "slab", d) for d in range(1, nslab)]
    depth = round_up(taps + SPAN - 1, LANES)

    def bank(begin, groups):
        return pl.pallas_call(
            functools.partial(filters_kernel, begin),
            out_shape=jax.ShapeDtypeStruct((groups, depth, count * SPAN), jnp.bfloat16),
            in_specs=[vmem],
            out_specs=vmem,
            compiler_params=params(16),
            name="filters",
        )(waves)

    groups = comps * js
    early = groups // 3
    bank_a = bank(0, early)
    column, sid_cols, bank_a = lax.optimization_barrier((column, sid_cols, bank_a))
    head = jnp.stack(column)
    heads = [head] + [swapped(head, "sub", m) for m in range(1, nsub)]
    near, *fars = pl.pallas_call(
        functools.partial(select_kernel, comps, rows_slab, nsub),
        out_shape=[jax.ShapeDtypeStruct((chans, width), jnp.float32)]
        + [jax.ShapeDtypeStruct((chans, width), records.dtype)] * (nslab - 1),
        in_specs=[vmem] * (nsub + nslab + 1),
        out_specs=[vmem] * nslab,
        compiler_params=params(16),
        name="select",
    )(*heads, *sid_cols, mask)
    fars = [swapped(far, "slab", d + 1) for d, far in enumerate(fars)]
    bank_b = bank(early, groups - early)
    fars, bank_b = lax.optimization_barrier((fars, bank_b))
    chunks = time // LANES
    each = width // nsub
    tall = chunks + 8
    keep, send = pl.pallas_call(
        functools.partial(correlate_kernel, nslab, nsub, taps, 2),
        out_shape=[
            jax.ShapeDtypeStruct((nslab, count, each), jnp.float32),
            jax.ShapeDtypeStruct((nsub - 1, nslab, count, each), jnp.float32),
        ],
        in_specs=[vmem] * (nslab + 6),
        out_specs=[vmem] * 2,
        scratch_shapes=[
            pltpu.VMEM((chans, time), jnp.float32),
            pltpu.VMEM((chans, tall, LANES), jnp.float32),
            pltpu.VMEM((chans, tall, LANES), jnp.float32),
            pltpu.VMEM((chans, chunks, LANES), jnp.float32),
            pltpu.VMEM((count, chunks, LANES), jnp.float32),
        ],
        compiler_params=params(32),
        name="correlate",
    )(near, *fars, bank_a, bank_b, off_col, mask, band, scale)
    for m in range(1, nsub):
        keep = keep + swapped(send[m - 1], "sub", m)
    lines = [keep[0]]
    for d in range(1, nslab):
        lines.append(swapped(keep[d], ("slab", "sub"), d * nsub + nsub - 1))
    result = []
    for s in range(nslab):
        line = lines[0]
        for d in range(1, nslab):
            line = jnp.where((here ^ d) == s, lines[d], line)
        result.append(line)
    return jnp.concatenate(result, axis=0)


def solution(mesh):
    in_specs = (
        P(("grp", "tmpl"), None, "slab"),
        P(("grp", "tmpl")),
        P("grp", None),
        P("grp", None),
        P(("grp", "tmpl", "slab"), "sub", None, None),
        P(("grp", "tmpl", "slab"), "sub"),
        P(("grp", "tmpl", "slab"), "sub"),
    )
    out_specs = P(("grp", "tmpl"), ("slab", "sub"))
    return jax.shard_map(
        on_device, mesh=mesh, in_specs=in_specs, out_specs=out_specs, check_vma=False
    )
```

```python
import functools

import jax
import jax.numpy as jnp
from jax import lax
from jax.experimental import pallas as pl
from jax.experimental.pallas import tpu as pltpu
from jax.sharding import PartitionSpec as P

LANES = 128
SPAN = 64
EXTRA = 8


def round_up(value, step):
    return -(-value // step) * step


def pack_kernel(owner_slots, records, block, owners, sems):
    comps, _, width = records.shape
    per = width // LANES
    half = (block.shape[0] - EXTRA) // (comps * per)
    first = pl.multiple_of(lax.axis_index("sub") * half, half)
    copies = [pltpu.make_async_copy(owner_slots, owners, sems.at[comps * per])]
    for i in range(comps * per):
        source = records.at[i // per, pl.ds(first, half), (i % per) * LANES : (i % per + 1) * LANES]
        copies.append(pltpu.make_async_copy(source, block.at[i * half : (i + 1) * half, :], sems.at[i]))
    for copy in copies:
        copy.start()
    copies[0].wait()
    lane = lax.rem(lax.broadcasted_iota(jnp.int32, (EXTRA, LANES), 1), half)
    line = jnp.full((EXTRA, LANES), -1, jnp.int32)
    for i in range(half):
        line = jnp.where(lane == i, owners[first + i], line)
    block[comps * per * half :, :] = line.astype(jnp.float32).astype(block.dtype)
    for copy in copies[1:]:
        copy.wait()


def tables_kernel(sids_in, offs_in, start_in, len_in, waves_in, sid_col, off_col, mask, band, scale, waves, *scratch):
    sids, offs, gap_start, gap_len, sems = scratch
    pairs = ((waves_in, waves), (sids_in, sids), (offs_in, offs), (start_in, gap_start), (len_in, gap_len))
    copies = [pltpu.make_async_copy(source, place, sems.at[i]) for i, (source, place) in enumerate(pairs)]
    for copy in copies:
        copy.start()
    js, comps, count, taps = waves.shape
    refs = count * js
    rows = lax.rem(lax.broadcasted_iota(jnp.int32, band.shape, 0), LANES)
    cols = lax.broadcasted_iota(jnp.int32, band.shape, 1)
    lead = rows + (cols // LANES) * LANES - lax.rem(cols, LANES)
    band[...] = jnp.where((lead >= 0) & (lead < taps), 1.0, 0.0).astype(jnp.bfloat16)
    for copy in copies:
        copy.wait()
    for k in range(count):
        for j in range(js):
            row = j * count + k
            off_col[row, :] = jnp.full((LANES,), offs[k, j], jnp.int32)
            sid_col[row, :] = jnp.full((LANES,), sids[k, j], jnp.int32)
    nstation = gap_start.shape[1]
    own = lax.broadcasted_iota(jnp.int32, (refs, nstation), 1) == sid_col[:, :nstation]
    starts = gap_start[...].astype(jnp.float32)
    ends = starts + gap_len[...].astype(jnp.float32)
    live = jnp.ones(mask.shape, jnp.float32)
    times = lax.broadcasted_iota(jnp.int32, mask.shape, 1).astype(jnp.float32)
    for g in range(starts.shape[0]):
        first = jnp.sum(jnp.where(own, starts[g : g + 1], 0.0), axis=1, keepdims=True)
        last = jnp.sum(jnp.where(own, ends[g : g + 1], 0.0), axis=1, keepdims=True)
        live = jnp.where((times >= first) & (times < last), 0.0, live)
    mask[...] = live
    for c in range(comps):
        for j in range(js):
            wave = waves[j, c].astype(jnp.float32)
            power = jnp.sum(wave * wave, axis=1, keepdims=True) / taps
            factor = 1.0 / (taps * jnp.sqrt(power + 1e-06))
            first = (c * js + j) * count
            scale[first : first + count, :] = jnp.broadcast_to(factor, (count, LANES))


def filters_kernel(begin, waves, filters):
    js, _, count, taps = waves.shape
    groups, depth, _ = filters.shape

    def one_group(i, carry):
        g = begin + i
        wave = waves[lax.rem(g, js), g // js].astype(jnp.float32)
        wave = jnp.concatenate([wave, jnp.zeros((count, depth - taps), jnp.float32)], axis=1)
        rows = []
        for k in range(count):
            row = jnp.broadcast_to(wave[k : k + 1], (SPAN, depth))
            rows.append(pltpu.roll(row, 0, 1, stride=1, stride_axis=0))
        filters[i] = jnp.concatenate(rows, axis=0).T.astype(jnp.bfloat16)
        return carry

    lax.fori_loop(0, groups, one_group, 0, unroll=5)


def select_kernel(comps, high, nsub, *args):
    heads, args = args[:nsub], args[nsub:]
    nslab = len(args) // 2
    sid_cols, mask, outs = args[:nslab], args[nslab], args[nslab + 1 :]
    refs = mask.shape[0]
    ntmpl = heads[0].shape[0]
    width = outs[0].shape[1]
    per = width // LANES
    here = lax.axis_index("slab")
    rows_slab = comps * high
    blocks = [(part, z) for part in heads for z in range(ntmpl)]
    depth = len(blocks) * rows_slab
    owner = []
    for q in range(0, depth, LANES):
        lane = lax.broadcasted_iota(jnp.int32, (1, LANES), 1) + q
        line = jnp.full((1, LANES), -1.0, jnp.float32)
        for b, (part, z) in enumerate(blocks):
            if b * rows_slab < q + LANES and (b + 1) * rows_slab > q:
                tail = part[z, rows_slab * per : rows_slab * per + EXTRA, :].astype(jnp.float32)
                inside = (lane >= b * rows_slab) & (lane < (b + 1) * rows_slab)
                line = jnp.where(inside, tail[:1], line)
        owner.append(line)
    owner = jnp.concatenate(owner, axis=1)[:, :depth]
    row = lax.broadcasted_iota(jnp.int32, (1, depth), 1)
    row = lax.rem(row, rows_slab) // high
    columns = []
    for q in range(per):
        tiles = []
        for part, z in blocks:
            for c in range(comps):
                first = (c * per + q) * high
                tiles.append(part[z, first : first + high, :])
        columns.append(jnp.concatenate(tiles, axis=0))
    stack = jnp.concatenate(columns, axis=1)
    owners = [jnp.where(row == c, owner, -1.0) for c in range(comps)]
    for d, out in enumerate(outs):
        wanted = sid_cols[d][:, :1].astype(jnp.float32)
        pick = [jnp.where(owners[c] == wanted, 1.0, 0.0).astype(jnp.bfloat16) for c in range(comps)]
        got = jnp.dot(jnp.concatenate(pick, axis=0), stack, preferred_element_type=jnp.float32)
        if d:
            out[...] = got.astype(out.dtype)
        else:
            live = mask[:, pl.ds(pl.multiple_of(here * width, LANES), width)]
            for c in range(comps):
                out[c * refs : (c + 1) * refs, :] = got[c * refs : (c + 1) * refs] * live


def correlate_kernel(nslab, nsub, taps, nbank, *args):
    near, fars, args = args[0], args[1:nslab], args[nslab:]
    banks, args = args[:nbank], args[nbank:]
    off_col, mask, band, scale, keep, send, segs, low, high, norm, total = args
    refs, time = mask.shape
    chans, width = near.shape
    comps = chans // refs
    chunks = time // LANES
    count = keep.shape[1]
    tall = low.shape[1]
    here, core = lax.axis_index("slab"), lax.axis_index("sub")
    for d in range(nslab):
        spot = pl.ds(pl.multiple_of(lax.bitwise_xor(here, d) * width, LANES), width)
        if d == 0:
            segs[:, spot] = near[...]
        else:
            live = mask[:, spot]
            for c in range(comps):
                got = fars[d - 1][c * refs : (c + 1) * refs, :].astype(jnp.float32)
                segs[c * refs : (c + 1) * refs, spot] = got * live
    lane = lax.broadcasted_iota(jnp.int32, (8, LANES), 1)
    zero = jnp.zeros((8, LANES), jnp.float32)
    for i in range(chans // 8):
        ref_row = (i * 8) % refs
        off = off_col[ref_row : ref_row + 8, :]
        place = lax.bitwise_and(lane + off, LANES - 1)
        fine = lax.bitwise_and(off, LANES - 1)
        close = lane + fine < LANES
        far = off >= LANES
        turned = [
            jnp.take_along_axis(segs[i * 8 : i * 8 + 8, r * LANES : (r + 1) * LANES], place, axis=1)
            for r in range(chunks)
        ]
        turned += [zero, zero]
        moved = [jnp.where(close, turned[r], turned[r + 1]) for r in range(chunks + 1)]
        mine = [jnp.where(far, moved[r + 1], moved[r]) for r in range(chunks)] + [zero]
        for r in range(chunks):
            segs[i * 8 : i * 8 + 8, r * LANES : (r + 1) * LANES] = mine[r]
            low[pl.ds(i * 8, 8), r, :] = mine[r]
            half = jnp.where(lane < LANES - SPAN, pltpu.roll(mine[r], SPAN, 1), pltpu.roll(mine[r + 1], SPAN, 1))
            high[pl.ds(i * 8, 8), r, :] = half
        for r in range(chunks, tall):
            low[pl.ds(i * 8, 8), r, :] = zero
            high[pl.ds(i * 8, 8), r, :] = zero
    reach = band.shape[1] // LANES
    sums = {}
    for r in reversed(range(chunks)):
        part = segs[:, r * LANES : (r + 1) * LANES]
        power = part * part
        lead = power.astype(jnp.bfloat16)
        rest = (power - lead.astype(jnp.float32)).astype(jnp.bfloat16)
        sums[r] = jnp.dot(jnp.concatenate([lead, rest], axis=1), band[...], preferred_element_type=jnp.float32)
        window = sums[r][:, :LANES]
        for p in range(1, min(reach, chunks - r)):
            window = window + sums[r + p][:, p * LANES : (p + 1) * LANES]
        factor = scale[...] * lax.rsqrt(window / taps + 1e-06)
        for i in range(chans // 8):
            norm[pl.ds(i * 8, 8), r, :] = factor[i * 8 : i * 8 + 8]
    span = banks[0].shape[1] // LANES
    accs = [jnp.zeros((chunks, LANES), jnp.float32) for _ in range(count)]
    side = lax.broadcasted_iota(jnp.int32, (chunks, LANES), 1) < SPAN
    weights = [(bank, i) for bank in banks for i in range(bank.shape[0])]
    for g, (bank, i) in enumerate(weights):
        base = g * count
        rows = []
        for ch in range(base, base + count):
            for source in (low, high):
                rows.append(jnp.concatenate([source[ch, p : p + chunks, :] for p in range(span)], axis=1))
        both = jnp.concatenate(rows, axis=0).astype(jnp.bfloat16)
        res = jnp.dot(both, bank[i], preferred_element_type=jnp.float32)
        for k in range(count):
            left = (k // 2) * LANES
            tile = res[2 * k * chunks : 2 * (k + 1) * chunks, left : left + LANES]
            early, late = tile[:chunks], tile[chunks:]
            if k % 2 == 0:
                wide = jnp.where(side, early, pltpu.roll(late, SPAN, 1))
            else:
                wide = jnp.where(side, pltpu.roll(early, SPAN, 1), late)
            accs[k] = accs[k] + wide * norm[base + k]
    for k in range(count):
        total[k] = accs[k]
    each = chunks // (nslab * nsub)
    for d in range(nslab):
        for e in range(each):
            first = lax.bitwise_xor(here, d) * nsub * each + e
            turn = nsub - 1 if d else 0
            mine = first + lax.bitwise_xor(core, turn) * each
            keep[d, :, e * LANES : (e + 1) * LANES] = total[:, mine, :]
            for m in range(1, nsub):
                other = first + lax.bitwise_xor(core, m ^ turn) * each
                send[m - 1, d, :, e * LANES : (e + 1) * LANES] = total[:, other, :]


def swapped(value, axis, distance):
    return lax.ppermute(value, axis, [(i, i ^ distance) for i in range(lax.axis_size(axis))])


def stays(value):
    return pltpu.with_memory_space_constraint(value, pltpu.HBM)


def params(mib):
    return pltpu.CompilerParams(vmem_limit_bytes=mib << 20)


def on_device(records, owner_slots, gap_start, gap_len, templates, station_ids, offsets):
    nloc, comps, width = records.shape
    count, js, _, taps = templates.shape
    nslab, nsub, ntmpl = (lax.axis_size(name) for name in ("slab", "sub", "tmpl"))
    time = width * nslab
    refs = count * js
    chans = comps * refs
    here, core = lax.axis_index("slab"), lax.axis_index("sub")
    vmem, smem = pl.BlockSpec(memory_space=pltpu.VMEM), pl.BlockSpec(memory_space=pltpu.SMEM)
    hbm = pl.BlockSpec(memory_space=pltpu.HBM)
    half = nloc // nsub
    high = round_up(half, 16)
    per = width // LANES
    if high == half:
        block = pl.pallas_call(
            pack_kernel,
            out_shape=jax.ShapeDtypeStruct((comps * high * per + EXTRA, LANES), records.dtype),
            in_specs=[hbm, hbm],
            out_specs=vmem,
            scratch_shapes=[pltpu.SMEM((nloc,), jnp.int32), pltpu.SemaphoreType.DMA((comps * per + 1,))],
            compiler_params=params(4),
            name="pack",
        )(stays(owner_slots), stays(records.transpose(1, 0, 2)))
    else:
        mine = lax.dynamic_slice_in_dim(records.transpose(1, 0, 2), half * core, half, 1)
        mine = jnp.pad(mine, ((0, 0), (0, high - half), (0, 0))).reshape(comps, high, per, LANES)
        mine = mine.transpose(0, 2, 1, 3).reshape(comps * per * high, LANES)
        own = lax.dynamic_slice_in_dim(owner_slots, half * core, half, 0)
        index = jnp.arange(EXTRA * LANES, dtype=jnp.int32).reshape(1, EXTRA, LANES) % high
        slots = jnp.arange(half, dtype=jnp.int32)[:, None, None]
        own = jnp.sum(jnp.where(index == slots, own[:, None, None] + 1, 0), axis=0) - 1
        block = jnp.concatenate([mine, own.astype(records.dtype)], axis=0)
    column = [block]
    if ntmpl <= 8:
        for d in range(1, ntmpl):
            column.append(lax.ppermute(block, "tmpl", [(i, (i + d) % ntmpl) for i in range(ntmpl)]))
    else:
        column = list(lax.all_gather(block, "tmpl", axis=0))
    waves = templates.transpose(1, 2, 0, 3)
    reach = round_up(taps + LANES - 1, LANES)
    sid_col, off_col, mask, band, scale, waves = pl.pallas_call(
        tables_kernel,
        out_shape=[
            jax.ShapeDtypeStruct((refs, LANES), jnp.int32),
            jax.ShapeDtypeStruct((refs, LANES), jnp.int32),
            jax.ShapeDtypeStruct((refs, time), jnp.float32),
            jax.ShapeDtypeStruct((2 * LANES, reach), jnp.bfloat16),
            jax.ShapeDtypeStruct((chans, LANES), jnp.float32),
            jax.ShapeDtypeStruct(waves.shape, waves.dtype),
        ],
        in_specs=[hbm] * 5,
        out_specs=[vmem] * 6,
        scratch_shapes=[
            pltpu.SMEM(station_ids.shape, jnp.int32),
            pltpu.SMEM(offsets.shape, jnp.int32),
            pltpu.VMEM(gap_start.T.shape, jnp.int32),
            pltpu.VMEM(gap_len.T.shape, jnp.int32),
            pltpu.SemaphoreType.DMA((5,)),
        ],
        compiler_params=params(8),
        name="tables",
    )(*[stays(value) for value in (station_ids, offsets, gap_start.T, gap_len.T, waves)])
    sid_cols = [sid_col] + [swapped(sid_col, "slab", d) for d in range(1, nslab)]
    depth = round_up(taps + SPAN - 1, LANES)

    def bank(begin, groups):
        return pl.pallas_call(
            functools.partial(filters_kernel, begin),
            out_shape=jax.ShapeDtypeStruct((groups, depth, count * SPAN), jnp.bfloat16),
            in_specs=[vmem],
            out_specs=vmem,
            compiler_params=params(16),
            name="filters",
        )(waves)

    groups = comps * js
    early = groups // 3
    bank_a = bank(0, early)
    column, mask = lax.optimization_barrier((column, mask))
    head = jnp.stack(column)
    heads = [head] + [swapped(head, "sub", m) for m in range(1, nsub)]
    heads, bank_a = lax.optimization_barrier((heads, bank_a))
    near, *fars = pl.pallas_call(
        functools.partial(select_kernel, comps, high, nsub),
        out_shape=[jax.ShapeDtypeStruct((chans, width), jnp.float32)]
        + [jax.ShapeDtypeStruct((chans, width), records.dtype)] * (nslab - 1),
        in_specs=[vmem] * (nsub + nslab + 1),
        out_specs=[vmem] * nslab,
        compiler_params=params(16),
        name="select",
    )(*heads, *sid_cols, mask)
    fars = [swapped(far, "slab", d + 1) for d, far in enumerate(fars)]
    bank_b = bank(early, groups - early)
    fars, bank_b = lax.optimization_barrier((fars, bank_b))
    chunks = time // LANES
    each = width // nsub
    tall = chunks + 8
    keep, send = pl.pallas_call(
        functools.partial(correlate_kernel, nslab, nsub, taps, 2),
        out_shape=[
            jax.ShapeDtypeStruct((nslab, count, each), jnp.float32),
            jax.ShapeDtypeStruct((nsub - 1, nslab, count, each), jnp.float32),
        ],
        in_specs=[vmem] * (nslab + 6),
        out_specs=[vmem] * 2,
        scratch_shapes=[
            pltpu.VMEM((chans, time), jnp.float32),
            pltpu.VMEM((chans, tall, LANES), jnp.float32),
            pltpu.VMEM((chans, tall, LANES), jnp.float32),
            pltpu.VMEM((chans, chunks, LANES), jnp.float32),
            pltpu.VMEM((count, chunks, LANES), jnp.float32),
        ],
        compiler_params=params(32),
        name="correlate",
    )(near, *fars, bank_a, bank_b, off_col, mask, band, scale)
    for m in range(1, nsub):
        keep = keep + swapped(send[m - 1], "sub", m)
    lines = [keep[0]]
    for d in range(1, nslab):
        lines.append(swapped(keep[d], ("slab", "sub"), d * nsub + nsub - 1))
    result = []
    for s in range(nslab):
        line = lines[0]
        for d in range(1, nslab):
            line = jnp.where((here ^ d) == s, lines[d], line)
        result.append(line)
    return jnp.concatenate(result, axis=0)


def solution(mesh):
    in_specs = (
        P(("grp", "tmpl"), None, "slab"),
        P(("grp", "tmpl")),
        P("grp", None),
        P("grp", None),
        P(("grp", "tmpl", "slab"), "sub", None, None),
        P(("grp", "tmpl", "slab"), "sub"),
        P(("grp", "tmpl", "slab"), "sub"),
    )
    out_specs = P(("grp", "tmpl"), ("slab", "sub"))
    return jax.shard_map(
        on_device, mesh=mesh, in_specs=in_specs, out_specs=out_specs, check_vma=False
    )
```

```python
import functools

import jax
import jax.numpy as jnp
from jax import lax
from jax.experimental import pallas as pl
from jax.experimental.pallas import tpu as pltpu
from jax.sharding import PartitionSpec as P

LANES = 128
SPAN = 64
EXTRA = 8
UNROLL = 6


def round_up(value, step):
    return -(-value // step) * step


def pack_kernel(owner_slots, records, block, owners, sems):
    comps, _, width = records.shape
    per = width // LANES
    half = (block.shape[0] - EXTRA) // (comps * per)
    first = pl.multiple_of(lax.axis_index("sub") * half, half)
    copies = [pltpu.make_async_copy(owner_slots, owners, sems.at[comps * per])]
    for i in range(comps * per):
        source = records.at[i // per, pl.ds(first, half), (i % per) * LANES : (i % per + 1) * LANES]
        copies.append(pltpu.make_async_copy(source, block.at[i * half : (i + 1) * half, :], sems.at[i]))
    for copy in copies:
        copy.start()
    copies[0].wait()
    lane = lax.rem(lax.broadcasted_iota(jnp.int32, (EXTRA, LANES), 1), half)
    line = jnp.full((EXTRA, LANES), -1, jnp.int32)
    for i in range(half):
        line = jnp.where(lane == i, owners[first + i], line)
    block[comps * per * half :, :] = line.astype(jnp.float32).astype(block.dtype)
    for copy in copies[1:]:
        copy.wait()


def build_filters(begin, waves, filters):
    js, _, count, taps = waves.shape
    groups, depth, _ = filters.shape

    def one_group(i):
        g = begin + i
        wave = waves[lax.rem(g, js), g // js].astype(jnp.float32)
        wave = jnp.concatenate([wave, jnp.zeros((count, depth - taps), jnp.float32)], axis=1)
        rows = []
        for k in range(count):
            row = jnp.broadcast_to(wave[k : k + 1], (SPAN, depth))
            rows.append(pltpu.roll(row, 0, 1, stride=1, stride_axis=0))
        filters[i] = jnp.concatenate(rows, axis=0).T.astype(jnp.bfloat16)

    def some_groups(t, carry):
        for u in range(UNROLL):
            one_group(t * UNROLL + u)
        return carry

    lax.fori_loop(0, groups // UNROLL, some_groups, 0)
    for i in range(groups // UNROLL * UNROLL, groups):
        one_group(i)


def tables_kernel(sids_in, offs_in, start_in, len_in, waves_in, sid_col, off_col, mask, band, scale, waves, filters, *scratch):
    sids, offs, gap_start, gap_len, sems = scratch
    pairs = ((waves_in, waves), (sids_in, sids), (offs_in, offs), (start_in, gap_start), (len_in, gap_len))
    copies = [pltpu.make_async_copy(source, place, sems.at[i]) for i, (source, place) in enumerate(pairs)]
    for copy in copies:
        copy.start()
    js, comps, count, taps = waves.shape
    refs = count * js
    rows = lax.rem(lax.broadcasted_iota(jnp.int32, band.shape, 0), LANES)
    cols = lax.broadcasted_iota(jnp.int32, band.shape, 1)
    lead = rows + (cols // LANES) * LANES - lax.rem(cols, LANES)
    band[...] = jnp.where((lead >= 0) & (lead < taps), 1.0, 0.0).astype(jnp.bfloat16)
    for copy in copies:
        copy.wait()
    for k in range(count):
        for j in range(js):
            row = j * count + k
            off_col[row, :] = jnp.full((LANES,), offs[k, j], jnp.int32)
            sid_col[row, :] = jnp.full((LANES,), sids[k, j], jnp.int32)
    nstation = gap_start.shape[1]
    own = lax.broadcasted_iota(jnp.int32, (refs, nstation), 1) == sid_col[:, :nstation]
    starts = gap_start[...].astype(jnp.float32)
    ends = starts + gap_len[...].astype(jnp.float32)
    live = jnp.ones(mask.shape, jnp.float32)
    times = lax.broadcasted_iota(jnp.int32, mask.shape, 1).astype(jnp.float32)
    for g in range(starts.shape[0]):
        first = jnp.sum(jnp.where(own, starts[g : g + 1], 0.0), axis=1, keepdims=True)
        last = jnp.sum(jnp.where(own, ends[g : g + 1], 0.0), axis=1, keepdims=True)
        live = jnp.where((times >= first) & (times < last), 0.0, live)
    mask[...] = live
    for c in range(comps):
        for j in range(js):
            wave = waves[j, c].astype(jnp.float32)
            power = jnp.sum(wave * wave, axis=1, keepdims=True) / taps
            factor = 1.0 / (taps * jnp.sqrt(power + 1e-06))
            first = (c * js + j) * count
            scale[first : first + count, :] = jnp.broadcast_to(factor, (count, LANES))
    build_filters(0, waves, filters)


def middle_kernel(begin, nfar, *args):
    asked, waves, columns, filters = args[:nfar], args[nfar], args[nfar + 1 : -1], args[-1]
    count, js = asked[0].shape
    for source, column in zip(asked, columns):
        for k in range(count):
            for j in range(js):
                column[j * count + k, :] = jnp.full((LANES,), source[k, j], jnp.int32)
    build_filters(begin, waves, filters)


def filters_kernel(begin, waves, filters):
    build_filters(begin, waves, filters)


def select_kernel(comps, high, nsub, *args):
    heads, args = args[:nsub], args[nsub:]
    nslab = len(args) // 2
    sid_cols, mask, outs = args[:nslab], args[nslab], args[nslab + 1 :]
    refs = mask.shape[0]
    ntmpl = heads[0].shape[0]
    width = outs[0].shape[1]
    per = width // LANES
    here = lax.axis_index("slab")
    rows_slab = comps * high
    blocks = [(part, z) for part in heads for z in range(ntmpl)]
    depth = len(blocks) * rows_slab
    owner = []
    for q in range(0, depth, LANES):
        lane = lax.broadcasted_iota(jnp.int32, (1, LANES), 1) + q
        line = jnp.full((1, LANES), -1.0, jnp.float32)
        for b, (part, z) in enumerate(blocks):
            if b * rows_slab < q + LANES and (b + 1) * rows_slab > q:
                tail = part[z, rows_slab * per : rows_slab * per + EXTRA, :].astype(jnp.float32)
                inside = (lane >= b * rows_slab) & (lane < (b + 1) * rows_slab)
                line = jnp.where(inside, tail[:1], line)
        owner.append(line)
    owner = jnp.concatenate(owner, axis=1)[:, :depth]
    row = lax.broadcasted_iota(jnp.int32, (1, depth), 1)
    row = lax.rem(row, rows_slab) // high
    columns = []
    for q in range(per):
        tiles = []
        for part, z in blocks:
            for c in range(comps):
                first = (c * per + q) * high
                tiles.append(part[z, first : first + high, :])
        columns.append(jnp.concatenate(tiles, axis=0))
    stack = jnp.concatenate(columns, axis=1)
    owners = [jnp.where(row == c, owner, -1.0) for c in range(comps)]
    for d, out in enumerate(outs):
        wanted = sid_cols[d][:, :1].astype(jnp.float32)
        pick = [jnp.where(owners[c] == wanted, 1.0, 0.0).astype(jnp.bfloat16) for c in range(comps)]
        got = jnp.dot(jnp.concatenate(pick, axis=0), stack, preferred_element_type=jnp.float32)
        if d:
            out[...] = got.astype(out.dtype)
        else:
            live = mask[:, pl.ds(pl.multiple_of(here * width, LANES), width)]
            for c in range(comps):
                out[c * refs : (c + 1) * refs, :] = got[c * refs : (c + 1) * refs] * live


def correlate_kernel(nslab, nsub, taps, nbank, *args):
    near, fars, args = args[0], args[1:nslab], args[nslab:]
    banks, args = args[:nbank], args[nbank:]
    off_col, mask, band, scale, keep, send, segs, low, high, norm, total = args
    refs, time = mask.shape
    chans, width = near.shape
    comps = chans // refs
    chunks = time // LANES
    count = keep.shape[1]
    tall = low.shape[1]
    here, core = lax.axis_index("slab"), lax.axis_index("sub")
    for d in range(nslab):
        spot = pl.ds(pl.multiple_of(lax.bitwise_xor(here, d) * width, LANES), width)
        if d == 0:
            segs[:, spot] = near[...]
        else:
            live = mask[:, spot]
            for c in range(comps):
                got = fars[d - 1][c * refs : (c + 1) * refs, :].astype(jnp.float32)
                segs[c * refs : (c + 1) * refs, spot] = got * live
    lane = lax.broadcasted_iota(jnp.int32, (8, LANES), 1)
    zero = jnp.zeros((8, LANES), jnp.float32)
    for i in range(chans // 8):
        ref_row = (i * 8) % refs
        off = off_col[ref_row : ref_row + 8, :]
        place = lax.bitwise_and(lane + off, LANES - 1)
        fine = lax.bitwise_and(off, LANES - 1)
        close = lane + fine < LANES
        far = off >= LANES
        turned = [
            jnp.take_along_axis(segs[i * 8 : i * 8 + 8, r * LANES : (r + 1) * LANES], place, axis=1)
            for r in range(chunks)
        ]
        turned += [zero, zero]
        moved = [jnp.where(close, turned[r], turned[r + 1]) for r in range(chunks + 1)]
        mine = [jnp.where(far, moved[r + 1], moved[r]) for r in range(chunks)] + [zero]
        for r in range(chunks):
            segs[i * 8 : i * 8 + 8, r * LANES : (r + 1) * LANES] = mine[r]
            low[pl.ds(i * 8, 8), r, :] = mine[r]
            half = jnp.where(lane < LANES - SPAN, pltpu.roll(mine[r], SPAN, 1), pltpu.roll(mine[r + 1], SPAN, 1))
            high[pl.ds(i * 8, 8), r, :] = half
        for r in range(chunks, tall):
            low[pl.ds(i * 8, 8), r, :] = zero
            high[pl.ds(i * 8, 8), r, :] = zero
    reach = band.shape[1] // LANES
    sums = {}
    for r in reversed(range(chunks)):
        part = segs[:, r * LANES : (r + 1) * LANES]
        power = part * part
        lead = power.astype(jnp.bfloat16)
        rest = (power - lead.astype(jnp.float32)).astype(jnp.bfloat16)
        sums[r] = jnp.dot(jnp.concatenate([lead, rest], axis=1), band[...], preferred_element_type=jnp.float32)
        window = sums[r][:, :LANES]
        for p in range(1, min(reach, chunks - r)):
            window = window + sums[r + p][:, p * LANES : (p + 1) * LANES]
        factor = scale[...] * lax.rsqrt(window / taps + 1e-06)
        for i in range(chans // 8):
            norm[pl.ds(i * 8, 8), r, :] = factor[i * 8 : i * 8 + 8]
    span = banks[0].shape[1] // LANES
    accs = [jnp.zeros((chunks, LANES), jnp.float32) for _ in range(count)]
    side = lax.broadcasted_iota(jnp.int32, (chunks, LANES), 1) < SPAN
    weights = [(bank, i) for bank in banks for i in range(bank.shape[0])]
    for g, (bank, i) in enumerate(weights):
        base = g * count
        rows = []
        for ch in range(base, base + count):
            for source in (low, high):
                rows.append(jnp.concatenate([source[ch, p : p + chunks, :] for p in range(span)], axis=1))
        both = jnp.concatenate(rows, axis=0).astype(jnp.bfloat16)
        res = jnp.dot(both, bank[i], preferred_element_type=jnp.float32)
        for k in range(count):
            left = (k // 2) * LANES
            tile = res[2 * k * chunks : 2 * (k + 1) * chunks, left : left + LANES]
            early, late = tile[:chunks], tile[chunks:]
            if k % 2 == 0:
                wide = jnp.where(side, early, pltpu.roll(late, SPAN, 1))
            else:
                wide = jnp.where(side, pltpu.roll(early, SPAN, 1), late)
            accs[k] = accs[k] + wide * norm[base + k]
    for k in range(count):
        total[k] = accs[k]
    each = chunks // (nslab * nsub)
    for d in range(nslab):
        for e in range(each):
            first = lax.bitwise_xor(here, d) * nsub * each + e
            turn = nsub - 1 if d else 0
            mine = first + lax.bitwise_xor(core, turn) * each
            keep[d, :, e * LANES : (e + 1) * LANES] = total[:, mine, :]
            for m in range(1, nsub):
                other = first + lax.bitwise_xor(core, m ^ turn) * each
                send[m - 1, d, :, e * LANES : (e + 1) * LANES] = total[:, other, :]


def swapped(value, axis, distance):
    return lax.ppermute(value, axis, [(i, i ^ distance) for i in range(lax.axis_size(axis))])


def crossed(value, distance):
    nsub = lax.axis_size("sub")
    count = lax.axis_size("slab") * nsub
    return lax.ppermute(value, ("slab", "sub"), [(i, i ^ (distance * nsub + nsub - 1)) for i in range(count)])


def stays(value):
    return pltpu.with_memory_space_constraint(value, pltpu.HBM)


def params(mib):
    return pltpu.CompilerParams(vmem_limit_bytes=mib << 20)


def on_device(records, owner_slots, gap_start, gap_len, templates, station_ids, offsets):
    nloc, comps, width = records.shape
    count, js, _, taps = templates.shape
    nslab, nsub, ntmpl = (lax.axis_size(name) for name in ("slab", "sub", "tmpl"))
    time = width * nslab
    refs = count * js
    chans = comps * refs
    here, core = lax.axis_index("slab"), lax.axis_index("sub")
    vmem, smem = pl.BlockSpec(memory_space=pltpu.VMEM), pl.BlockSpec(memory_space=pltpu.SMEM)
    hbm = pl.BlockSpec(memory_space=pltpu.HBM)
    half = nloc // nsub
    high = round_up(half, 16)
    per = width // LANES
    if high == half:
        block = pl.pallas_call(
            pack_kernel,
            out_shape=jax.ShapeDtypeStruct((comps * high * per + EXTRA, LANES), records.dtype),
            in_specs=[hbm, hbm],
            out_specs=vmem,
            scratch_shapes=[pltpu.SMEM((nloc,), jnp.int32), pltpu.SemaphoreType.DMA((comps * per + 1,))],
            compiler_params=params(4),
            name="pack",
        )(stays(owner_slots), stays(records.transpose(1, 0, 2)))
    else:
        mine = lax.dynamic_slice_in_dim(records.transpose(1, 0, 2), half * core, half, 1)
        mine = jnp.pad(mine, ((0, 0), (0, high - half), (0, 0))).reshape(comps, high, per, LANES)
        mine = mine.transpose(0, 2, 1, 3).reshape(comps * per * high, LANES)
        own = lax.dynamic_slice_in_dim(owner_slots, half * core, half, 0)
        index = jnp.arange(EXTRA * LANES, dtype=jnp.int32).reshape(1, EXTRA, LANES) % high
        slots = jnp.arange(half, dtype=jnp.int32)[:, None, None]
        own = jnp.sum(jnp.where(index == slots, own[:, None, None] + 1, 0), axis=0) - 1
        block = jnp.concatenate([mine, own.astype(records.dtype)], axis=0)
    column = [block]
    if ntmpl <= 8:
        for d in range(1, ntmpl):
            column.append(lax.ppermute(block, "tmpl", [(i, (i + d) % ntmpl) for i in range(ntmpl)]))
    else:
        column = list(lax.all_gather(block, "tmpl", axis=0))
    asked = [crossed(station_ids, d) for d in range(1, nslab)]
    waves = templates.transpose(1, 2, 0, 3)
    reach = round_up(taps + LANES - 1, LANES)
    depth = round_up(taps + SPAN - 1, LANES)
    groups = comps * js
    first, second = groups // 5, groups // 5

    def bank(size):
        return jax.ShapeDtypeStruct((size, depth, count * SPAN), jnp.bfloat16)

    column_type = jax.ShapeDtypeStruct((refs, LANES), jnp.int32)
    sid_col, off_col, mask, band, scale, waves, bank_a = pl.pallas_call(
        tables_kernel,
        out_shape=[
            column_type,
            column_type,
            jax.ShapeDtypeStruct((refs, time), jnp.float32),
            jax.ShapeDtypeStruct((2 * LANES, reach), jnp.bfloat16),
            jax.ShapeDtypeStruct((chans, LANES), jnp.float32),
            jax.ShapeDtypeStruct(waves.shape, waves.dtype),
            bank(first),
        ],
        in_specs=[hbm] * 5,
        out_specs=[vmem] * 7,
        scratch_shapes=[
            pltpu.SMEM(station_ids.shape, jnp.int32),
            pltpu.SMEM(offsets.shape, jnp.int32),
            pltpu.VMEM(gap_start.T.shape, jnp.int32),
            pltpu.VMEM(gap_len.T.shape, jnp.int32),
            pltpu.SemaphoreType.DMA((5,)),
        ],
        compiler_params=params(12),
        name="tables",
    )(*[stays(value) for value in (station_ids, offsets, gap_start.T, gap_len.T, waves)])
    column, asked, mask = lax.optimization_barrier((column, asked, mask))
    head = jnp.stack(column)
    heads = [head] + [swapped(head, "sub", m) for m in range(1, nsub)]
    *sid_far, bank_b = pl.pallas_call(
        functools.partial(middle_kernel, first, nslab - 1),
        out_shape=[column_type] * (nslab - 1) + [bank(second)],
        in_specs=[smem] * (nslab - 1) + [vmem],
        out_specs=[vmem] * nslab,
        compiler_params=params(12),
        name="middle",
    )(*asked, waves)
    heads, sid_far, bank_b = lax.optimization_barrier((heads, sid_far, bank_b))
    sid_cols = [sid_col] + list(sid_far)
    near, *fars = pl.pallas_call(
        functools.partial(select_kernel, comps, high, nsub),
        out_shape=[jax.ShapeDtypeStruct((chans, width), jnp.float32)]
        + [jax.ShapeDtypeStruct((chans, width), records.dtype)] * (nslab - 1),
        in_specs=[vmem] * (nsub + nslab + 1),
        out_specs=[vmem] * nslab,
        compiler_params=params(16),
        name="select",
    )(*heads, *sid_cols, mask)
    fars = [crossed(far, d + 1) for d, far in enumerate(fars)]
    bank_c = pl.pallas_call(
        functools.partial(filters_kernel, first + second),
        out_shape=bank(groups - first - second),
        in_specs=[vmem],
        out_specs=vmem,
        compiler_params=params(16),
        name="filters",
    )(waves)
    fars, bank_c = lax.optimization_barrier((fars, bank_c))
    chunks = time // LANES
    each = width // nsub
    tall = chunks + 8
    keep, send = pl.pallas_call(
        functools.partial(correlate_kernel, nslab, nsub, taps, 3),
        out_shape=[
            jax.ShapeDtypeStruct((nslab, count, each), jnp.float32),
            jax.ShapeDtypeStruct((nsub - 1, nslab, count, each), jnp.float32),
        ],
        in_specs=[vmem] * (nslab + 7),
        out_specs=[vmem] * 2,
        scratch_shapes=[
            pltpu.VMEM((chans, time), jnp.float32),
            pltpu.VMEM((chans, tall, LANES), jnp.float32),
            pltpu.VMEM((chans, tall, LANES), jnp.float32),
            pltpu.VMEM((chans, chunks, LANES), jnp.float32),
            pltpu.VMEM((count, chunks, LANES), jnp.float32),
        ],
        compiler_params=params(32),
        name="correlate",
    )(near, *fars, bank_a, bank_b, bank_c, off_col, mask, band, scale)
    for m in range(1, nsub):
        keep = keep + swapped(send[m - 1], "sub", m)
    lines = [keep[0]]
    for d in range(1, nslab):
        lines.append(crossed(keep[d], d))
    result = []
    for s in range(nslab):
        line = lines[0]
        for d in range(1, nslab):
            line = jnp.where((here ^ d) == s, lines[d], line)
        result.append(line)
    return jnp.concatenate(result, axis=0)


def solution(mesh):
    in_specs = (
        P(("grp", "tmpl"), None, "slab"),
        P(("grp", "tmpl")),
        P("grp", None),
        P("grp", None),
        P(("grp", "tmpl", "slab"), "sub", None, None),
        P(("grp", "tmpl", "slab"), "sub"),
        P(("grp", "tmpl", "slab"), "sub"),
    )
    out_specs = P(("grp", "tmpl"), ("slab", "sub"))
    return jax.shard_map(
        on_device, mesh=mesh, in_specs=in_specs, out_specs=out_specs, check_vma=False
    )
```

```python
import functools

import jax
import jax.numpy as jnp
from jax import lax
from jax.experimental import pallas as pl
from jax.experimental.pallas import tpu as pltpu
from jax.sharding import PartitionSpec as P

LANES = 128
SPAN = 64
EXTRA = 8
UNROLL = 6


def round_up(value, step):
    return -(-value // step) * step


def pack_kernel(owner_slots, records, block, owners, sems):
    comps, _, width = records.shape
    per = width // LANES
    half = (block.shape[0] - EXTRA) // (comps * per)
    first = pl.multiple_of(lax.axis_index("sub") * half, half)
    copies = [pltpu.make_async_copy(owner_slots, owners, sems.at[comps * per])]
    for i in range(comps * per):
        source = records.at[i // per, pl.ds(first, half), (i % per) * LANES : (i % per + 1) * LANES]
        copies.append(pltpu.make_async_copy(source, block.at[i * half : (i + 1) * half, :], sems.at[i]))
    for copy in copies:
        copy.start()
    copies[0].wait()
    lane = lax.rem(lax.broadcasted_iota(jnp.int32, (EXTRA, LANES), 1), half)
    line = jnp.full((EXTRA, LANES), -1, jnp.int32)
    for i in range(half):
        line = jnp.where(lane == i, owners[first + i], line)
    block[comps * per * half :, :] = line.astype(jnp.float32).astype(block.dtype)
    for copy in copies[1:]:
        copy.wait()


def build_filters(begin, waves, filters):
    js, _, count, taps = waves.shape
    groups, depth, _ = filters.shape

    def one_group(i):
        g = begin + i
        wave = waves[lax.rem(g, js), g // js].astype(jnp.float32)
        wave = jnp.concatenate([wave, jnp.zeros((count, depth - taps), jnp.float32)], axis=1)
        rows = []
        for k in range(count):
            row = jnp.broadcast_to(wave[k : k + 1], (SPAN, depth))
            rows.append(pltpu.roll(row, 0, 1, stride=1, stride_axis=0))
        filters[i] = jnp.concatenate(rows, axis=0).T.astype(jnp.bfloat16)

    def some_groups(t, carry):
        for u in range(UNROLL):
            one_group(t * UNROLL + u)
        return carry

    lax.fori_loop(0, groups // UNROLL, some_groups, 0)
    for i in range(groups // UNROLL * UNROLL, groups):
        one_group(i)


def tables_kernel(sids_in, offs_in, start_in, len_in, waves_in, sid_col, off_col, mask, band, scale, waves, filters, *scratch):
    sids, offs, gap_start, gap_len, sems = scratch
    pairs = ((waves_in, waves), (sids_in, sids), (offs_in, offs), (start_in, gap_start), (len_in, gap_len))
    copies = [pltpu.make_async_copy(source, place, sems.at[i]) for i, (source, place) in enumerate(pairs)]
    for copy in copies:
        copy.start()
    js, comps, count, taps = waves.shape
    refs = count * js
    rows = lax.rem(lax.broadcasted_iota(jnp.int32, band.shape, 0), LANES)
    cols = lax.broadcasted_iota(jnp.int32, band.shape, 1)
    lead = rows + (cols // LANES) * LANES - lax.rem(cols, LANES)
    band[...] = jnp.where((lead >= 0) & (lead < taps), 1.0, 0.0).astype(jnp.bfloat16)
    for copy in copies:
        copy.wait()
    for k in range(count):
        for j in range(js):
            row = j * count + k
            off_col[row, :] = jnp.full((LANES,), offs[k, j], jnp.int32)
            sid_col[row, :] = jnp.full((LANES,), sids[k, j], jnp.int32)
    nstation = gap_start.shape[1]
    own = lax.broadcasted_iota(jnp.int32, (refs, nstation), 1) == sid_col[:, :nstation]
    starts = gap_start[...].astype(jnp.float32)
    ends = starts + gap_len[...].astype(jnp.float32)
    live = jnp.ones(mask.shape, jnp.float32)
    times = lax.broadcasted_iota(jnp.int32, mask.shape, 1).astype(jnp.float32)
    for g in range(starts.shape[0]):
        first = jnp.sum(jnp.where(own, starts[g : g + 1], 0.0), axis=1, keepdims=True)
        last = jnp.sum(jnp.where(own, ends[g : g + 1], 0.0), axis=1, keepdims=True)
        live = jnp.where((times >= first) & (times < last), 0.0, live)
    mask[...] = live
    for c in range(comps):
        for j in range(js):
            wave = waves[j, c].astype(jnp.float32)
            power = jnp.sum(wave * wave, axis=1, keepdims=True) / taps
            factor = 1.0 / (taps * jnp.sqrt(power + 1e-06))
            first = (c * js + j) * count
            scale[first : first + count, :] = jnp.broadcast_to(factor, (count, LANES))
    build_filters(0, waves, filters)


def middle_kernel(begin, nfar, *args):
    asked, waves, columns, filters = args[:nfar], args[nfar], args[nfar + 1 : -1], args[-1]
    count, js = asked[0].shape
    for source, column in zip(asked, columns):
        for k in range(count):
            for j in range(js):
                column[j * count + k, :] = jnp.full((LANES,), source[k, j], jnp.int32)
    build_filters(begin, waves, filters)


def filters_kernel(begin, waves, filters):
    build_filters(begin, waves, filters)


def select_kernel(comps, high, nsub, *args):
    heads, args = args[:nsub], args[nsub:]
    nslab = len(args) // 2
    sid_cols, mask, outs = args[:nslab], args[nslab], args[nslab + 1 :]
    refs = mask.shape[0]
    ntmpl = heads[0].shape[0]
    width = outs[0].shape[1]
    per = width // LANES
    here = lax.axis_index("slab")
    rows_slab = comps * high
    blocks = [(part, z) for part in heads for z in range(ntmpl)]
    depth = len(blocks) * rows_slab
    owner = []
    for q in range(0, depth, LANES):
        lane = lax.broadcasted_iota(jnp.int32, (1, LANES), 1) + q
        line = jnp.full((1, LANES), -1.0, jnp.float32)
        for b, (part, z) in enumerate(blocks):
            if b * rows_slab < q + LANES and (b + 1) * rows_slab > q:
                tail = part[z, rows_slab * per : rows_slab * per + EXTRA, :].astype(jnp.float32)
                inside = (lane >= b * rows_slab) & (lane < (b + 1) * rows_slab)
                line = jnp.where(inside, tail[:1], line)
        owner.append(line)
    owner = jnp.concatenate(owner, axis=1)[:, :depth]
    row = lax.broadcasted_iota(jnp.int32, (1, depth), 1)
    row = lax.rem(row, rows_slab) // high
    columns = []
    for q in range(per):
        tiles = []
        for part, z in blocks:
            for c in range(comps):
                first = (c * per + q) * high
                tiles.append(part[z, first : first + high, :])
        columns.append(jnp.concatenate(tiles, axis=0))
    stack = jnp.concatenate(columns, axis=1)
    owners = [jnp.where(row == c, owner, -1.0) for c in range(comps)]
    for d, out in enumerate(outs):
        wanted = sid_cols[d][:, :1].astype(jnp.float32)
        pick = [jnp.where(owners[c] == wanted, 1.0, 0.0).astype(jnp.bfloat16) for c in range(comps)]
        got = jnp.dot(jnp.concatenate(pick, axis=0), stack, preferred_element_type=jnp.float32)
        if d:
            out[...] = got.astype(out.dtype)
        else:
            live = mask[:, pl.ds(pl.multiple_of(here * width, LANES), width)]
            for c in range(comps):
                out[c * refs : (c + 1) * refs, :] = got[c * refs : (c + 1) * refs] * live


def correlate_kernel(nslab, nsub, taps, nbank, *args):
    near, fars, args = args[0], args[1:nslab], args[nslab:]
    banks, args = args[:nbank], args[nbank:]
    off_col, mask, band, scale, keep, send, segs, low, high, norm, total = args
    refs, time = mask.shape
    chans, width = near.shape
    comps = chans // refs
    chunks = time // LANES
    count = keep.shape[1]
    here, core = lax.axis_index("slab"), lax.axis_index("sub")
    for d in range(nslab):
        spot = pl.ds(pl.multiple_of(lax.bitwise_xor(here, d) * width, LANES), width)
        if d == 0:
            segs[:, spot] = near[...]
        else:
            live = mask[:, spot]
            for c in range(comps):
                got = fars[d - 1][c * refs : (c + 1) * refs, :].astype(jnp.float32)
                segs[c * refs : (c + 1) * refs, spot] = got * live
    span = banks[0].shape[1] // LANES
    lane = lax.broadcasted_iota(jnp.int32, (8, LANES), 1)
    zero = jnp.zeros((8, LANES), jnp.float32)
    for i in range(chans // 8):
        ref_row = (i * 8) % refs
        off = off_col[ref_row : ref_row + 8, :]
        place = lax.bitwise_and(lane + off, LANES - 1)
        fine = lax.bitwise_and(off, LANES - 1)
        close = lane + fine < LANES
        far = off >= LANES
        turned = [
            jnp.take_along_axis(segs[i * 8 : i * 8 + 8, r * LANES : (r + 1) * LANES], place, axis=1)
            for r in range(chunks)
        ]
        turned += [zero, zero]
        moved = [jnp.where(close, turned[r], turned[r + 1]) for r in range(chunks + 1)]
        mine = [jnp.where(far, moved[r + 1], moved[r]) for r in range(chunks)]
        swung = [pltpu.roll(part, SPAN, 1) for part in mine] + [zero]
        for r in range(chunks):
            segs[i * 8 : i * 8 + 8, r * LANES : (r + 1) * LANES] = mine[r]
            low[pl.ds(i * 8, 8), r, :] = mine[r]
            high[pl.ds(i * 8, 8), r, :] = jnp.where(lane < LANES - SPAN, swung[r], swung[r + 1])
        for r in range(chunks, chunks + span - 1):
            low[pl.ds(i * 8, 8), r, :] = zero
            high[pl.ds(i * 8, 8), r, :] = zero
    reach = band.shape[1] // LANES
    sums = {}
    for first in range(0, chunks, 2):
        batch = range(first, first + 2)
        power = jnp.concatenate([segs[:, r * LANES : (r + 1) * LANES] for r in batch], axis=0)
        power = power * power
        lead = power.astype(jnp.bfloat16)
        rest = (power - lead.astype(jnp.float32)).astype(jnp.bfloat16)
        both = jnp.concatenate([lead, rest], axis=1)
        got = jnp.dot(both, band[...], preferred_element_type=jnp.float32)
        for r in batch:
            sums[r] = got[(r - first) * chans : (r - first + 1) * chans]
    for r in range(chunks):
        window = sums[r][:, :LANES]
        for p in range(1, min(reach, chunks - r)):
            window = window + sums[r + p][:, p * LANES : (p + 1) * LANES]
        factor = scale[...] * lax.rsqrt(window / taps + 1e-06)
        for i in range(chans // 8):
            norm[pl.ds(i * 8, 8), r, :] = factor[i * 8 : i * 8 + 8]
    accs = [jnp.zeros((chunks, LANES), jnp.float32) for _ in range(count)]
    side = lax.broadcasted_iota(jnp.int32, (chunks, LANES), 1) < SPAN
    weights = [(bank, i) for bank in banks for i in range(bank.shape[0])]
    def operand(g):
        rows = []
        for ch in range(g * count, (g + 1) * count):
            for source in (low, high):
                rows.append(jnp.concatenate([source[ch, p : p + chunks, :] for p in range(span)], axis=1))
        return jnp.concatenate(rows, axis=0).astype(jnp.bfloat16)

    def gather_sums(g, res):
        base = g * count
        for k in range(count):
            left = (k // 2) * LANES
            tile = res[2 * k * chunks : 2 * (k + 1) * chunks, left : left + LANES]
            early, late = tile[:chunks], tile[chunks:]
            if k % 2 == 0:
                first, turned = early, late
            else:
                turned = pltpu.roll(jnp.where(side, turned, early), SPAN, 1)
                even, odd = jnp.where(side, first, turned), jnp.where(side, turned, late)
                accs[k - 1] = accs[k - 1] + even * norm[base + k - 1]
                accs[k] = accs[k] + odd * norm[base + k]

    for g, (bank, i) in enumerate(weights):
        gather_sums(g, jnp.dot(operand(g), bank[i], preferred_element_type=jnp.float32))
    for k in range(count):
        total[k] = accs[k]
    each = chunks // (nslab * nsub)
    for d in range(nslab):
        for e in range(each):
            first = lax.bitwise_xor(here, d) * nsub * each + e
            turn = nsub - 1 if d else 0
            mine = first + lax.bitwise_xor(core, turn) * each
            keep[d, :, e * LANES : (e + 1) * LANES] = total[:, mine, :]
            for m in range(1, nsub):
                other = first + lax.bitwise_xor(core, m ^ turn) * each
                send[m - 1, d, :, e * LANES : (e + 1) * LANES] = total[:, other, :]


def swapped(value, axis, distance):
    return lax.ppermute(value, axis, [(i, i ^ distance) for i in range(lax.axis_size(axis))])


def crossed(value, distance):
    nsub = lax.axis_size("sub")
    count = lax.axis_size("slab") * nsub
    return lax.ppermute(value, ("slab", "sub"), [(i, i ^ (distance * nsub + nsub - 1)) for i in range(count)])


def stays(value):
    return pltpu.with_memory_space_constraint(value, pltpu.HBM)


def params(mib):
    return pltpu.CompilerParams(vmem_limit_bytes=mib << 20)


def on_device(records, owner_slots, gap_start, gap_len, templates, station_ids, offsets):
    nloc, comps, width = records.shape
    count, js, _, taps = templates.shape
    nslab, nsub, ntmpl = (lax.axis_size(name) for name in ("slab", "sub", "tmpl"))
    time = width * nslab
    refs = count * js
    chans = comps * refs
    here, core = lax.axis_index("slab"), lax.axis_index("sub")
    vmem, smem = pl.BlockSpec(memory_space=pltpu.VMEM), pl.BlockSpec(memory_space=pltpu.SMEM)
    hbm = pl.BlockSpec(memory_space=pltpu.HBM)
    half = nloc // nsub
    high = round_up(half, 16)
    per = width // LANES
    if high == half:
        block = pl.pallas_call(
            pack_kernel,
            out_shape=jax.ShapeDtypeStruct((comps * high * per + EXTRA, LANES), records.dtype),
            in_specs=[hbm, hbm],
            out_specs=vmem,
            scratch_shapes=[pltpu.SMEM((nloc,), jnp.int32), pltpu.SemaphoreType.DMA((comps * per + 1,))],
            compiler_params=params(4),
            name="pack",
        )(stays(owner_slots), stays(records.transpose(1, 0, 2)))
    else:
        mine = lax.dynamic_slice_in_dim(records.transpose(1, 0, 2), half * core, half, 1)
        mine = jnp.pad(mine, ((0, 0), (0, high - half), (0, 0))).reshape(comps, high, per, LANES)
        mine = mine.transpose(0, 2, 1, 3).reshape(comps * per * high, LANES)
        own = lax.dynamic_slice_in_dim(owner_slots, half * core, half, 0)
        index = jnp.arange(EXTRA * LANES, dtype=jnp.int32).reshape(1, EXTRA, LANES) % high
        slots = jnp.arange(half, dtype=jnp.int32)[:, None, None]
        own = jnp.sum(jnp.where(index == slots, own[:, None, None] + 1, 0), axis=0) - 1
        block = jnp.concatenate([mine, own.astype(records.dtype)], axis=0)
    column = [block]
    if ntmpl <= 8:
        for d in range(1, ntmpl):
            column.append(lax.ppermute(block, "tmpl", [(i, (i + d) % ntmpl) for i in range(ntmpl)]))
    else:
        column = list(lax.all_gather(block, "tmpl", axis=0))
    asked = [crossed(station_ids, d) for d in range(1, nslab)]
    waves = templates.transpose(1, 2, 0, 3)
    reach = round_up(taps + LANES - 1, LANES)
    depth = round_up(taps + SPAN - 1, LANES)
    groups = comps * js
    first, second = groups // 5, groups // 5

    def bank(size):
        return jax.ShapeDtypeStruct((size, depth, count * SPAN), jnp.bfloat16)

    column_type = jax.ShapeDtypeStruct((refs, LANES), jnp.int32)
    sid_col, off_col, mask, band, scale, waves, bank_a = pl.pallas_call(
        tables_kernel,
        out_shape=[
            column_type,
            column_type,
            jax.ShapeDtypeStruct((refs, time), jnp.float32),
            jax.ShapeDtypeStruct((2 * LANES, reach), jnp.bfloat16),
            jax.ShapeDtypeStruct((chans, LANES), jnp.float32),
            jax.ShapeDtypeStruct(waves.shape, waves.dtype),
            bank(first),
        ],
        in_specs=[hbm] * 5,
        out_specs=[vmem] * 7,
        scratch_shapes=[
            pltpu.SMEM(station_ids.shape, jnp.int32),
            pltpu.SMEM(offsets.shape, jnp.int32),
            pltpu.VMEM(gap_start.T.shape, jnp.int32),
            pltpu.VMEM(gap_len.T.shape, jnp.int32),
            pltpu.SemaphoreType.DMA((5,)),
        ],
        compiler_params=params(12),
        name="tables",
    )(*[stays(value) for value in (station_ids, offsets, gap_start.T, gap_len.T, waves)])
    column, asked, mask = lax.optimization_barrier((column, asked, mask))
    head = jnp.stack(column)
    heads = [head] + [swapped(head, "sub", m) for m in range(1, nsub)]
    *sid_far, bank_b = pl.pallas_call(
        functools.partial(middle_kernel, first, nslab - 1),
        out_shape=[column_type] * (nslab - 1) + [bank(second)],
        in_specs=[smem] * (nslab - 1) + [vmem],
        out_specs=[vmem] * nslab,
        compiler_params=params(12),
        name="middle",
    )(*asked, waves)
    heads, sid_far, bank_b = lax.optimization_barrier((heads, sid_far, bank_b))
    sid_cols = [sid_col] + list(sid_far)
    near, *fars = pl.pallas_call(
        functools.partial(select_kernel, comps, high, nsub),
        out_shape=[jax.ShapeDtypeStruct((chans, width), jnp.float32)]
        + [jax.ShapeDtypeStruct((chans, width), records.dtype)] * (nslab - 1),
        in_specs=[vmem] * (nsub + nslab + 1),
        out_specs=[vmem] * nslab,
        compiler_params=params(16),
        name="select",
    )(*heads, *sid_cols, mask)
    fars = [crossed(far, d + 1) for d, far in enumerate(fars)]
    bank_c = pl.pallas_call(
        functools.partial(filters_kernel, first + second),
        out_shape=bank(groups - first - second),
        in_specs=[vmem],
        out_specs=vmem,
        compiler_params=params(16),
        name="filters",
    )(waves)
    fars, bank_c = lax.optimization_barrier((fars, bank_c))
    chunks = time // LANES
    each = width // nsub
    tall = chunks + 8
    keep, send = pl.pallas_call(
        functools.partial(correlate_kernel, nslab, nsub, taps, 3),
        out_shape=[
            jax.ShapeDtypeStruct((nslab, count, each), jnp.float32),
            jax.ShapeDtypeStruct((nsub - 1, nslab, count, each), jnp.float32),
        ],
        in_specs=[vmem] * (nslab + 7),
        out_specs=[vmem] * 2,
        scratch_shapes=[
            pltpu.VMEM((chans, time), jnp.float32),
            pltpu.VMEM((chans, tall, LANES), jnp.float32),
            pltpu.VMEM((chans, tall, LANES), jnp.float32),
            pltpu.VMEM((chans, chunks, LANES), jnp.float32),
            pltpu.VMEM((count, chunks, LANES), jnp.float32),
        ],
        compiler_params=params(32),
        name="correlate",
    )(near, *fars, bank_a, bank_b, bank_c, off_col, mask, band, scale)
    for m in range(1, nsub):
        keep = keep + swapped(send[m - 1], "sub", m)
    lines = [keep[0]]
    for d in range(1, nslab):
        lines.append(crossed(keep[d], d))
    result = []
    for s in range(nslab):
        line = lines[0]
        for d in range(1, nslab):
            line = jnp.where((here ^ d) == s, lines[d], line)
        result.append(line)
    return jnp.concatenate(result, axis=0)


def solution(mesh):
    in_specs = (
        P(("grp", "tmpl"), None, "slab"),
        P(("grp", "tmpl")),
        P("grp", None),
        P("grp", None),
        P(("grp", "tmpl", "slab"), "sub", None, None),
        P(("grp", "tmpl", "slab"), "sub"),
        P(("grp", "tmpl", "slab"), "sub"),
    )
    out_specs = P(("grp", "tmpl"), ("slab", "sub"))
    return jax.shard_map(
        on_device, mesh=mesh, in_specs=in_specs, out_specs=out_specs, check_vma=False
    )
```

```python
import functools

import jax
import jax.numpy as jnp
from jax import lax
from jax.experimental import pallas as pl
from jax.experimental.pallas import tpu as pltpu
from jax.sharding import PartitionSpec as P

LANES = 128
SPAN = 64
EXTRA = 8
UNROLL = 6


def round_up(value, step):
    return -(-value // step) * step


def pack_kernel(owner_slots, records, block, owners, sems):
    comps, _, width = records.shape
    per = width // LANES
    half = (block.shape[0] - EXTRA) // (comps * per)
    first = pl.multiple_of(lax.axis_index("sub") * half, half)
    copies = [pltpu.make_async_copy(owner_slots, owners, sems.at[comps * per])]
    for i in range(comps * per):
        source = records.at[i // per, pl.ds(first, half), (i % per) * LANES : (i % per + 1) * LANES]
        copies.append(pltpu.make_async_copy(source, block.at[i * half : (i + 1) * half, :], sems.at[i]))
    for copy in copies:
        copy.start()
    copies[0].wait()
    lane = lax.rem(lax.broadcasted_iota(jnp.int32, (EXTRA, LANES), 1), half)
    line = jnp.full((EXTRA, LANES), -1, jnp.int32)
    for i in range(half):
        line = jnp.where(lane == i, owners[first + i], line)
    block[comps * per * half :, :] = line.astype(jnp.float32).astype(block.dtype)
    for copy in copies[1:]:
        copy.wait()


def build_filters(begin, waves, filters):
    js, _, count, taps = waves.shape
    groups, depth, _ = filters.shape

    def one_group(i):
        g = begin + i
        wave = waves[lax.rem(g, js), g // js].astype(jnp.float32)
        wave = jnp.concatenate([wave, jnp.zeros((count, depth - taps), jnp.float32)], axis=1)
        rows = []
        for k in range(count):
            row = jnp.broadcast_to(wave[k : k + 1], (SPAN, depth))
            rows.append(pltpu.roll(row, 0, 1, stride=1, stride_axis=0))
        filters[i] = jnp.concatenate(rows, axis=0).T.astype(jnp.bfloat16)

    def some_groups(t, carry):
        for u in range(UNROLL):
            one_group(t * UNROLL + u)
        return carry

    lax.fori_loop(0, groups // UNROLL, some_groups, 0)
    for i in range(groups // UNROLL * UNROLL, groups):
        one_group(i)


def tables_kernel(sids_in, offs_in, start_in, len_in, waves_in, sid_col, off_col, mask, band, scale, waves, filters, *scratch):
    sids, offs, gap_start, gap_len, sems = scratch
    pairs = ((waves_in, waves), (sids_in, sids), (offs_in, offs), (start_in, gap_start), (len_in, gap_len))
    copies = [pltpu.make_async_copy(source, place, sems.at[i]) for i, (source, place) in enumerate(pairs)]
    for copy in copies:
        copy.start()
    js, comps, count, taps = waves.shape
    refs = count * js
    rows = lax.rem(lax.broadcasted_iota(jnp.int32, band.shape, 0), LANES)
    cols = lax.broadcasted_iota(jnp.int32, band.shape, 1)
    lead = rows + (cols // LANES) * LANES - lax.rem(cols, LANES)
    band[...] = jnp.where((lead >= 0) & (lead < taps), 1.0, 0.0).astype(jnp.bfloat16)
    for copy in copies:
        copy.wait()
    for k in range(count):
        for j in range(js):
            row = j * count + k
            off_col[row, :] = jnp.full((LANES,), offs[k, j], jnp.int32)
            sid_col[row, :] = jnp.full((LANES,), sids[k, j], jnp.int32)
    nstation = gap_start.shape[1]
    own = lax.broadcasted_iota(jnp.int32, (refs, nstation), 1) == sid_col[:, :nstation]
    starts = gap_start[...].astype(jnp.float32)
    ends = starts + gap_len[...].astype(jnp.float32)
    live = jnp.ones(mask.shape, jnp.float32)
    times = lax.broadcasted_iota(jnp.int32, mask.shape, 1).astype(jnp.float32)
    for g in range(starts.shape[0]):
        first = jnp.sum(jnp.where(own, starts[g : g + 1], 0.0), axis=1, keepdims=True)
        last = jnp.sum(jnp.where(own, ends[g : g + 1], 0.0), axis=1, keepdims=True)
        live = jnp.where((times >= first) & (times < last), 0.0, live)
    mask[...] = live
    for c in range(comps):
        for j in range(js):
            wave = waves[j, c].astype(jnp.float32)
            power = jnp.sum(wave * wave, axis=1, keepdims=True) / taps
            factor = 1.0 / (taps * jnp.sqrt(power + 1e-06))
            first = (c * js + j) * count
            scale[first : first + count, :] = jnp.broadcast_to(factor, (count, LANES))
    build_filters(0, waves, filters)


def middle_kernel(begin, nfar, *args):
    asked, waves, columns, filters = args[:nfar], args[nfar], args[nfar + 1 : -1], args[-1]
    count, js = asked[0].shape
    for source, column in zip(asked, columns):
        for k in range(count):
            for j in range(js):
                column[j * count + k, :] = jnp.full((LANES,), source[k, j], jnp.int32)
    build_filters(begin, waves, filters)


def filters_kernel(begin, waves, filters):
    build_filters(begin, waves, filters)


def select_kernel(comps, high, nsub, *args):
    heads, args = args[:nsub], args[nsub:]
    asks = len(args) // 2
    sid_cols, outs = args[:asks], args[-asks:]
    masks = args[asks:-asks]
    refs = sid_cols[0].shape[0]
    ntmpl = heads[0].shape[0]
    width = outs[0].shape[1]
    per = width // LANES
    here = lax.axis_index("slab")
    rows_slab = comps * high
    blocks = [(part, z) for part in heads for z in range(ntmpl)]
    depth = len(blocks) * rows_slab
    owner = []
    for q in range(0, depth, LANES):
        lane = lax.broadcasted_iota(jnp.int32, (1, LANES), 1) + q
        line = jnp.full((1, LANES), -1.0, jnp.float32)
        for b, (part, z) in enumerate(blocks):
            if b * rows_slab < q + LANES and (b + 1) * rows_slab > q:
                tail = part[z, rows_slab * per : rows_slab * per + EXTRA, :].astype(jnp.float32)
                inside = (lane >= b * rows_slab) & (lane < (b + 1) * rows_slab)
                line = jnp.where(inside, tail[:1], line)
        owner.append(line)
    owner = jnp.concatenate(owner, axis=1)[:, :depth]
    row = lax.broadcasted_iota(jnp.int32, (1, depth), 1)
    row = lax.rem(row, rows_slab) // high
    columns = []
    for q in range(per):
        tiles = []
        for part, z in blocks:
            for c in range(comps):
                first = (c * per + q) * high
                tiles.append(part[z, first : first + high, :])
        columns.append(jnp.concatenate(tiles, axis=0))
    stack = jnp.concatenate(columns, axis=1)
    owners = [jnp.where(row == c, owner, -1.0) for c in range(comps)]
    for sid_col, out in zip(sid_cols, outs):
        wanted = sid_col[:, :1].astype(jnp.float32)
        pick = [jnp.where(owners[c] == wanted, 1.0, 0.0).astype(jnp.bfloat16) for c in range(comps)]
        got = jnp.dot(jnp.concatenate(pick, axis=0), stack, preferred_element_type=jnp.float32)
        if not masks:
            out[...] = got.astype(out.dtype)
        else:
            live = masks[0][:, pl.ds(pl.multiple_of(here * width, LANES), width)]
            for c in range(comps):
                out[c * refs : (c + 1) * refs, :] = got[c * refs : (c + 1) * refs] * live


def correlate_kernel(nslab, nsub, taps, nbank, *args):
    near, fars, args = args[0], args[1:nslab], args[nslab:]
    banks, args = args[:nbank], args[nbank:]
    off_col, mask, band, scale, keep, send, segs, low, high, norm, total = args
    refs, time = mask.shape
    chans, width = near.shape
    comps = chans // refs
    chunks = time // LANES
    count = keep.shape[1]
    here, core = lax.axis_index("slab"), lax.axis_index("sub")
    for d in range(nslab):
        spot = pl.ds(pl.multiple_of(lax.bitwise_xor(here, d) * width, LANES), width)
        if d == 0:
            segs[:, spot] = near[...]
        else:
            live = mask[:, spot]
            for c in range(comps):
                got = fars[d - 1][c * refs : (c + 1) * refs, :].astype(jnp.float32)
                segs[c * refs : (c + 1) * refs, spot] = got * live
    span = banks[0].shape[1] // LANES
    lane = lax.broadcasted_iota(jnp.int32, (8, LANES), 1)
    zero = jnp.zeros((8, LANES), jnp.float32)
    for i in range(chans // 8):
        ref_row = (i * 8) % refs
        off = off_col[ref_row : ref_row + 8, :]
        place = lax.bitwise_and(lane + off, LANES - 1)
        fine = lax.bitwise_and(off, LANES - 1)
        close = lane + fine < LANES
        far = off >= LANES
        turned = [
            jnp.take_along_axis(segs[i * 8 : i * 8 + 8, r * LANES : (r + 1) * LANES], place, axis=1)
            for r in range(chunks)
        ]
        turned += [zero, zero]
        moved = [jnp.where(close, turned[r], turned[r + 1]) for r in range(chunks + 1)]
        mine = [jnp.where(far, moved[r + 1], moved[r]) for r in range(chunks)]
        swung = [pltpu.roll(part, SPAN, 1) for part in mine] + [zero]
        for r in range(chunks):
            segs[i * 8 : i * 8 + 8, r * LANES : (r + 1) * LANES] = mine[r]
            low[pl.ds(i * 8, 8), r, :] = mine[r]
            high[pl.ds(i * 8, 8), r, :] = jnp.where(lane < LANES - SPAN, swung[r], swung[r + 1])
        for r in range(chunks, chunks + span - 1):
            low[pl.ds(i * 8, 8), r, :] = zero
            high[pl.ds(i * 8, 8), r, :] = zero
    reach = band.shape[1] // LANES
    sums = {}
    for first in range(0, chunks, 2):
        batch = range(first, first + 2)
        power = jnp.concatenate([segs[:, r * LANES : (r + 1) * LANES] for r in batch], axis=0)
        power = power * power
        lead = power.astype(jnp.bfloat16)
        rest = (power - lead.astype(jnp.float32)).astype(jnp.bfloat16)
        both = jnp.concatenate([lead, rest], axis=1)
        got = jnp.dot(both, band[...], preferred_element_type=jnp.float32)
        for r in batch:
            sums[r] = got[(r - first) * chans : (r - first + 1) * chans]
    for r in range(chunks):
        window = sums[r][:, :LANES]
        for p in range(1, min(reach, chunks - r)):
            window = window + sums[r + p][:, p * LANES : (p + 1) * LANES]
        factor = scale[...] * lax.rsqrt(window / taps + 1e-06)
        for i in range(chans // 8):
            norm[pl.ds(i * 8, 8), r, :] = factor[i * 8 : i * 8 + 8]
    accs = [jnp.zeros((chunks, LANES), jnp.float32) for _ in range(count)]
    side = lax.broadcasted_iota(jnp.int32, (chunks, LANES), 1) < SPAN
    weights = [(bank, i) for bank in banks for i in range(bank.shape[0])]
    def operand(g):
        rows = []
        for ch in range(g * count, (g + 1) * count):
            for source in (low, high):
                rows.append(jnp.concatenate([source[ch, p : p + chunks, :] for p in range(span)], axis=1))
        return jnp.concatenate(rows, axis=0).astype(jnp.bfloat16)

    def gather_sums(g, res):
        base = g * count
        for k in range(count):
            left = (k // 2) * LANES
            tile = res[2 * k * chunks : 2 * (k + 1) * chunks, left : left + LANES]
            early, late = tile[:chunks], tile[chunks:]
            if k % 2 == 0:
                first, turned = early, late
            else:
                turned = pltpu.roll(jnp.where(side, turned, early), SPAN, 1)
                even, odd = jnp.where(side, first, turned), jnp.where(side, turned, late)
                accs[k - 1] = accs[k - 1] + even * norm[base + k - 1]
                accs[k] = accs[k] + odd * norm[base + k]

    for g, (bank, i) in enumerate(weights):
        gather_sums(g, jnp.dot(operand(g), bank[i], preferred_element_type=jnp.float32))
    for k in range(count):
        total[k] = accs[k]
    each = chunks // (nslab * nsub)
    for d in range(nslab):
        for e in range(each):
            first = lax.bitwise_xor(here, d) * nsub * each + e
            turn = nsub - 1 if d else 0
            mine = first + lax.bitwise_xor(core, turn) * each
            keep[d, :, e * LANES : (e + 1) * LANES] = total[:, mine, :]
            for m in range(1, nsub):
                other = first + lax.bitwise_xor(core, m ^ turn) * each
                send[m - 1, d, :, e * LANES : (e + 1) * LANES] = total[:, other, :]


def swapped(value, axis, distance):
    return lax.ppermute(value, axis, [(i, i ^ distance) for i in range(lax.axis_size(axis))])


def crossed(value, distance):
    nsub = lax.axis_size("sub")
    count = lax.axis_size("slab") * nsub
    return lax.ppermute(value, ("slab", "sub"), [(i, i ^ (distance * nsub + nsub - 1)) for i in range(count)])


def stays(value):
    return pltpu.with_memory_space_constraint(value, pltpu.HBM)


def params(mib):
    return pltpu.CompilerParams(vmem_limit_bytes=mib << 20)


def on_device(records, owner_slots, gap_start, gap_len, templates, station_ids, offsets):
    nloc, comps, width = records.shape
    count, js, _, taps = templates.shape
    nslab, nsub, ntmpl = (lax.axis_size(name) for name in ("slab", "sub", "tmpl"))
    time = width * nslab
    refs = count * js
    chans = comps * refs
    here, core = lax.axis_index("slab"), lax.axis_index("sub")
    vmem, smem = pl.BlockSpec(memory_space=pltpu.VMEM), pl.BlockSpec(memory_space=pltpu.SMEM)
    hbm = pl.BlockSpec(memory_space=pltpu.HBM)
    half = nloc // nsub
    high = round_up(half, 16)
    per = width // LANES
    if high == half:
        block = pl.pallas_call(
            pack_kernel,
            out_shape=jax.ShapeDtypeStruct((comps * high * per + EXTRA, LANES), records.dtype),
            in_specs=[hbm, hbm],
            out_specs=vmem,
            scratch_shapes=[pltpu.SMEM((nloc,), jnp.int32), pltpu.SemaphoreType.DMA((comps * per + 1,))],
            compiler_params=params(4),
            name="pack",
        )(stays(owner_slots), stays(records.transpose(1, 0, 2)))
    else:
        mine = lax.dynamic_slice_in_dim(records.transpose(1, 0, 2), half * core, half, 1)
        mine = jnp.pad(mine, ((0, 0), (0, high - half), (0, 0))).reshape(comps, high, per, LANES)
        mine = mine.transpose(0, 2, 1, 3).reshape(comps * per * high, LANES)
        own = lax.dynamic_slice_in_dim(owner_slots, half * core, half, 0)
        index = jnp.arange(EXTRA * LANES, dtype=jnp.int32).reshape(1, EXTRA, LANES) % high
        slots = jnp.arange(half, dtype=jnp.int32)[:, None, None]
        own = jnp.sum(jnp.where(index == slots, own[:, None, None] + 1, 0), axis=0) - 1
        block = jnp.concatenate([mine, own.astype(records.dtype)], axis=0)
    column = [block]
    if ntmpl <= 8:
        for d in range(1, ntmpl):
            column.append(lax.ppermute(block, "tmpl", [(i, (i + d) % ntmpl) for i in range(ntmpl)]))
    else:
        column = list(lax.all_gather(block, "tmpl", axis=0))
    asked = [crossed(station_ids, d) for d in range(1, nslab)]
    waves = templates.transpose(1, 2, 0, 3)
    reach = round_up(taps + LANES - 1, LANES)
    depth = round_up(taps + SPAN - 1, LANES)
    groups = comps * js
    first, second = max(groups // 15, 1), groups // 5

    def bank(size):
        return jax.ShapeDtypeStruct((size, depth, count * SPAN), jnp.bfloat16)

    column_type = jax.ShapeDtypeStruct((refs, LANES), jnp.int32)
    sid_col, off_col, mask, band, scale, waves, bank_a = pl.pallas_call(
        tables_kernel,
        out_shape=[
            column_type,
            column_type,
            jax.ShapeDtypeStruct((refs, time), jnp.float32),
            jax.ShapeDtypeStruct((2 * LANES, reach), jnp.bfloat16),
            jax.ShapeDtypeStruct((chans, LANES), jnp.float32),
            jax.ShapeDtypeStruct(waves.shape, waves.dtype),
            bank(first),
        ],
        in_specs=[hbm] * 5,
        out_specs=[vmem] * 7,
        scratch_shapes=[
            pltpu.SMEM(station_ids.shape, jnp.int32),
            pltpu.SMEM(offsets.shape, jnp.int32),
            pltpu.VMEM(gap_start.T.shape, jnp.int32),
            pltpu.VMEM(gap_len.T.shape, jnp.int32),
            pltpu.SemaphoreType.DMA((5,)),
        ],
        compiler_params=params(12),
        name="tables",
    )(*[stays(value) for value in (station_ids, offsets, gap_start.T, gap_len.T, waves)])
    column, asked, mask = lax.optimization_barrier((column, asked, mask))
    head = jnp.stack(column)
    heads = [head] + [swapped(head, "sub", m) for m in range(1, nsub)]
    *sid_far, bank_b = pl.pallas_call(
        functools.partial(middle_kernel, first, nslab - 1),
        out_shape=[column_type] * (nslab - 1) + [bank(second)],
        in_specs=[smem] * (nslab - 1) + [vmem],
        out_specs=[vmem] * nslab,
        compiler_params=params(12),
        name="middle",
    )(*asked, waves)
    heads, sid_far, bank_b = lax.optimization_barrier((heads, sid_far, bank_b))

    def select(columns, masks, dtype):
        return pl.pallas_call(
            functools.partial(select_kernel, comps, high, nsub),
            out_shape=[jax.ShapeDtypeStruct((chans, width), dtype)] * len(columns),
            in_specs=[vmem] * (nsub + len(columns) + len(masks)),
            out_specs=[vmem] * len(columns),
            compiler_params=params(16),
            name="select",
        )(*heads, *columns, *masks)

    fars = select(sid_far, [], records.dtype)
    fars = [crossed(far, d + 1) for d, far in enumerate(fars)]
    bank_c = pl.pallas_call(
        functools.partial(filters_kernel, first + second),
        out_shape=bank(groups - first - second),
        in_specs=[vmem],
        out_specs=vmem,
        compiler_params=params(16),
        name="filters",
    )(waves)
    (near,) = select([sid_col], [mask], jnp.float32)
    fars, bank_c, near = lax.optimization_barrier((fars, bank_c, near))
    chunks = time // LANES
    each = width // nsub
    tall = chunks + 8
    keep, send = pl.pallas_call(
        functools.partial(correlate_kernel, nslab, nsub, taps, 3),
        out_shape=[
            jax.ShapeDtypeStruct((nslab, count, each), jnp.float32),
            jax.ShapeDtypeStruct((nsub - 1, nslab, count, each), jnp.float32),
        ],
        in_specs=[vmem] * (nslab + 7),
        out_specs=[vmem] * 2,
        scratch_shapes=[
            pltpu.VMEM((chans, time), jnp.float32),
            pltpu.VMEM((chans, tall, LANES), jnp.float32),
            pltpu.VMEM((chans, tall, LANES), jnp.float32),
            pltpu.VMEM((chans, chunks, LANES), jnp.float32),
            pltpu.VMEM((count, chunks, LANES), jnp.float32),
        ],
        compiler_params=params(32),
        name="correlate",
    )(near, *fars, bank_a, bank_b, bank_c, off_col, mask, band, scale)
    for m in range(1, nsub):
        keep = keep + swapped(send[m - 1], "sub", m)
    lines = [keep[0]]
    for d in range(1, nslab):
        lines.append(crossed(keep[d], d))
    result = []
    for s in range(nslab):
        line = lines[0]
        for d in range(1, nslab):
            line = jnp.where((here ^ d) == s, lines[d], line)
        result.append(line)
    return jnp.concatenate(result, axis=0)


def solution(mesh):
    in_specs = (
        P(("grp", "tmpl"), None, "slab"),
        P(("grp", "tmpl")),
        P("grp", None),
        P("grp", None),
        P(("grp", "tmpl", "slab"), "sub", None, None),
        P(("grp", "tmpl", "slab"), "sub"),
        P(("grp", "tmpl", "slab"), "sub"),
    )
    out_specs = P(("grp", "tmpl"), ("slab", "sub"))
    return jax.shard_map(
        on_device, mesh=mesh, in_specs=in_specs, out_specs=out_specs, check_vma=False
    )
```

```python
import functools

import jax
import jax.numpy as jnp
from jax import lax
from jax.experimental import pallas as pl
from jax.experimental.pallas import tpu as pltpu
from jax.sharding import PartitionSpec as P

LANES = 128
SPAN = 64
EXTRA = 8
UNROLL = 6


def round_up(value, step):
    return -(-value // step) * step


def pack_kernel(owner_slots, records, block, owners, sems):
    comps, _, width = records.shape
    per = width // LANES
    half = (block.shape[0] - EXTRA) // (comps * per)
    first = pl.multiple_of(lax.axis_index("sub") * half, half)
    copies = [pltpu.make_async_copy(owner_slots, owners, sems.at[comps * per])]
    for i in range(comps * per):
        source = records.at[i // per, pl.ds(first, half), (i % per) * LANES : (i % per + 1) * LANES]
        copies.append(pltpu.make_async_copy(source, block.at[i * half : (i + 1) * half, :], sems.at[i]))
    for copy in copies:
        copy.start()
    copies[0].wait()
    lane = lax.rem(lax.broadcasted_iota(jnp.int32, (EXTRA, LANES), 1), half)
    line = jnp.full((EXTRA, LANES), -1, jnp.int32)
    for i in range(half):
        line = jnp.where(lane == i, owners[first + i], line)
    block[comps * per * half :, :] = line.astype(jnp.float32).astype(block.dtype)
    for copy in copies[1:]:
        copy.wait()


def build_filters(begin, waves, filters):
    js, _, count, taps = waves.shape
    groups, depth, _ = filters.shape

    def one_group(i):
        g = begin + i
        wave = waves[lax.rem(g, js), g // js].astype(jnp.float32)
        wave = jnp.concatenate([wave, jnp.zeros((count, depth - taps), jnp.float32)], axis=1)
        rows = []
        for k in range(count):
            row = jnp.broadcast_to(wave[k : k + 1], (SPAN, depth))
            rows.append(pltpu.roll(row, 0, 1, stride=1, stride_axis=0))
        filters[i] = jnp.concatenate(rows, axis=0).T.astype(jnp.bfloat16)

    def some_groups(t, carry):
        for u in range(UNROLL):
            one_group(t * UNROLL + u)
        return carry

    lax.fori_loop(0, groups // UNROLL, some_groups, 0)
    for i in range(groups // UNROLL * UNROLL, groups):
        one_group(i)


def tables_kernel(sids_in, offs_in, start_in, len_in, waves_in, sid_col, off_col, mask, band, scale, waves, filters, *scratch):
    sids, offs, gap_start, gap_len, sems = scratch
    pairs = ((waves_in, waves), (sids_in, sids), (offs_in, offs), (start_in, gap_start), (len_in, gap_len))
    copies = [pltpu.make_async_copy(source, place, sems.at[i]) for i, (source, place) in enumerate(pairs)]
    for copy in copies:
        copy.start()
    js, comps, count, taps = waves.shape
    refs = count * js
    rows = lax.rem(lax.broadcasted_iota(jnp.int32, band.shape, 0), LANES)
    cols = lax.broadcasted_iota(jnp.int32, band.shape, 1)
    lead = rows + (cols // LANES) * LANES - lax.rem(cols, LANES)
    band[...] = jnp.where((lead >= 0) & (lead < taps), 1.0, 0.0).astype(jnp.bfloat16)
    for copy in copies:
        copy.wait()
    for k in range(count):
        for j in range(js):
            row = j * count + k
            off_col[row, :] = jnp.full((LANES,), offs[k, j], jnp.int32)
            sid_col[row, :] = jnp.full((LANES,), sids[k, j], jnp.int32)
    nstation = gap_start.shape[1]
    own = lax.broadcasted_iota(jnp.int32, (refs, nstation), 1) == sid_col[:, :nstation]
    starts = gap_start[...].astype(jnp.float32)
    ends = starts + gap_len[...].astype(jnp.float32)
    live = jnp.ones(mask.shape, jnp.float32)
    times = lax.broadcasted_iota(jnp.int32, mask.shape, 1).astype(jnp.float32)
    for g in range(starts.shape[0]):
        first = jnp.sum(jnp.where(own, starts[g : g + 1], 0.0), axis=1, keepdims=True)
        last = jnp.sum(jnp.where(own, ends[g : g + 1], 0.0), axis=1, keepdims=True)
        live = jnp.where((times >= first) & (times < last), 0.0, live)
    mask[...] = live
    for c in range(comps):
        for j in range(js):
            wave = waves[j, c].astype(jnp.float32)
            power = jnp.sum(wave * wave, axis=1, keepdims=True) / taps
            factor = 1.0 / (taps * jnp.sqrt(power + 1e-06))
            first = (c * js + j) * count
            scale[first : first + count, :] = jnp.broadcast_to(factor, (count, LANES))
    build_filters(0, waves, filters)


def middle_kernel(begin, nfar, *args):
    asked, waves, columns, filters = args[:nfar], args[nfar], args[nfar + 1 : -1], args[-1]
    count, js = asked[0].shape
    for source, column in zip(asked, columns):
        for k in range(count):
            for j in range(js):
                column[j * count + k, :] = jnp.full((LANES,), source[k, j], jnp.int32)
    build_filters(begin, waves, filters)


def filters_kernel(begin, waves, filters):
    build_filters(begin, waves, filters)


def select_kernel(comps, high, nsub, asks, nmask, *args):
    heads, args = args[:nsub], args[nsub:]
    sid_cols, masks, outs = args[:asks], args[asks : asks + nmask], args[asks + nmask :]
    refs = sid_cols[0].shape[0]
    ntmpl = heads[0].shape[0]
    width = outs[0].shape[1]
    per = width // LANES
    here = lax.axis_index("slab")
    rows_slab = comps * high
    blocks = [(part, z) for part in heads for z in range(ntmpl)]
    depth = len(blocks) * rows_slab
    owner = []
    for q in range(0, depth, LANES):
        lane = lax.broadcasted_iota(jnp.int32, (1, LANES), 1) + q
        line = jnp.full((1, LANES), -1.0, jnp.float32)
        for b, (part, z) in enumerate(blocks):
            if b * rows_slab < q + LANES and (b + 1) * rows_slab > q:
                tail = part[z, rows_slab * per : rows_slab * per + EXTRA, :].astype(jnp.float32)
                inside = (lane >= b * rows_slab) & (lane < (b + 1) * rows_slab)
                line = jnp.where(inside, tail[:1], line)
        owner.append(line)
    owner = jnp.concatenate(owner, axis=1)[:, :depth]
    row = lax.broadcasted_iota(jnp.int32, (1, depth), 1)
    row = lax.rem(row, rows_slab) // high
    columns = []
    for q in range(per):
        tiles = []
        for part, z in blocks:
            for c in range(comps):
                first = (c * per + q) * high
                tiles.append(part[z, first : first + high, :])
        columns.append(jnp.concatenate(tiles, axis=0))
    stack = jnp.concatenate(columns, axis=1)
    owners = [jnp.where(row == c, owner, -1.0) for c in range(comps)]
    for d, (sid_col, out) in enumerate(zip(sid_cols, outs)):
        wanted = sid_col[:, :1].astype(jnp.float32)
        pick = [jnp.where(owners[c] == wanted, 1.0, 0.0).astype(jnp.bfloat16) for c in range(comps)]
        got = jnp.dot(jnp.concatenate(pick, axis=0), stack, preferred_element_type=jnp.float32)
        if not masks:
            split = out.shape[0]
            out[...] = got[:split].astype(out.dtype)
            outs[asks + d][...] = got[split:].astype(out.dtype)
        else:
            live = masks[0][:, pl.ds(pl.multiple_of(here * width, LANES), width)]
            for c in range(comps):
                out[c * refs : (c + 1) * refs, :] = got[c * refs : (c + 1) * refs] * live


def correlate_kernel(nslab, nsub, taps, nbank, start, last, *args):
    near, fars, args = args[0], args[1:nslab], args[nslab:]
    banks, args = args[:nbank], args[nbank:]
    if start:
        before, args = args[0], args[1:]
    off_col, mask, band, scale, args = *args[:4], args[4:]
    if last:
        keep, send, segs, low, high, norm, total = args
    else:
        total, segs, low, high, norm = args
    refs, time = mask.shape
    chans, width = fars[0].shape
    comps = chans // refs
    chunks = time // LANES
    count = total.shape[0]
    js = refs // count
    here, core = lax.axis_index("slab"), lax.axis_index("sub")
    for d in range(nslab):
        spot = pl.ds(pl.multiple_of(lax.bitwise_xor(here, d) * width, LANES), width)
        if d == 0:
            segs[:, spot] = near[start * refs : start * refs + chans, :]
        else:
            live = mask[:, spot]
            for c in range(comps):
                got = fars[d - 1][c * refs : (c + 1) * refs, :].astype(jnp.float32)
                segs[c * refs : (c + 1) * refs, spot] = got * live
    lane = lax.broadcasted_iota(jnp.int32, (8, LANES), 1)
    zero = jnp.zeros((8, LANES), jnp.float32)
    span = banks[0].shape[1] // LANES
    for i in range(chans // 8):
        ref_row = (i * 8) % refs
        off = off_col[ref_row : ref_row + 8, :]
        place = lax.bitwise_and(lane + off, LANES - 1)
        fine = lax.bitwise_and(off, LANES - 1)
        close = lane + fine < LANES
        far = off >= LANES
        turned = [
            jnp.take_along_axis(segs[i * 8 : i * 8 + 8, r * LANES : (r + 1) * LANES], place, axis=1)
            for r in range(chunks)
        ]
        turned += [zero, zero]
        moved = [jnp.where(close, turned[r], turned[r + 1]) for r in range(chunks + 1)]
        mine = [jnp.where(far, moved[r + 1], moved[r]) for r in range(chunks)]
        swung = [pltpu.roll(part, SPAN, 1) for part in mine] + [zero]
        for r in range(chunks):
            segs[i * 8 : i * 8 + 8, r * LANES : (r + 1) * LANES] = mine[r]
            low[pl.ds(i * 8, 8), r, :] = mine[r]
            high[pl.ds(i * 8, 8), r, :] = jnp.where(lane < LANES - SPAN, swung[r], swung[r + 1])
        for r in range(chunks, chunks + span - 1):
            low[pl.ds(i * 8, 8), r, :] = zero
            high[pl.ds(i * 8, 8), r, :] = zero
    reach = band.shape[1] // LANES
    sums = {}
    for first in range(0, chunks, 2):
        batch = range(first, first + 2)
        power = jnp.concatenate([segs[:, r * LANES : (r + 1) * LANES] for r in batch], axis=0)
        power = power * power
        lead = power.astype(jnp.bfloat16)
        rest = (power - lead.astype(jnp.float32)).astype(jnp.bfloat16)
        both = jnp.concatenate([lead, rest], axis=1)
        got = jnp.dot(both, band[...], preferred_element_type=jnp.float32)
        for r in batch:
            sums[r] = got[(r - first) * chans : (r - first + 1) * chans]
    for r in range(chunks):
        window = sums[r][:, :LANES]
        for p in range(1, min(reach, chunks - r)):
            window = window + sums[r + p][:, p * LANES : (p + 1) * LANES]
        factor = scale[start * refs : start * refs + chans, :] * lax.rsqrt(window / taps + 1e-06)
        for i in range(chans // 8):
            norm[pl.ds(i * 8, 8), r, :] = factor[i * 8 : i * 8 + 8]
    accs = [before[k] if start else jnp.zeros((chunks, LANES), jnp.float32) for k in range(count)]
    side = lax.broadcasted_iota(jnp.int32, (chunks, LANES), 1) < SPAN
    weights = [(bank, i) for bank in banks for i in range(bank.shape[0])]
    weights = weights[start * js : (start + comps) * js]
    def operand(g):
        rows = []
        for ch in range(g * count, (g + 1) * count):
            for source in (low, high):
                rows.append(jnp.concatenate([source[ch, p : p + chunks, :] for p in range(span)], axis=1))
        return jnp.concatenate(rows, axis=0).astype(jnp.bfloat16)

    def gather_sums(g, res):
        base = g * count
        for k in range(count):
            left = (k // 2) * LANES
            tile = res[2 * k * chunks : 2 * (k + 1) * chunks, left : left + LANES]
            early, late = tile[:chunks], tile[chunks:]
            if k % 2 == 0:
                first, turned = early, late
            else:
                turned = pltpu.roll(jnp.where(side, turned, early), SPAN, 1)
                even, odd = jnp.where(side, first, turned), jnp.where(side, turned, late)
                accs[k - 1] = accs[k - 1] + even * norm[base + k - 1]
                accs[k] = accs[k] + odd * norm[base + k]

    for g, (bank, i) in enumerate(weights):
        gather_sums(g, jnp.dot(operand(g), bank[i], preferred_element_type=jnp.float32))
    for k in range(count):
        total[k] = accs[k]
    if not last:
        return
    each = chunks // (nslab * nsub)
    for d in range(nslab):
        for e in range(each):
            first = lax.bitwise_xor(here, d) * nsub * each + e
            turn = nsub - 1 if d else 0
            mine = first + lax.bitwise_xor(core, turn) * each
            keep[d, :, e * LANES : (e + 1) * LANES] = total[:, mine, :]
            for m in range(1, nsub):
                other = first + lax.bitwise_xor(core, m ^ turn) * each
                send[m - 1, d, :, e * LANES : (e + 1) * LANES] = total[:, other, :]


def swapped(value, axis, distance):
    return lax.ppermute(value, axis, [(i, i ^ distance) for i in range(lax.axis_size(axis))])


def crossed(value, distance):
    nsub = lax.axis_size("sub")
    count = lax.axis_size("slab") * nsub
    return lax.ppermute(value, ("slab", "sub"), [(i, i ^ (distance * nsub + nsub - 1)) for i in range(count)])


def stays(value):
    return pltpu.with_memory_space_constraint(value, pltpu.HBM)


def params(mib):
    return pltpu.CompilerParams(vmem_limit_bytes=mib << 20)


def on_device(records, owner_slots, gap_start, gap_len, templates, station_ids, offsets):
    nloc, comps, width = records.shape
    count, js, _, taps = templates.shape
    nslab, nsub, ntmpl = (lax.axis_size(name) for name in ("slab", "sub", "tmpl"))
    time = width * nslab
    refs = count * js
    chans = comps * refs
    here, core = lax.axis_index("slab"), lax.axis_index("sub")
    vmem, smem = pl.BlockSpec(memory_space=pltpu.VMEM), pl.BlockSpec(memory_space=pltpu.SMEM)
    hbm = pl.BlockSpec(memory_space=pltpu.HBM)
    half = nloc // nsub
    high = round_up(half, 16)
    per = width // LANES
    if high == half:
        block = pl.pallas_call(
            pack_kernel,
            out_shape=jax.ShapeDtypeStruct((comps * high * per + EXTRA, LANES), records.dtype),
            in_specs=[hbm, hbm],
            out_specs=vmem,
            scratch_shapes=[pltpu.SMEM((nloc,), jnp.int32), pltpu.SemaphoreType.DMA((comps * per + 1,))],
            compiler_params=params(4),
            name="pack",
        )(stays(owner_slots), stays(records.transpose(1, 0, 2)))
    else:
        mine = lax.dynamic_slice_in_dim(records.transpose(1, 0, 2), half * core, half, 1)
        mine = jnp.pad(mine, ((0, 0), (0, high - half), (0, 0))).reshape(comps, high, per, LANES)
        mine = mine.transpose(0, 2, 1, 3).reshape(comps * per * high, LANES)
        own = lax.dynamic_slice_in_dim(owner_slots, half * core, half, 0)
        index = jnp.arange(EXTRA * LANES, dtype=jnp.int32).reshape(1, EXTRA, LANES) % high
        slots = jnp.arange(half, dtype=jnp.int32)[:, None, None]
        own = jnp.sum(jnp.where(index == slots, own[:, None, None] + 1, 0), axis=0) - 1
        block = jnp.concatenate([mine, own.astype(records.dtype)], axis=0)
    column = [block]
    if ntmpl <= 8:
        for d in range(1, ntmpl):
            column.append(lax.ppermute(block, "tmpl", [(i, (i + d) % ntmpl) for i in range(ntmpl)]))
    else:
        column = list(lax.all_gather(block, "tmpl", axis=0))
    asked = [crossed(station_ids, d) for d in range(1, nslab)]
    waves = templates.transpose(1, 2, 0, 3)
    reach = round_up(taps + LANES - 1, LANES)
    depth = round_up(taps + SPAN - 1, LANES)
    groups = comps * js
    first, second = max(groups // 15, 1), groups // 5

    def bank(size):
        return jax.ShapeDtypeStruct((size, depth, count * SPAN), jnp.bfloat16)

    column_type = jax.ShapeDtypeStruct((refs, LANES), jnp.int32)
    sid_col, off_col, mask, band, scale, waves, bank_a = pl.pallas_call(
        tables_kernel,
        out_shape=[
            column_type,
            column_type,
            jax.ShapeDtypeStruct((refs, time), jnp.float32),
            jax.ShapeDtypeStruct((2 * LANES, reach), jnp.bfloat16),
            jax.ShapeDtypeStruct((chans, LANES), jnp.float32),
            jax.ShapeDtypeStruct(waves.shape, waves.dtype),
            bank(first),
        ],
        in_specs=[hbm] * 5,
        out_specs=[vmem] * 7,
        scratch_shapes=[
            pltpu.SMEM(station_ids.shape, jnp.int32),
            pltpu.SMEM(offsets.shape, jnp.int32),
            pltpu.VMEM(gap_start.T.shape, jnp.int32),
            pltpu.VMEM(gap_len.T.shape, jnp.int32),
            pltpu.SemaphoreType.DMA((5,)),
        ],
        compiler_params=params(12),
        name="tables",
    )(*[stays(value) for value in (station_ids, offsets, gap_start.T, gap_len.T, waves)])
    column, asked, mask = lax.optimization_barrier((column, asked, mask))
    head = jnp.stack(column)
    heads = [head] + [swapped(head, "sub", m) for m in range(1, nsub)]
    *sid_far, bank_b = pl.pallas_call(
        functools.partial(middle_kernel, first, nslab - 1),
        out_shape=[column_type] * (nslab - 1) + [bank(second)],
        in_specs=[smem] * (nslab - 1) + [vmem],
        out_specs=[vmem] * nslab,
        compiler_params=params(12),
        name="middle",
    )(*asked, waves)
    heads, sid_far, bank_b = lax.optimization_barrier((heads, sid_far, bank_b))

    def select(columns, masks, heights, dtype):
        sizes = [size for size in heights for _ in columns]
        return pl.pallas_call(
            functools.partial(select_kernel, comps, high, nsub, len(columns), len(masks)),
            out_shape=[jax.ShapeDtypeStruct((size, width), dtype) for size in sizes],
            in_specs=[vmem] * (nsub + len(columns) + len(masks)),
            out_specs=[vmem] * len(sizes),
            compiler_params=params(16),
            name="select",
        )(*heads, *columns, *masks)

    ahead = comps - 1
    fars = select(sid_far, [], [ahead * refs, chans - ahead * refs], records.dtype)
    early = [crossed(far, d + 1) for d, far in enumerate(fars[: nslab - 1])]
    late = [crossed(far, d + 1) for d, far in enumerate(fars[nslab - 1 :])]
    bank_c = pl.pallas_call(
        functools.partial(filters_kernel, first + second),
        out_shape=bank(groups - first - second),
        in_specs=[vmem],
        out_specs=vmem,
        compiler_params=params(16),
        name="filters",
    )(waves)
    (near,) = select([sid_col], [mask], [chans], jnp.float32)
    early, bank_c, near = lax.optimization_barrier((early, bank_c, near))
    chunks = time // LANES
    each = width // nsub
    tall = chunks + 8
    stack_type = jax.ShapeDtypeStruct((count, chunks, LANES), jnp.float32)

    def correlate(start, far, before, last):
        size = far[0].shape[0]
        scratch = [
            pltpu.VMEM((size, time), jnp.float32),
            pltpu.VMEM((size, tall, LANES), jnp.float32),
            pltpu.VMEM((size, tall, LANES), jnp.float32),
            pltpu.VMEM((size, chunks, LANES), jnp.float32),
        ]
        shapes = [stack_type]
        if last:
            scratch.append(pltpu.VMEM(stack_type.shape, jnp.float32))
            shapes = [
                jax.ShapeDtypeStruct((nslab, count, each), jnp.float32),
                jax.ShapeDtypeStruct((nsub - 1, nslab, count, each), jnp.float32),
            ]
        operands = [near, *far, bank_a, bank_b, bank_c, *before, off_col, mask, band, scale]
        return pl.pallas_call(
            functools.partial(correlate_kernel, nslab, nsub, taps, 3, start, last),
            out_shape=shapes,
            in_specs=[vmem] * len(operands),
            out_specs=[vmem] * len(shapes),
            scratch_shapes=scratch,
            compiler_params=params(24),
            name="correlate",
        )(*operands)

    before = correlate(0, early, [], False)
    keep, send = correlate(ahead, late, before, True)
    for m in range(1, nsub):
        keep = keep + swapped(send[m - 1], "sub", m)
    lines = [keep[0]]
    for d in range(1, nslab):
        lines.append(crossed(keep[d], d))
    result = []
    for s in range(nslab):
        line = lines[0]
        for d in range(1, nslab):
            line = jnp.where((here ^ d) == s, lines[d], line)
        result.append(line)
    return jnp.concatenate(result, axis=0)


def solution(mesh):
    in_specs = (
        P(("grp", "tmpl"), None, "slab"),
        P(("grp", "tmpl")),
        P("grp", None),
        P("grp", None),
        P(("grp", "tmpl", "slab"), "sub", None, None),
        P(("grp", "tmpl", "slab"), "sub"),
        P(("grp", "tmpl", "slab"), "sub"),
    )
    out_specs = P(("grp", "tmpl"), ("slab", "sub"))
    return jax.shard_map(
        on_device, mesh=mesh, in_specs=in_specs, out_specs=out_specs, check_vma=False
    )
```

```python
import functools

import jax
import jax.numpy as jnp
from jax import lax
from jax.experimental import pallas as pl
from jax.experimental.pallas import tpu as pltpu
from jax.sharding import PartitionSpec as P

LANES = 128
SPAN = 64
EXTRA = 8
UNROLL = 6


def round_up(value, step):
    return -(-value // step) * step


def pack_kernel(owner_slots, records, block, owners, sems):
    comps, _, width = records.shape
    per = width // LANES
    half = (block.shape[0] - EXTRA) // (comps * per)
    first = pl.multiple_of(lax.axis_index("sub") * half, half)
    copies = [pltpu.make_async_copy(owner_slots, owners, sems.at[comps * per])]
    for i in range(comps * per):
        source = records.at[i // per, pl.ds(first, half), (i % per) * LANES : (i % per + 1) * LANES]
        copies.append(pltpu.make_async_copy(source, block.at[i * half : (i + 1) * half, :], sems.at[i]))
    for copy in copies:
        copy.start()
    copies[0].wait()
    lane = lax.rem(lax.broadcasted_iota(jnp.int32, (EXTRA, LANES), 1), half)
    line = jnp.full((EXTRA, LANES), -1, jnp.int32)
    for i in range(half):
        line = jnp.where(lane == i, owners[first + i], line)
    block[comps * per * half :, :] = line.astype(jnp.float32).astype(block.dtype)
    for copy in copies[1:]:
        copy.wait()


def build_filters(begin, waves, filters):
    js, _, count, taps = waves.shape
    groups, depth, _ = filters.shape

    def one_group(i):
        g = begin + i
        wave = waves[lax.rem(g, js), g // js].astype(jnp.float32)
        wave = jnp.concatenate([wave, jnp.zeros((count, depth - taps), jnp.float32)], axis=1)
        rows = []
        for k in range(count):
            row = jnp.broadcast_to(wave[k : k + 1], (SPAN, depth))
            rows.append(pltpu.roll(row, 0, 1, stride=1, stride_axis=0))
        filters[i] = jnp.concatenate(rows, axis=0).T.astype(jnp.bfloat16)

    def some_groups(t, carry):
        for u in range(UNROLL):
            one_group(t * UNROLL + u)
        return carry

    lax.fori_loop(0, groups // UNROLL, some_groups, 0)
    for i in range(groups // UNROLL * UNROLL, groups):
        one_group(i)


def tables_kernel(sids_in, offs_in, start_in, len_in, waves_in, sid_col, off_col, mask, band, scale, waves, filters, *scratch):
    sids, offs, gap_start, gap_len, sems = scratch
    pairs = ((waves_in, waves), (sids_in, sids), (offs_in, offs), (start_in, gap_start), (len_in, gap_len))
    copies = [pltpu.make_async_copy(source, place, sems.at[i]) for i, (source, place) in enumerate(pairs)]
    for copy in copies:
        copy.start()
    js, comps, count, taps = waves.shape
    refs = count * js
    rows = lax.rem(lax.broadcasted_iota(jnp.int32, band.shape, 0), LANES)
    cols = lax.broadcasted_iota(jnp.int32, band.shape, 1)
    lead = rows + (cols // LANES) * LANES - lax.rem(cols, LANES)
    band[...] = jnp.where((lead >= 0) & (lead < taps), 1.0, 0.0).astype(jnp.bfloat16)
    for copy in copies:
        copy.wait()
    for k in range(count):
        for j in range(js):
            row = j * count + k
            off_col[row, :] = jnp.full((LANES,), offs[k, j], jnp.int32)
            sid_col[row, :] = jnp.full((LANES,), sids[k, j], jnp.int32)
    nstation = gap_start.shape[1]
    own = lax.broadcasted_iota(jnp.int32, (refs, nstation), 1) == sid_col[:, :nstation]
    starts = gap_start[...].astype(jnp.float32)
    ends = starts + gap_len[...].astype(jnp.float32)
    live = jnp.ones(mask.shape, jnp.float32)
    times = lax.broadcasted_iota(jnp.int32, mask.shape, 1).astype(jnp.float32)
    for g in range(starts.shape[0]):
        first = jnp.sum(jnp.where(own, starts[g : g + 1], 0.0), axis=1, keepdims=True)
        last = jnp.sum(jnp.where(own, ends[g : g + 1], 0.0), axis=1, keepdims=True)
        live = jnp.where((times >= first) & (times < last), 0.0, live)
    mask[...] = live
    for c in range(comps):
        for j in range(js):
            wave = waves[j, c].astype(jnp.float32)
            power = jnp.sum(wave * wave, axis=1, keepdims=True) / taps
            factor = 1.0 / (taps * jnp.sqrt(power + 1e-06))
            first = (c * js + j) * count
            scale[first : first + count, :] = jnp.broadcast_to(factor, (count, LANES))
    build_filters(0, waves, filters)


def middle_kernel(begin, nfar, *args):
    asked, waves, columns, filters = args[:nfar], args[nfar], args[nfar + 1 : -1], args[-1]
    count, js = asked[0].shape
    for source, column in zip(asked, columns):
        for k in range(count):
            for j in range(js):
                column[j * count + k, :] = jnp.full((LANES,), source[k, j], jnp.int32)
    build_filters(begin, waves, filters)


def filters_kernel(begin, waves, filters):
    build_filters(begin, waves, filters)


def select_kernel(comps, high, nsub, asks, nmask, *args):
    heads, args = args[:nsub], args[nsub:]
    sid_cols, masks, outs = args[:asks], args[asks : asks + nmask], args[asks + nmask :]
    refs = sid_cols[0].shape[0]
    ntmpl = heads[0].shape[0]
    width = outs[0].shape[1]
    per = width // LANES
    here = lax.axis_index("slab")
    rows_slab = comps * high
    blocks = [(part, z) for part in heads for z in range(ntmpl)]
    depth = len(blocks) * rows_slab
    owner = []
    for q in range(0, depth, LANES):
        lane = lax.broadcasted_iota(jnp.int32, (1, LANES), 1) + q
        line = jnp.full((1, LANES), -1.0, jnp.float32)
        for b, (part, z) in enumerate(blocks):
            if b * rows_slab < q + LANES and (b + 1) * rows_slab > q:
                tail = part[z, rows_slab * per : rows_slab * per + EXTRA, :].astype(jnp.float32)
                inside = (lane >= b * rows_slab) & (lane < (b + 1) * rows_slab)
                line = jnp.where(inside, tail[:1], line)
        owner.append(line)
    owner = jnp.concatenate(owner, axis=1)[:, :depth]
    row = lax.broadcasted_iota(jnp.int32, (1, depth), 1)
    row = lax.rem(row, rows_slab) // high
    columns = []
    for q in range(per):
        tiles = []
        for part, z in blocks:
            for c in range(comps):
                first = (c * per + q) * high
                tiles.append(part[z, first : first + high, :])
        columns.append(jnp.concatenate(tiles, axis=0))
    stack = jnp.concatenate(columns, axis=1)
    owners = [jnp.where(row == c, owner, -1.0) for c in range(comps)]
    for d, (sid_col, out) in enumerate(zip(sid_cols, outs)):
        wanted = sid_col[:, :1].astype(jnp.float32)
        pick = [jnp.where(owners[c] == wanted, 1.0, 0.0).astype(jnp.bfloat16) for c in range(comps)]
        got = jnp.dot(jnp.concatenate(pick, axis=0), stack, preferred_element_type=jnp.float32)
        if not masks:
            split = out.shape[0]
            out[...] = got[:split].astype(out.dtype)
            outs[asks + d][...] = got[split:].astype(out.dtype)
        else:
            live = masks[0][:, pl.ds(pl.multiple_of(here * width, LANES), width)]
            for c in range(comps):
                out[c * refs : (c + 1) * refs, :] = got[c * refs : (c + 1) * refs] * live


def correlate_kernel(nslab, nsub, taps, nbank, start, last, *args):
    near, fars, args = args[0], args[1:nslab], args[nslab:]
    banks, args = args[:nbank], args[nbank:]
    if start:
        before, args = args[0], args[1:]
    off_col, mask, band, scale, args = *args[:4], args[4:]
    if last:
        keep, send, segs, low, high, norm, total = args
    else:
        total, segs, low, high, norm = args
    refs, time = mask.shape
    chans, width = fars[0].shape
    comps = chans // refs
    chunks = time // LANES
    count = total.shape[0]
    js = refs // count
    here, core = lax.axis_index("slab"), lax.axis_index("sub")
    for d in range(nslab):
        spot = pl.ds(pl.multiple_of(lax.bitwise_xor(here, d) * width, LANES), width)
        if d == 0:
            segs[:, spot] = near[start * refs : start * refs + chans, :]
        else:
            live = mask[:, spot]
            for c in range(comps):
                got = fars[d - 1][c * refs : (c + 1) * refs, :].astype(jnp.float32)
                segs[c * refs : (c + 1) * refs, spot] = got * live
    lane = lax.broadcasted_iota(jnp.int32, (8, LANES), 1)
    zero = jnp.zeros((8, LANES), jnp.float32)
    span = banks[0].shape[1] // LANES
    for i in range(chans // 8):
        ref_row = (i * 8) % refs
        off = off_col[ref_row : ref_row + 8, :]
        place = lax.bitwise_and(lane + off, LANES - 1)
        fine = lax.bitwise_and(off, LANES - 1)
        close = lane + fine < LANES
        far = off >= LANES
        turned = [
            jnp.take_along_axis(segs[i * 8 : i * 8 + 8, r * LANES : (r + 1) * LANES], place, axis=1)
            for r in range(chunks)
        ]
        turned += [zero, zero]
        moved = [jnp.where(close, turned[r], turned[r + 1]) for r in range(chunks + 1)]
        mine = [jnp.where(far, moved[r + 1], moved[r]) for r in range(chunks)]
        swung = [pltpu.roll(part, SPAN, 1) for part in mine] + [zero]
        for r in range(chunks):
            segs[i * 8 : i * 8 + 8, r * LANES : (r + 1) * LANES] = mine[r]
            low[pl.ds(i * 8, 8), r, :] = mine[r]
            high[pl.ds(i * 8, 8), r, :] = jnp.where(lane < LANES - SPAN, swung[r], swung[r + 1])
        for r in range(chunks, chunks + span - 1):
            low[pl.ds(i * 8, 8), r, :] = zero
            high[pl.ds(i * 8, 8), r, :] = zero
    reach = band.shape[1] // LANES
    sums = {}
    for first in range(0, chunks, 2):
        batch = range(first, first + 2)
        power = jnp.concatenate([segs[:, r * LANES : (r + 1) * LANES] for r in batch], axis=0)
        power = power * power
        lead = power.astype(jnp.bfloat16)
        rest = (power - lead.astype(jnp.float32)).astype(jnp.bfloat16)
        both = jnp.concatenate([lead, rest], axis=1)
        got = jnp.dot(both, band[...], preferred_element_type=jnp.float32)
        for r in batch:
            sums[r] = got[(r - first) * chans : (r - first + 1) * chans]
    for r in range(chunks):
        window = sums[r][:, :LANES]
        for p in range(1, min(reach, chunks - r)):
            window = window + sums[r + p][:, p * LANES : (p + 1) * LANES]
        factor = scale[start * refs : start * refs + chans, :] * lax.rsqrt(window / taps + 1e-06)
        for i in range(chans // 8):
            norm[pl.ds(i * 8, 8), r, :] = factor[i * 8 : i * 8 + 8]
    accs = [before[k] if start else jnp.zeros((chunks, LANES), jnp.float32) for k in range(count)]
    side = lax.broadcasted_iota(jnp.int32, (chunks, LANES), 1) < SPAN
    weights = [(bank, i) for bank in banks for i in range(bank.shape[0])]
    weights = weights[start * js : (start + comps) * js]
    def operand(g):
        rows = []
        for ch in range(g * count, (g + 1) * count):
            for source in (low, high):
                rows.append(jnp.concatenate([source[ch, p : p + chunks, :] for p in range(span)], axis=1))
        return jnp.concatenate(rows, axis=0).astype(jnp.bfloat16)

    def gather_sums(g, res):
        base = g * count
        for k in range(count):
            left = (k // 2) * LANES
            tile = res[2 * k * chunks : 2 * (k + 1) * chunks, left : left + LANES]
            early, late = tile[:chunks], tile[chunks:]
            if k % 2 == 0:
                first, turned = early, late
            else:
                turned = pltpu.roll(jnp.where(side, turned, early), SPAN, 1)
                even, odd = jnp.where(side, first, turned), jnp.where(side, turned, late)
                accs[k - 1] = accs[k - 1] + even * norm[base + k - 1]
                accs[k] = accs[k] + odd * norm[base + k]

    for g, (bank, i) in enumerate(weights):
        gather_sums(g, jnp.dot(operand(g), bank[i], preferred_element_type=jnp.float32))
    for k in range(count):
        total[k] = accs[k]
    if not last:
        return
    each = chunks // (nslab * nsub)
    for d in range(nslab):
        for e in range(each):
            first = lax.bitwise_xor(here, d) * nsub * each + e
            turn = nsub - 1 if d else 0
            mine = first + lax.bitwise_xor(core, turn) * each
            keep[d, :, e * LANES : (e + 1) * LANES] = total[:, mine, :]
            for m in range(1, nsub):
                other = first + lax.bitwise_xor(core, m ^ turn) * each
                send[m - 1, d, :, e * LANES : (e + 1) * LANES] = total[:, other, :]


def swapped(value, axis, distance):
    return lax.ppermute(value, axis, [(i, i ^ distance) for i in range(lax.axis_size(axis))])


def crossed(value, distance):
    nsub = lax.axis_size("sub")
    count = lax.axis_size("slab") * nsub
    return lax.ppermute(value, ("slab", "sub"), [(i, i ^ (distance * nsub + nsub - 1)) for i in range(count)])


def stays(value):
    return pltpu.with_memory_space_constraint(value, pltpu.HBM)


def params(mib):
    return pltpu.CompilerParams(vmem_limit_bytes=mib << 20)


def on_device(records, owner_slots, gap_start, gap_len, templates, station_ids, offsets):
    nloc, comps, width = records.shape
    count, js, _, taps = templates.shape
    nslab, nsub, ntmpl = (lax.axis_size(name) for name in ("slab", "sub", "tmpl"))
    time = width * nslab
    refs = count * js
    chans = comps * refs
    here, core = lax.axis_index("slab"), lax.axis_index("sub")
    vmem, smem = pl.BlockSpec(memory_space=pltpu.VMEM), pl.BlockSpec(memory_space=pltpu.SMEM)
    hbm = pl.BlockSpec(memory_space=pltpu.HBM)
    half = nloc // nsub
    high = round_up(half, 16)
    per = width // LANES
    if high == half:
        block = pl.pallas_call(
            pack_kernel,
            out_shape=jax.ShapeDtypeStruct((comps * high * per + EXTRA, LANES), records.dtype),
            in_specs=[hbm, hbm],
            out_specs=vmem,
            scratch_shapes=[pltpu.SMEM((nloc,), jnp.int32), pltpu.SemaphoreType.DMA((comps * per + 1,))],
            compiler_params=params(4),
            name="pack",
        )(stays(owner_slots), stays(records.transpose(1, 0, 2)))
    else:
        mine = lax.dynamic_slice_in_dim(records.transpose(1, 0, 2), half * core, half, 1)
        mine = jnp.pad(mine, ((0, 0), (0, high - half), (0, 0))).reshape(comps, high, per, LANES)
        mine = mine.transpose(0, 2, 1, 3).reshape(comps * per * high, LANES)
        own = lax.dynamic_slice_in_dim(owner_slots, half * core, half, 0)
        index = jnp.arange(EXTRA * LANES, dtype=jnp.int32).reshape(1, EXTRA, LANES) % high
        slots = jnp.arange(half, dtype=jnp.int32)[:, None, None]
        own = jnp.sum(jnp.where(index == slots, own[:, None, None] + 1, 0), axis=0) - 1
        block = jnp.concatenate([mine, own.astype(records.dtype)], axis=0)
    column = [block]
    if ntmpl <= 8:
        for d in range(1, ntmpl):
            column.append(lax.ppermute(block, "tmpl", [(i, (i + d) % ntmpl) for i in range(ntmpl)]))
    else:
        column = list(lax.all_gather(block, "tmpl", axis=0))
    asked = [crossed(station_ids, d) for d in range(1, nslab)]
    waves = templates.transpose(1, 2, 0, 3)
    reach = round_up(taps + LANES - 1, LANES)
    depth = round_up(taps + SPAN - 1, LANES)
    groups = comps * js
    first, second = groups * 4 // 15, groups // 5

    def bank(size):
        return jax.ShapeDtypeStruct((size, depth, count * SPAN), jnp.bfloat16)

    column_type = jax.ShapeDtypeStruct((refs, LANES), jnp.int32)
    sid_col, off_col, mask, band, scale, waves, bank_a = pl.pallas_call(
        tables_kernel,
        out_shape=[
            column_type,
            column_type,
            jax.ShapeDtypeStruct((refs, time), jnp.float32),
            jax.ShapeDtypeStruct((2 * LANES, reach), jnp.bfloat16),
            jax.ShapeDtypeStruct((chans, LANES), jnp.float32),
            jax.ShapeDtypeStruct(waves.shape, waves.dtype),
            bank(first),
        ],
        in_specs=[hbm] * 5,
        out_specs=[vmem] * 7,
        scratch_shapes=[
            pltpu.SMEM(station_ids.shape, jnp.int32),
            pltpu.SMEM(offsets.shape, jnp.int32),
            pltpu.VMEM(gap_start.T.shape, jnp.int32),
            pltpu.VMEM(gap_len.T.shape, jnp.int32),
            pltpu.SemaphoreType.DMA((5,)),
        ],
        compiler_params=params(12),
        name="tables",
    )(*[stays(value) for value in (station_ids, offsets, gap_start.T, gap_len.T, waves)])
    column, asked, mask = lax.optimization_barrier((column, asked, mask))
    head = jnp.stack(column)
    heads = [head] + [swapped(head, "sub", m) for m in range(1, nsub)]
    *sid_far, bank_b = pl.pallas_call(
        functools.partial(middle_kernel, first, nslab - 1),
        out_shape=[column_type] * (nslab - 1) + [bank(second)],
        in_specs=[smem] * (nslab - 1) + [vmem],
        out_specs=[vmem] * nslab,
        compiler_params=params(12),
        name="middle",
    )(*asked, waves)
    heads, sid_far, bank_b = lax.optimization_barrier((heads, sid_far, bank_b))

    def select(columns, masks, heights, dtype):
        sizes = [size for size in heights for _ in columns]
        return pl.pallas_call(
            functools.partial(select_kernel, comps, high, nsub, len(columns), len(masks)),
            out_shape=[jax.ShapeDtypeStruct((size, width), dtype) for size in sizes],
            in_specs=[vmem] * (nsub + len(columns) + len(masks)),
            out_specs=[vmem] * len(sizes),
            compiler_params=params(16),
            name="select",
        )(*heads, *columns, *masks)

    ahead = comps - 1
    fars = select(sid_far, [], [ahead * refs, chans - ahead * refs], records.dtype)
    early = [crossed(far, d + 1) for d, far in enumerate(fars[: nslab - 1])]
    late = [crossed(far, d + 1) for d, far in enumerate(fars[nslab - 1 :])]
    bank_c = pl.pallas_call(
        functools.partial(filters_kernel, first + second),
        out_shape=bank(groups - first - second),
        in_specs=[vmem],
        out_specs=vmem,
        compiler_params=params(16),
        name="filters",
    )(waves)
    (near,) = select([sid_col], [mask], [chans], jnp.float32)
    early, bank_c, near = lax.optimization_barrier((early, bank_c, near))
    chunks = time // LANES
    each = width // nsub
    tall = chunks + 8
    stack_type = jax.ShapeDtypeStruct((count, chunks, LANES), jnp.float32)

    def correlate(start, far, before, last):
        size = far[0].shape[0]
        scratch = [
            pltpu.VMEM((size, time), jnp.float32),
            pltpu.VMEM((size, tall, LANES), jnp.float32),
            pltpu.VMEM((size, tall, LANES), jnp.float32),
            pltpu.VMEM((size, chunks, LANES), jnp.float32),
        ]
        shapes = [stack_type]
        if last:
            scratch.append(pltpu.VMEM(stack_type.shape, jnp.float32))
            shapes = [
                jax.ShapeDtypeStruct((nslab, count, each), jnp.float32),
                jax.ShapeDtypeStruct((nsub - 1, nslab, count, each), jnp.float32),
            ]
        operands = [near, *far, bank_a, bank_b, bank_c, *before, off_col, mask, band, scale]
        return pl.pallas_call(
            functools.partial(correlate_kernel, nslab, nsub, taps, 3, start, last),
            out_shape=shapes,
            in_specs=[vmem] * len(operands),
            out_specs=[vmem] * len(shapes),
            scratch_shapes=scratch,
            compiler_params=params(24),
            name="correlate",
        )(*operands)

    before = correlate(0, early, [], False)
    keep, send = correlate(ahead, late, before, True)
    for m in range(1, nsub):
        keep = keep + swapped(send[m - 1], "sub", m)
    lines = [keep[0]]
    for d in range(1, nslab):
        lines.append(crossed(keep[d], d))
    result = []
    for s in range(nslab):
        line = lines[0]
        for d in range(1, nslab):
            line = jnp.where((here ^ d) == s, lines[d], line)
        result.append(line)
    return jnp.concatenate(result, axis=0)


def solution(mesh):
    in_specs = (
        P(("grp", "tmpl"), None, "slab"),
        P(("grp", "tmpl")),
        P("grp", None),
        P("grp", None),
        P(("grp", "tmpl", "slab"), "sub", None, None),
        P(("grp", "tmpl", "slab"), "sub"),
        P(("grp", "tmpl", "slab"), "sub"),
    )
    out_specs = P(("grp", "tmpl"), ("slab", "sub"))
    return jax.shard_map(
        on_device, mesh=mesh, in_specs=in_specs, out_specs=out_specs, check_vma=False
    )
```

```python
import functools

import jax
import jax.numpy as jnp
from jax import lax
from jax.experimental import pallas as pl
from jax.experimental.pallas import tpu as pltpu
from jax.sharding import PartitionSpec as P

LANES = 128
SPAN = 64
EXTRA = 8
UNROLL = 6


def round_up(value, step):
    return -(-value // step) * step


def pack_kernel(owner_slots, records, block, owners, sems):
    comps, _, width = records.shape
    per = width // LANES
    half = (block.shape[0] - EXTRA) // (comps * per)
    first = pl.multiple_of(lax.axis_index("sub") * half, half)
    copies = [pltpu.make_async_copy(owner_slots, owners, sems.at[comps * per])]
    for i in range(comps * per):
        source = records.at[i // per, pl.ds(first, half), (i % per) * LANES : (i % per + 1) * LANES]
        copies.append(pltpu.make_async_copy(source, block.at[i * half : (i + 1) * half, :], sems.at[i]))
    for copy in copies:
        copy.start()
    copies[0].wait()
    lane = lax.rem(lax.broadcasted_iota(jnp.int32, (EXTRA, LANES), 1), half)
    line = jnp.full((EXTRA, LANES), -1, jnp.int32)
    for i in range(half):
        line = jnp.where(lane == i, owners[first + i], line)
    block[comps * per * half :, :] = line.astype(jnp.float32).astype(block.dtype)
    for copy in copies[1:]:
        copy.wait()


def build_filters(begin, waves, filters):
    js, _, count, taps = waves.shape
    groups, depth, _ = filters.shape

    def one_group(i):
        g = begin + i
        wave = waves[lax.rem(g, js), g // js].astype(jnp.float32)
        wave = jnp.concatenate([wave, jnp.zeros((count, depth - taps), jnp.float32)], axis=1)
        rows = []
        for k in range(count):
            row = jnp.broadcast_to(wave[k : k + 1], (SPAN, depth))
            rows.append(pltpu.roll(row, 0, 1, stride=1, stride_axis=0))
        filters[i] = jnp.concatenate(rows, axis=0).T.astype(jnp.bfloat16)

    def some_groups(t, carry):
        for u in range(UNROLL):
            one_group(t * UNROLL + u)
        return carry

    lax.fori_loop(0, groups // UNROLL, some_groups, 0)
    for i in range(groups // UNROLL * UNROLL, groups):
        one_group(i)


def tables_kernel(sids_in, offs_in, start_in, len_in, waves_in, sid_col, off_col, mask, band, scale, waves, filters, *scratch):
    sids, offs, gap_start, gap_len, sems = scratch
    pairs = ((waves_in, waves), (sids_in, sids), (offs_in, offs), (start_in, gap_start), (len_in, gap_len))
    copies = [pltpu.make_async_copy(source, place, sems.at[i]) for i, (source, place) in enumerate(pairs)]
    for copy in copies:
        copy.start()
    js, comps, count, taps = waves.shape
    refs = count * js
    rows = lax.rem(lax.broadcasted_iota(jnp.int32, band.shape, 0), LANES)
    cols = lax.broadcasted_iota(jnp.int32, band.shape, 1)
    lead = rows + (cols // LANES) * LANES - lax.rem(cols, LANES)
    band[...] = jnp.where((lead >= 0) & (lead < taps), 1.0, 0.0).astype(jnp.bfloat16)
    for copy in copies:
        copy.wait()
    for k in range(count):
        for j in range(js):
            row = j * count + k
            off_col[row, :] = jnp.full((LANES,), offs[k, j], jnp.int32)
            sid_col[row, :] = jnp.full((LANES,), sids[k, j], jnp.int32)
    nstation = gap_start.shape[1]
    own = lax.broadcasted_iota(jnp.int32, (refs, nstation), 1) == sid_col[:, :nstation]
    starts = gap_start[...].astype(jnp.float32)
    ends = starts + gap_len[...].astype(jnp.float32)
    live = jnp.ones(mask.shape, jnp.float32)
    times = lax.broadcasted_iota(jnp.int32, mask.shape, 1).astype(jnp.float32)
    for g in range(starts.shape[0]):
        first = jnp.sum(jnp.where(own, starts[g : g + 1], 0.0), axis=1, keepdims=True)
        last = jnp.sum(jnp.where(own, ends[g : g + 1], 0.0), axis=1, keepdims=True)
        live = jnp.where((times >= first) & (times < last), 0.0, live)
    mask[...] = live
    for c in range(comps):
        for j in range(js):
            wave = waves[j, c].astype(jnp.float32)
            power = jnp.sum(wave * wave, axis=1, keepdims=True) / taps
            factor = 1.0 / (taps * jnp.sqrt(power + 1e-06))
            first = (c * js + j) * count
            scale[first : first + count, :] = jnp.broadcast_to(factor, (count, LANES))
    build_filters(0, waves, filters)


def middle_kernel(begin, nfar, *args):
    asked, waves, columns, filters = args[:nfar], args[nfar], args[nfar + 1 : -1], args[-1]
    count, js = asked[0].shape
    for source, column in zip(asked, columns):
        for k in range(count):
            for j in range(js):
                column[j * count + k, :] = jnp.full((LANES,), source[k, j], jnp.int32)
    build_filters(begin, waves, filters)


def filters_kernel(begin, waves, filters):
    build_filters(begin, waves, filters)


def select_kernel(comps, high, nsub, asks, nmask, *args):
    heads, args = args[:nsub], args[nsub:]
    sid_cols, masks, outs = args[:asks], args[asks : asks + nmask], args[asks + nmask :]
    refs = sid_cols[0].shape[0]
    ntmpl = heads[0].shape[0]
    width = outs[0].shape[1]
    per = width // LANES
    here = lax.axis_index("slab")
    rows_slab = comps * high
    blocks = [(part, z) for part in heads for z in range(ntmpl)]
    depth = len(blocks) * rows_slab
    owner = []
    for q in range(0, depth, LANES):
        lane = lax.broadcasted_iota(jnp.int32, (1, LANES), 1) + q
        line = jnp.full((1, LANES), -1.0, jnp.float32)
        for b, (part, z) in enumerate(blocks):
            if b * rows_slab < q + LANES and (b + 1) * rows_slab > q:
                tail = part[z, rows_slab * per : rows_slab * per + EXTRA, :].astype(jnp.float32)
                inside = (lane >= b * rows_slab) & (lane < (b + 1) * rows_slab)
                line = jnp.where(inside, tail[:1], line)
        owner.append(line)
    owner = jnp.concatenate(owner, axis=1)[:, :depth]
    row = lax.broadcasted_iota(jnp.int32, (1, depth), 1)
    row = lax.rem(row, rows_slab) // high
    columns = []
    for q in range(per):
        tiles = []
        for part, z in blocks:
            for c in range(comps):
                first = (c * per + q) * high
                tiles.append(part[z, first : first + high, :])
        columns.append(jnp.concatenate(tiles, axis=0))
    stack = jnp.concatenate(columns, axis=1)
    owners = [jnp.where(row == c, owner, -1.0) for c in range(comps)]
    for d, (sid_col, out) in enumerate(zip(sid_cols, outs)):
        wanted = sid_col[:, :1].astype(jnp.float32)
        pick = [jnp.where(owners[c] == wanted, 1.0, 0.0).astype(jnp.bfloat16) for c in range(comps)]
        got = jnp.dot(jnp.concatenate(pick, axis=0), stack, preferred_element_type=jnp.float32)
        if not masks:
            split = out.shape[0]
            out[...] = got[:split].astype(out.dtype)
            outs[asks + d][...] = got[split:].astype(out.dtype)
        else:
            live = masks[0][:, pl.ds(pl.multiple_of(here * width, LANES), width)]
            for c in range(comps):
                out[c * refs : (c + 1) * refs, :] = got[c * refs : (c + 1) * refs] * live


def correlate_kernel(nslab, nsub, taps, nbank, start, last, *args):
    near, fars, args = args[0], args[1:nslab], args[nslab:]
    banks, args = args[:nbank], args[nbank:]
    if start:
        before, args = args[0], args[1:]
    off_col, mask, band, scale, args = *args[:4], args[4:]
    if last:
        keep, send, segs, low, high, norm, total = args
    else:
        total, segs, low, high, norm = args
    refs, time = mask.shape
    chans, width = fars[0].shape
    comps = chans // refs
    chunks = time // LANES
    count = total.shape[0]
    js = refs // count
    here, core = lax.axis_index("slab"), lax.axis_index("sub")
    for d in range(nslab):
        spot = pl.ds(pl.multiple_of(lax.bitwise_xor(here, d) * width, LANES), width)
        if d == 0:
            segs[:, spot] = near[start * refs : start * refs + chans, :]
        else:
            live = mask[:, spot]
            for c in range(comps):
                got = fars[d - 1][c * refs : (c + 1) * refs, :].astype(jnp.float32)
                segs[c * refs : (c + 1) * refs, spot] = got * live
    lane = lax.broadcasted_iota(jnp.int32, (8, LANES), 1)
    zero = jnp.zeros((8, LANES), jnp.float32)
    span = banks[0].shape[1] // LANES
    for i in range(chans // 8):
        ref_row = (i * 8) % refs
        off = off_col[ref_row : ref_row + 8, :]
        place = lax.bitwise_and(lane + off, LANES - 1)
        fine = lax.bitwise_and(off, LANES - 1)
        close = lane + fine < LANES
        far = off >= LANES
        turned = [
            jnp.take_along_axis(segs[i * 8 : i * 8 + 8, r * LANES : (r + 1) * LANES], place, axis=1)
            for r in range(chunks)
        ]
        turned += [zero, zero]
        moved = [jnp.where(close, turned[r], turned[r + 1]) for r in range(chunks + 1)]
        mine = [jnp.where(far, moved[r + 1], moved[r]) for r in range(chunks)]
        swung = [pltpu.roll(part, SPAN, 1) for part in mine] + [zero]
        for r in range(chunks):
            segs[i * 8 : i * 8 + 8, r * LANES : (r + 1) * LANES] = mine[r]
            low[pl.ds(i * 8, 8), r, :] = mine[r]
            high[pl.ds(i * 8, 8), r, :] = jnp.where(lane < LANES - SPAN, swung[r], swung[r + 1])
        for r in range(chunks, chunks + span - 1):
            low[pl.ds(i * 8, 8), r, :] = zero
            high[pl.ds(i * 8, 8), r, :] = zero
    reach = band.shape[1] // LANES
    sums = {}
    for first in range(0, chunks, 2):
        batch = range(first, first + 2)
        power = jnp.concatenate([segs[:, r * LANES : (r + 1) * LANES] for r in batch], axis=0)
        power = power * power
        lead = power.astype(jnp.bfloat16)
        rest = (power - lead.astype(jnp.float32)).astype(jnp.bfloat16)
        both = jnp.concatenate([lead, rest], axis=1)
        got = jnp.dot(both, band[...], preferred_element_type=jnp.float32)
        for r in batch:
            sums[r] = got[(r - first) * chans : (r - first + 1) * chans]
    for r in range(chunks):
        window = sums[r][:, :LANES]
        for p in range(1, min(reach, chunks - r)):
            window = window + sums[r + p][:, p * LANES : (p + 1) * LANES]
        factor = scale[start * refs : start * refs + chans, :] * lax.rsqrt(window / taps + 1e-06)
        for i in range(chans // 8):
            norm[pl.ds(i * 8, 8), r, :] = factor[i * 8 : i * 8 + 8]
    accs = [before[k] if start else jnp.zeros((chunks, LANES), jnp.float32) for k in range(count)]
    side = lax.broadcasted_iota(jnp.int32, (chunks, LANES), 1) < SPAN
    weights = [(bank, i) for bank in banks for i in range(bank.shape[0])]
    weights = weights[start * js : (start + comps) * js]
    def operand(g):
        rows = []
        for ch in range(g * count, (g + 1) * count):
            for source in (low, high):
                rows.append(jnp.concatenate([source[ch, p : p + chunks, :] for p in range(span)], axis=1))
        return jnp.concatenate(rows, axis=0).astype(jnp.bfloat16)

    def gather_sums(g, res):
        base = g * count
        for k in range(count):
            left = (k // 2) * LANES
            tile = res[2 * k * chunks : 2 * (k + 1) * chunks, left : left + LANES]
            early, late = tile[:chunks], tile[chunks:]
            if k % 2 == 0:
                first, turned = early, late
            else:
                turned = pltpu.roll(jnp.where(side, turned, early), SPAN, 1)
                even, odd = jnp.where(side, first, turned), jnp.where(side, turned, late)
                accs[k - 1] = accs[k - 1] + even * norm[base + k - 1]
                accs[k] = accs[k] + odd * norm[base + k]

    for g, (bank, i) in enumerate(weights):
        gather_sums(g, jnp.dot(operand(g), bank[i], preferred_element_type=jnp.float32))
    for k in range(count):
        total[k] = accs[k]
    if not last:
        return
    each = chunks // (nslab * nsub)
    for d in range(nslab):
        for e in range(each):
            first = lax.bitwise_xor(here, d) * nsub * each + e
            turn = nsub - 1 if d else 0
            mine = first + lax.bitwise_xor(core, turn) * each
            keep[d, :, e * LANES : (e + 1) * LANES] = total[:, mine, :]
            for m in range(1, nsub):
                other = first + lax.bitwise_xor(core, m ^ turn) * each
                send[m - 1, d, :, e * LANES : (e + 1) * LANES] = total[:, other, :]


def swapped(value, axis, distance):
    return lax.ppermute(value, axis, [(i, i ^ distance) for i in range(lax.axis_size(axis))])


def crossed(value, distance):
    nsub = lax.axis_size("sub")
    count = lax.axis_size("slab") * nsub
    return lax.ppermute(value, ("slab", "sub"), [(i, i ^ (distance * nsub + nsub - 1)) for i in range(count)])


def stays(value):
    return pltpu.with_memory_space_constraint(value, pltpu.HBM)


def params(mib):
    return pltpu.CompilerParams(vmem_limit_bytes=mib << 20)


def on_device(records, owner_slots, gap_start, gap_len, templates, station_ids, offsets):
    nloc, comps, width = records.shape
    count, js, _, taps = templates.shape
    nslab, nsub, ntmpl = (lax.axis_size(name) for name in ("slab", "sub", "tmpl"))
    time = width * nslab
    refs = count * js
    chans = comps * refs
    here, core = lax.axis_index("slab"), lax.axis_index("sub")
    vmem, smem = pl.BlockSpec(memory_space=pltpu.VMEM), pl.BlockSpec(memory_space=pltpu.SMEM)
    hbm = pl.BlockSpec(memory_space=pltpu.HBM)
    half = nloc // nsub
    high = round_up(half, 16)
    per = width // LANES
    if high == half:
        block = pl.pallas_call(
            pack_kernel,
            out_shape=jax.ShapeDtypeStruct((comps * high * per + EXTRA, LANES), records.dtype),
            in_specs=[hbm, hbm],
            out_specs=vmem,
            scratch_shapes=[pltpu.SMEM((nloc,), jnp.int32), pltpu.SemaphoreType.DMA((comps * per + 1,))],
            compiler_params=params(4),
            name="pack",
        )(stays(owner_slots), stays(records.transpose(1, 0, 2)))
    else:
        mine = lax.dynamic_slice_in_dim(records.transpose(1, 0, 2), half * core, half, 1)
        mine = jnp.pad(mine, ((0, 0), (0, high - half), (0, 0))).reshape(comps, high, per, LANES)
        mine = mine.transpose(0, 2, 1, 3).reshape(comps * per * high, LANES)
        own = lax.dynamic_slice_in_dim(owner_slots, half * core, half, 0)
        index = jnp.arange(EXTRA * LANES, dtype=jnp.int32).reshape(1, EXTRA, LANES) % high
        slots = jnp.arange(half, dtype=jnp.int32)[:, None, None]
        own = jnp.sum(jnp.where(index == slots, own[:, None, None] + 1, 0), axis=0) - 1
        block = jnp.concatenate([mine, own.astype(records.dtype)], axis=0)
    column = [block]
    if ntmpl <= 8:
        for d in range(1, ntmpl):
            column.append(lax.ppermute(block, "tmpl", [(i, (i + d) % ntmpl) for i in range(ntmpl)]))
    else:
        column = list(lax.all_gather(block, "tmpl", axis=0))
    asked = [crossed(station_ids, d) for d in range(1, nslab)]
    waves = templates.transpose(1, 2, 0, 3)
    reach = round_up(taps + LANES - 1, LANES)
    depth = round_up(taps + SPAN - 1, LANES)
    groups = comps * js
    first, second = max(groups // 6, 1), groups // 5

    def bank(size):
        return jax.ShapeDtypeStruct((size, depth, count * SPAN), jnp.bfloat16)

    column_type = jax.ShapeDtypeStruct((refs, LANES), jnp.int32)
    sid_col, off_col, mask, band, scale, waves, bank_a = pl.pallas_call(
        tables_kernel,
        out_shape=[
            column_type,
            column_type,
            jax.ShapeDtypeStruct((refs, time), jnp.float32),
            jax.ShapeDtypeStruct((2 * LANES, reach), jnp.bfloat16),
            jax.ShapeDtypeStruct((chans, LANES), jnp.float32),
            jax.ShapeDtypeStruct(waves.shape, waves.dtype),
            bank(first),
        ],
        in_specs=[hbm] * 5,
        out_specs=[vmem] * 7,
        scratch_shapes=[
            pltpu.SMEM(station_ids.shape, jnp.int32),
            pltpu.SMEM(offsets.shape, jnp.int32),
            pltpu.VMEM(gap_start.T.shape, jnp.int32),
            pltpu.VMEM(gap_len.T.shape, jnp.int32),
            pltpu.SemaphoreType.DMA((5,)),
        ],
        compiler_params=params(12),
        name="tables",
    )(*[stays(value) for value in (station_ids, offsets, gap_start.T, gap_len.T, waves)])
    column, asked, mask = lax.optimization_barrier((column, asked, mask))
    head = jnp.stack(column)
    heads = [head] + [swapped(head, "sub", m) for m in range(1, nsub)]
    *sid_far, bank_b = pl.pallas_call(
        functools.partial(middle_kernel, first, nslab - 1),
        out_shape=[column_type] * (nslab - 1) + [bank(second)],
        in_specs=[smem] * (nslab - 1) + [vmem],
        out_specs=[vmem] * nslab,
        compiler_params=params(12),
        name="middle",
    )(*asked, waves)
    heads, sid_far, bank_b = lax.optimization_barrier((heads, sid_far, bank_b))

    def select(columns, masks, heights, dtype):
        sizes = [size for size in heights for _ in columns]
        return pl.pallas_call(
            functools.partial(select_kernel, comps, high, nsub, len(columns), len(masks)),
            out_shape=[jax.ShapeDtypeStruct((size, width), dtype) for size in sizes],
            in_specs=[vmem] * (nsub + len(columns) + len(masks)),
            out_specs=[vmem] * len(sizes),
            compiler_params=params(16),
            name="select",
        )(*heads, *columns, *masks)

    ahead = comps - 1
    fars = select(sid_far, [], [ahead * refs, chans - ahead * refs], records.dtype)
    early = [crossed(far, d + 1) for d, far in enumerate(fars[: nslab - 1])]
    late = [crossed(far, d + 1) for d, far in enumerate(fars[nslab - 1 :])]
    bank_c = pl.pallas_call(
        functools.partial(filters_kernel, first + second),
        out_shape=bank(groups - first - second),
        in_specs=[vmem],
        out_specs=vmem,
        compiler_params=params(16),
        name="filters",
    )(waves)
    (near,) = select([sid_col], [mask], [chans], jnp.float32)
    early, bank_c, near = lax.optimization_barrier((early, bank_c, near))
    chunks = time // LANES
    each = width // nsub
    tall = chunks + 8
    stack_type = jax.ShapeDtypeStruct((count, chunks, LANES), jnp.float32)

    def correlate(start, far, before, last):
        size = far[0].shape[0]
        scratch = [
            pltpu.VMEM((size, time), jnp.float32),
            pltpu.VMEM((size, tall, LANES), jnp.float32),
            pltpu.VMEM((size, tall, LANES), jnp.float32),
            pltpu.VMEM((size, chunks, LANES), jnp.float32),
        ]
        shapes = [stack_type]
        if last:
            scratch.append(pltpu.VMEM(stack_type.shape, jnp.float32))
            shapes = [
                jax.ShapeDtypeStruct((nslab, count, each), jnp.float32),
                jax.ShapeDtypeStruct((nsub - 1, nslab, count, each), jnp.float32),
            ]
        operands = [near, *far, bank_a, bank_b, bank_c, *before, off_col, mask, band, scale]
        return pl.pallas_call(
            functools.partial(correlate_kernel, nslab, nsub, taps, 3, start, last),
            out_shape=shapes,
            in_specs=[vmem] * len(operands),
            out_specs=[vmem] * len(shapes),
            scratch_shapes=scratch,
            compiler_params=params(24),
            name="correlate",
        )(*operands)

    before = correlate(0, early, [], False)
    keep, send = correlate(ahead, late, before, True)
    for m in range(1, nsub):
        keep = keep + swapped(send[m - 1], "sub", m)
    lines = [keep[0]]
    for d in range(1, nslab):
        lines.append(crossed(keep[d], d))
    result = []
    for s in range(nslab):
        line = lines[0]
        for d in range(1, nslab):
            line = jnp.where((here ^ d) == s, lines[d], line)
        result.append(line)
    return jnp.concatenate(result, axis=0)


def solution(mesh):
    in_specs = (
        P(("grp", "tmpl"), None, "slab"),
        P(("grp", "tmpl")),
        P("grp", None),
        P("grp", None),
        P(("grp", "tmpl", "slab"), "sub", None, None),
        P(("grp", "tmpl", "slab"), "sub"),
        P(("grp", "tmpl", "slab"), "sub"),
    )
    out_specs = P(("grp", "tmpl"), ("slab", "sub"))
    return jax.shard_map(
        on_device, mesh=mesh, in_specs=in_specs, out_specs=out_specs, check_vma=False
    )
```
